32 devices in a mesh: section: 2 (over x), dp: 16 (over z, y, core).
Axes of the slice: x: 2, y: 2, z: 4, core: 2. Of those that a mesh axis runs over, the one named last changes fastest.
Arguments:
- block_input: bfloat16 [2, 2560, 1024], P(None, 'dp'), may hold values from -6 to 6
- conditioning: bfloat16 [2, 2, 1024], replicated, may hold values from -6 to 6
- text_embed: bfloat16 [2, 160, 1024], P(None, 'dp'), may hold values from -6 to 6
- text_keep: int32 [2, 2], replicated, may hold values 0 or 1
- cotangent: bfloat16 [2, 2560, 1024], P(None, 'dp'), may hold values from -6 to 6
- self_input: float32 [2, 1024, 3072], P('section', 'dp'), may hold values from -0.1875 to 0.1875
- self_output: float32 [2, 1024, 1024], P('section', 'dp'), may hold values from -0.75 to 0.75
- cross_query: float32 [2, 1024, 1024], P('section', 'dp'), may hold values from -0.1875 to 0.1875
- cross_memory: float32 [2, 1024, 2048], P('section', 'dp'), may hold values from -0.1875 to 0.1875
- cross_output: float32 [2, 1024, 1024], P('section', 'dp'), may hold values from -0.5 to 0.5
- up_weight: float32 [2, 1024, 4096], P('section', 'dp'), may hold values from -0.1875 to 0.1875
- down_weight: float32 [2, 4096, 1024], P('section', 'dp'), may hold values from -0.09375 to 0.09375
- modulation: float32 [2, 1024, 6144], P('section', 'dp'), may hold values from -0.1875 to 0.1875
- modulation_bias: float32 [2, 6144], P('section'), may hold values from -3 to 3
- position_bias: float32 [2, 16, 71], P('section'), may hold values from -4 to 4
Outputs:
- block_outputs: bfloat16 [2, 2, 2560, 1024], P('section', None, 'dp')
- input_grads: bfloat16 [2, 2, 2560, 1024], P('section', None, 'dp')
- grad_self_input: float32 [2, 1024, 3072], P('section', 'dp')
- grad_self_output: float32 [2, 1024, 1024], P('section', 'dp')
- grad_cross_query: float32 [2, 1024, 1024], P('section', 'dp')
- grad_cross_memory: float32 [2, 1024, 2048], P('section', 'dp')
- grad_cross_output: float32 [2, 1024, 1024], P('section', 'dp')
- grad_up_weight: float32 [2, 1024, 4096], P('section', 'dp')
- grad_down_weight: float32 [2, 4096, 1024], P('section', 'dp')
- grad_modulation: float32 [2, 1024, 6144], P('section', 'dp')
- grad_modulation_bias: float32 [2, 6144], P('section')
- grad_position_bias: float32 [2, 16, 71], P('section')
The draws below stay inside these ranges and needn't reach their ends.
All inputs are finite; a program needn't handle non-finite values.
Results may differ from the reference program's by a relative error of at most 0.024.
The reference program's roundings to bfloat16 on the way count: a program that leaves them out, or rounds other values in their place, can miss the bound.
Values may be sent and summed in bfloat16 or wider, within the bound.
No kernel may reach another device: no remote copies, remote signals or barrier semaphores. Data moves between devices by JAX's collectives and lax.ppermute only.
A program may use at most 384 MiB of HBM per device.

```python
import jax
import jax.numpy as jnp
from jax import lax

D = 1024
HEADS = 16
HEAD = 64
FF = 4096
FRAMES = 5
BH = 8
BW = 4
TXT_DEV = 10
MB = 2
ROWS = 160
CLIPS = 2
TOKENS = 2560
TEXTS = 160
REL = 71


def plant(drawn, rng, smallest, high):
    shape = drawn.shape
    index_at = [jax.random.randint(jax.random.fold_in(rng, axis), (), 0, shape[axis]) for axis in range(len(shape))]
    drawn = drawn.at[tuple(index_at)].set(smallest)
    longest = shape.index(max(shape))
    index_at[longest] = (index_at[longest] + 1) % shape[longest]
    return drawn.at[tuple(index_at)].set(high)


def levels(rng, extent, shards, smallest, largest):
    loudness = 1.0
    for position, shards_of in shards:
        draws = jax.random.uniform(jax.random.fold_in(jax.random.fold_in(rng, 6), position), (shards_of,), jnp.float32, smallest / len(shards), largest / len(shards))
        loudness = loudness * jnp.repeat(jnp.exp(draws), extent[position] // shards_of).reshape((-1,) + (1,) * (len(extent) - 1 - position))
    return loudness


def normal_values(rng, extent, scale, reach, shards=(), held_as=jnp.bfloat16):
    entries = scale * jax.random.normal(rng, extent, jnp.float32)
    if shards:
        entries = entries * levels(rng, extent, shards, -0.22, 0.18)
    return jnp.clip(entries, -reach, reach).astype(held_as)


def setup_inputs(seed: int = 0) -> dict:
    key_list = jax.random.split(jax.random.key(seed), 16)
    return {
        "block_input": normal_values(key_list[0], (MB, TOKENS, D), 1.0, 6.0, ((1, 16),)),
        "conditioning": normal_values(key_list[1], (MB, CLIPS, D), 1.0, 6.0),
        "text_embed": normal_values(key_list[2], (MB, TEXTS, D), 1.0, 6.0, ((1, 16),)),
        "text_keep": plant((jax.random.randint(key_list[3], (MB, CLIPS), 0, 4) < 3).astype(jnp.int32), jax.random.fold_in(key_list[3], 1), 0, 1),
        "cotangent": normal_values(key_list[4], (MB, TOKENS, D), 1.0, 6.0, ((1, 16),)),
        "self_input": normal_values(key_list[5], (2, D, 3 * D), D ** -0.5, 0.1875, ((0, 2), (1, 16)), jnp.float32),
        "self_output": normal_values(key_list[6], (2, D, D), (D // 16) ** -0.5, 0.75, ((0, 2), (1, 16)), jnp.float32),
        "cross_query": normal_values(key_list[7], (2, D, D), D ** -0.5, 0.1875, ((0, 2), (1, 16)), jnp.float32),
        "cross_memory": normal_values(key_list[8], (2, D, 2 * D), D ** -0.5, 0.1875, ((0, 2), (1, 16)), jnp.float32),
        "cross_output": normal_values(key_list[9], (2, D, D), (D // 8) ** -0.5, 0.5, ((0, 2), (1, 16)), jnp.float32),
        "up_weight": normal_values(key_list[10], (2, D, FF), D ** -0.5, 0.1875, ((0, 2), (1, 16)), jnp.float32),
        "down_weight": normal_values(key_list[11], (2, FF, D), FF ** -0.5, 0.09375, ((0, 2), (1, 16)), jnp.float32),
        "modulation": normal_values(key_list[12], (2, D, 6 * D), D ** -0.5, 0.1875, ((0, 2), (1, 16)), jnp.float32),
        "modulation_bias": normal_values(key_list[13], (2, 6 * D), 0.7, 3.0, ((0, 2),), jnp.float32),
        "position_bias": normal_values(key_list[14], (2, HEADS, REL), 1.0, 4.0, ((0, 2),), jnp.float32),
    }


EPSILON = 1e-06
NEGATIVE = -1e+30

@jax.custom_vjp
def low(v):
    return lax.optimization_barrier(v.astype(jnp.bfloat16)).astype(jnp.float32)

@jax.custom_vjp
def low_back(v):
    return v

def low_keep(v):
    return (low(v), None)

def low_pass(kept, grad):
    return (grad,)

def back_keep(v):
    return (v, None)

def back_low(kept, grad):
    return (low(grad),)
low.defvjp(low_keep, low_pass)
low_back.defvjp(back_keep, back_low)

def both_round(operand):
    return low_back(low(operand))

def matmul_high(left_side, right_side):
    return jnp.einsum('...d,de->...e', left_side, right_side, precision=lax.Precision.HIGHEST)

def layer_mod(inputs, offset, factor):
    average = lax.optimization_barrier(jnp.mean(inputs, axis=-1, keepdims=True))
    centred = inputs - average
    spread = lax.optimization_barrier(jnp.mean(centred * centred, axis=-1, keepdims=True))
    return centred * lax.rsqrt(spread + EPSILON) * (1.0 + factor) + offset

def places_of(member, within):
    frame_id = within // (BH * BW)
    cell_id = within % (BH * BW)
    row_at = member // 4 * BH + cell_id // BW
    col_at = member % 4 * BW + cell_id % BW
    return (member, frame_id, row_at, col_at)

def bias_indices(query_places, key_places):
    time_index = query_places[1][:, None] - key_places[1][None, :] + FRAMES - 1
    row_index = query_places[2][:, None] - key_places[2][None, :] + 2 * BH - 1 + 2 * FRAMES - 1
    col_index = query_places[3][:, None] - key_places[3][None, :] + 4 * BW - 1 + 2 * FRAMES - 1 + 4 * BH - 1
    return (time_index, row_index, col_index)

def attend(queries, key_rows, values, additive, window):
    row_count = queries.shape[0]
    query_heads = queries.reshape(row_count, HEADS, HEAD)
    key_heads = key_rows.reshape(key_rows.shape[0], HEADS, HEAD)
    value_heads = values.reshape(values.shape[0], HEADS, HEAD)
    scores = low_back(jnp.einsum('qhd,khd->hqk', query_heads, key_heads, precision=lax.Precision.HIGHEST)) * HEAD ** (-0.5) + additive
    if window is not None:
        scores = jnp.where(window[None], scores, NEGATIVE)
    highest = lax.optimization_barrier(jnp.max(scores, axis=-1, keepdims=True))
    exponent = jnp.exp(scores - highest)
    softmaxed = exponent / lax.optimization_barrier(jnp.sum(exponent, axis=-1, keepdims=True))
    mixture = jnp.einsum('hqk,khd->qhd', low(softmaxed), value_heads, precision=lax.Precision.HIGHEST)
    return both_round(mixture.reshape(row_count, HEADS * HEAD))

def section_block(section_weights, inputs, condition, text_words, indices, window):
    joint_master, self_out_master, query_master, memory_master, cross_out_master, upper_master, lower_master, modul_master, gain_bias, bias_values = section_weights
    w_joint = low(joint_master)
    w_self_out = low(self_out_master)
    w_query = low(query_master)
    w_memory = low(memory_master)
    w_cross_out = low(cross_out_master)
    w_upper = low(upper_master)
    w_lower = low(lower_master)
    w_modul = low(modul_master)
    relative = bias_values[:, indices[0]] + bias_values[:, indices[1]] + bias_values[:, indices[2]]
    modulated = matmul_high(low(jax.nn.silu(condition)), w_modul) + gain_bias
    mod_parts = modulated.reshape(MB, CLIPS, 1, 6, D)
    tokens = inputs.reshape(MB, CLIPS, 8 * ROWS, D)
    hidden = low(layer_mod(tokens, mod_parts[:, :, :, 0], mod_parts[:, :, :, 1]))
    joint_rows = both_round(matmul_high(hidden, w_joint))
    text_query = both_round(matmul_high(hidden, w_query))
    memory = both_round(matmul_high(text_words, w_memory))
    clip_total = MB * CLIPS

    def per_clip(pieces):
        clip_joint, clip_query, clip_memory = pieces
        first_out = attend(clip_joint[:, :D], clip_joint[:, D:2 * D], clip_joint[:, 2 * D:], relative, window)
        second_out = attend(clip_query, clip_memory[:, :D], clip_memory[:, D:], 0.0, None)
        return (first_out, second_out)
    mixture, mixture_text = lax.map(jax.checkpoint(per_clip), (joint_rows.reshape(clip_total, 8 * ROWS, 3 * D), text_query.reshape(clip_total, 8 * ROWS, D), memory.reshape(clip_total, 8 * TXT_DEV, 2 * D)))
    branch = low_back(matmul_high(mixture, w_self_out) + matmul_high(mixture_text, w_cross_out))
    branch = branch.reshape(MB, CLIPS, 8 * ROWS, D)
    middle = tokens + mod_parts[:, :, :, 2] * branch
    hidden_two = low(layer_mod(middle, mod_parts[:, :, :, 3], mod_parts[:, :, :, 4]))
    upper_pre = low_back(matmul_high(hidden_two, w_upper))
    active = low(jax.nn.gelu(upper_pre))
    feed_out = low_back(matmul_high(active, w_lower))
    result = middle + mod_parts[:, :, :, 5] * feed_out
    return result.reshape(MB, CLIPS * 8 * ROWS, D)

def reference(block_input, conditioning, text_embed, text_keep, cotangent, self_input, self_output, cross_query, cross_memory, cross_output, up_weight, down_weight, modulation, modulation_bias, position_bias):
    condition = conditioning.astype(jnp.float32)
    keep_flags = text_keep.astype(jnp.float32)
    text_words = text_embed.astype(jnp.float32).reshape(MB, CLIPS, 8 * TXT_DEV, D) * keep_flags[:, :, None, None]
    key_order = jnp.arange(8 * ROWS)
    key_places = places_of(key_order // ROWS, key_order % ROWS)
    indices = bias_indices(key_places, key_places)
    same_frame = key_places[1][:, None] == key_places[1][None, :]
    same_pair = (key_places[0] // 2)[:, None] == (key_places[0] // 2)[None, :]
    masters = (self_input, self_output, cross_query, cross_memory, cross_output, up_weight, down_weight, modulation, modulation_bias, position_bias)
    first_weights = tuple((master[0] for master in masters))
    second_weights = tuple((master[1] for master in masters))

    def first_section(inputs, section_weights):
        return section_block(section_weights, inputs, condition, text_words, indices, same_frame)

    def second_section(inputs, section_weights):
        return section_block(section_weights, inputs, condition, text_words, indices, same_pair)
    first_result, first_back = jax.vjp(first_section, block_input.astype(jnp.float32), first_weights)
    sent_first = first_result.astype(jnp.bfloat16)
    second_result, second_back = jax.vjp(second_section, sent_first.astype(jnp.float32), second_weights)
    grad_sent, second_grads = second_back(cotangent.astype(jnp.float32))
    grad_sent_low = grad_sent.astype(jnp.bfloat16)
    grad_first, first_grads = first_back(grad_sent_low.astype(jnp.float32))
    block_outputs = jnp.stack([sent_first, second_result.astype(jnp.bfloat16)])
    input_grads = jnp.stack([grad_first.astype(jnp.bfloat16), grad_sent_low])
    stacked = [jnp.stack([first_grads[number], second_grads[number]]) for number in range(10)]
    return (block_outputs, input_grads, stacked[0], stacked[1], stacked[2], stacked[3], stacked[4], stacked[5], stacked[6], stacked[7], stacked[8], stacked[9])
```

```python
import functools

import jax
import jax.numpy as jnp
import numpy as np
from jax import lax
from jax.experimental import pallas as pl
from jax.experimental.pallas import tpu as pltpu
from jax.sharding import PartitionSpec as P

D = 1024
HEADS = 16
HEAD = 64
FF = 4096
FRAMES = 5
BH = 8
BW = 4
CELLS = BH * BW
ROWS = 160
REL = 71
MEMBERS = 8
PAIR = 2 * HEAD
TEXT_PAD = 16
EPSILON = 1e-06
NEGATIVE = -1e30
LOW = jnp.bfloat16
HIGH = jnp.float32
MIB = 1024 * 1024


def dot(left, right):
    return lax.dot_general(left, right, (((1,), (0,)), ((), ())), preferred_element_type=HIGH)


def dot_right_t(left, right):
    return lax.dot_general(left, right, (((1,), (1,)), ((), ())), preferred_element_type=HIGH)


def dot_left_t(left, right):
    return lax.dot_general(left, right, (((0,), (0,)), ((), ())), preferred_element_type=HIGH)


def low(v):
    return v.astype(LOW)


def high(v):
    return v.astype(HIGH)


def layer_mod(inputs, offset, factor):
    average = jnp.mean(inputs, axis=-1, keepdims=True)
    centred = inputs - average
    spread = jnp.mean(centred * centred, axis=-1, keepdims=True)
    return centred * lax.rsqrt(spread + EPSILON) * (1.0 + factor) + offset


def swap(x, bits, sections=(0, 1)):
    count = lax.axis_size("dp")
    route = [(s * count + i, s * count + (i ^ bits)) for s in sections for i in range(count)]
    return lax.ppermute(x, ("section", "dp"), route)


def xor_blocks(x, axis, block, member, parts=1):
    stride = x.shape[axis] // parts
    pieces = [
        lax.dynamic_slice_in_dim(x, part * stride + block * (member ^ k), block, axis)
        for k in range(MEMBERS)
        for part in range(parts)
    ]
    return jnp.concatenate(pieces, axis)


def xor_blocks_back(x, axis, block, member, parts):
    pieces = [
        lax.dynamic_slice_in_dim(x, block * (parts * (member ^ k) + part), block, axis)
        for part in range(parts)
        for k in range(MEMBERS)
    ]
    return jnp.concatenate(pieces, axis)


def head_masks(dtype):
    lane = lax.broadcasted_iota(jnp.int32, (1, PAIR), 1)
    first = (lane < HEAD).astype(dtype)
    return first, 1 - first


def soft_rows(queries, keys, bias):
    scores = dot_right_t(queries, keys) * HEAD ** (-0.5) + bias
    exponent = jnp.exp(scores - jnp.max(scores, axis=-1, keepdims=True))
    return exponent * (1.0 / jnp.sum(exponent, axis=-1, keepdims=True))


def attend_kernel(shared, q_ref, k_ref, v_ref, bias_ref, o_ref):
    masks = head_masks(LOW)
    q, k, v = q_ref[0], k_ref[0], v_ref[0]
    mixed = []
    for a in range(2):
        soft = soft_rows(q * masks[a], k, bias_ref[0 if shared else a])
        mixed.append(dot(low(soft), v))
    lane = lax.broadcasted_iota(jnp.int32, (1, PAIR), 1)
    o_ref[0] = low(jnp.where(lane < HEAD, mixed[0], mixed[1]))


def attend_back_kernel(shared, q_ref, k_ref, v_ref, bias_ref, do_ref, dq_ref, dk_ref, dv_ref, *rest):
    masks = head_masks(LOW)
    q, k, v, do = q_ref[0], k_ref[0], v_ref[0], do_ref[0]
    lane = lax.broadcasted_iota(jnp.int32, (1, PAIR), 1)
    dq, dk, dv = [], [], []
    for a in range(2):
        soft = soft_rows(q * masks[a], k, bias_ref[0 if shared else a])
        dv.append(dot_left_t(low(soft), do))
        grad = dot_right_t(do * masks[a], v)
        grad = soft * (grad - jnp.sum(soft * grad, axis=-1, keepdims=True))
        if rest:
            dbias_ref = rest[0]

            @pl.when(pl.program_id(1) == 0)
            def _():
                dbias_ref[a] = grad

            @pl.when(pl.program_id(1) > 0)
            def _():
                dbias_ref[a] += grad

        raw = low(grad * HEAD ** (-0.5))
        dq.append(dot(raw, k))
        dk.append(dot_left_t(raw, q))
    dq_ref[0] = low(jnp.where(lane < HEAD, dq[0], dq[1]))
    dk_ref[0] = low(jnp.where(lane < HEAD, dk[0], dk[1]))
    dv_ref[0] = low(jnp.where(lane < HEAD, dv[0], dv[1]))


def column_spec(rows, first):
    return pl.BlockSpec((1, rows, PAIR), lambda h, w: (w, 0, first + h))


def attend_shapes(q, k, heads):
    pairs = heads // 2
    return q[0].shape[0], q[0].shape[1], k[0].shape[1], pairs


def attend(q, k, v, bias, heads):
    windows, rows, keys, pairs = attend_shapes(q, k, heads)
    shared = bias.shape[0] == 1
    if shared:
        bias_spec = pl.BlockSpec((1,) + bias.shape[1:], lambda h, w: (0, 0, 0))
    else:
        bias_spec = pl.BlockSpec((2,) + bias.shape[1:], lambda h, w: (h, 0, 0))
    return pl.pallas_call(
        functools.partial(attend_kernel, shared),
        grid=(pairs, windows),
        in_specs=[
            column_spec(rows, q[1]),
            column_spec(keys, k[1]),
            column_spec(keys, v[1]),
            bias_spec,
        ],
        out_specs=column_spec(rows, 0),
        out_shape=jax.ShapeDtypeStruct((windows, rows, pairs * PAIR), LOW),
        cost_estimate=pl.CostEstimate(
            flops=8 * windows * pairs * rows * keys * PAIR,
            bytes_accessed=windows * pairs * PAIR * 4 * (rows + keys),
            transcendentals=2 * windows * pairs * rows * keys,
        ),
        compiler_params=pltpu.CompilerParams(vmem_limit_bytes=32 * MIB),
    )(q[0], k[0], v[0], bias)


def attend_back(q, k, v, bias, do, heads):
    windows, rows, keys, pairs = attend_shapes(q, k, heads)
    shared = bias.shape[0] == 1
    if shared:
        bias_spec = pl.BlockSpec((1,) + bias.shape[1:], lambda h, w: (0, 0, 0))
    else:
        bias_spec = pl.BlockSpec((2,) + bias.shape[1:], lambda h, w: (h, 0, 0))
    out_specs = [column_spec(rows, 0), column_spec(keys, 0), column_spec(keys, 0)]
    out_shape = [
        jax.ShapeDtypeStruct((windows, rows, pairs * PAIR), LOW),
        jax.ShapeDtypeStruct((windows, keys, pairs * PAIR), LOW),
        jax.ShapeDtypeStruct((windows, keys, pairs * PAIR), LOW),
    ]
    if not shared:
        out_specs.append(pl.BlockSpec((2, rows, keys), lambda h, w: (h, 0, 0)))
        out_shape.append(jax.ShapeDtypeStruct((heads, rows, keys), HIGH))
    return pl.pallas_call(
        functools.partial(attend_back_kernel, shared),
        grid=(pairs, windows),
        in_specs=[
            column_spec(rows, q[1]),
            column_spec(keys, k[1]),
            column_spec(keys, v[1]),
            bias_spec,
            column_spec(rows, do[1]),
        ],
        out_specs=out_specs,
        out_shape=out_shape,
        cost_estimate=pl.CostEstimate(
            flops=20 * windows * pairs * rows * keys * PAIR,
            bytes_accessed=windows * pairs * PAIR * 6 * (rows + keys),
            transcendentals=2 * windows * pairs * rows * keys,
        ),
        compiler_params=pltpu.CompilerParams(vmem_limit_bytes=32 * MIB),
    )(q[0], k[0], v[0], bias, do[0])


SPANS = ((FRAMES, FRAMES - 1), (2 * BH, 2 * FRAMES - 1 + 2 * BH - 1), (4 * BW, 2 * FRAMES - 1 + 4 * BH - 1 + 4 * BW - 1))
SPAN = sum(size for size, _ in SPANS)


def table_picks():
    picks = np.zeros((SPAN, SPAN, REL), np.float32)
    start = 0
    for size, middle in SPANS:
        for i in range(size):
            for j in range(size):
                picks[start + i, start + j, middle + i - j] = 1
        start += size
    return picks


def place_hot(frame, row, column):
    marks = []
    for (size, _), place in zip(SPANS, (frame, row, column)):
        marks.append(place[:, None] == jnp.arange(size)[None, :])
    return jnp.concatenate(marks, 1).astype(HIGH)


def places_of(member, within):
    cell = within % CELLS
    return (
        within // CELLS + 0 * member,
        member // 4 * BH + cell // BW,
        member % 4 * BW + cell % BW,
    )


def bias_of(table, hot_q, hot_k):
    exact = lax.Precision.HIGHEST
    blocks = jnp.einsum("hn,abn->hab", table, table_picks(), precision=exact)
    left = jnp.einsum("ia,hab->hib", hot_q, blocks, precision=exact)
    return jnp.einsum("hib,jb->hij", left, hot_k, precision=exact)


def bias_grad(grad, hot_q, hot_k):
    exact = lax.Precision.HIGHEST
    right = jnp.einsum("hij,jb->hib", grad, hot_k, precision=exact)
    blocks = jnp.einsum("ia,hib->hab", hot_q, right, precision=exact)
    return jnp.einsum("hab,abn->hn", blocks, table_picks(), precision=exact)


def ring_sums(rights, lefts):
    count = lax.axis_size("dp")
    if count != 16:
        done = [
            high(lax.psum_scatter(x, "dp", scatter_dimension=0, tiled=True)) for x in rights + lefts
        ]
        return done[: len(rights)], done[len(rights) :]
    chips = count // 2
    order = [0, 2, 4, 6, 7, 5, 3, 1]
    chip_at = jnp.array(order, jnp.int32)
    place_of = jnp.array([order.index(i) for i in range(chips)], jnp.int32)
    device = lax.axis_index("dp")
    core = device % 2
    place = place_of[device // 2]

    def hop(x, way):
        route = []
        for s in range(2):
            for i in range(chips):
                for c in range(2):
                    route.append((s * count + order[i] * 2 + c, s * count + order[(i + way) % chips] * 2 + c))
        return lax.ppermute(x, ("section", "dp"), route)

    def prepare(x):
        x = x.reshape(chips, 2, x.shape[0] // count, x.shape[1])
        mine = lax.dynamic_index_in_dim(x, core, 1, keepdims=False)
        other = swap(lax.dynamic_index_in_dim(x, 1 - core, 1, keepdims=False), 1)
        return mine, other

    def at(pair, spot):
        chip = chip_at[spot % chips]
        return sum(high(lax.dynamic_index_in_dim(x, chip, 0, keepdims=False)) for x in pair)

    ways = [(prepare(x), 1) for x in rights] + [(prepare(x), -1) for x in lefts]
    totals = [at(pair, place - way + chips) for pair, way in ways]
    for step in range(1, chips):
        totals = [
            high(hop(low(total), way)) + at(pair, place - way * (step + 1) + 2 * chips)
            for total, (pair, way) in zip(totals, ways)
        ]
    return totals[: len(rights)], totals[len(rights) :]


def per_device(
    block_input,
    conditioning,
    text_embed,
    text_keep,
    cotangent,
    self_input,
    self_output,
    cross_query,
    cross_memory,
    cross_output,
    up_weight,
    down_weight,
    modulation,
    modulation_bias,
    position_bias,
):
    section = lax.axis_index("section")
    device = lax.axis_index("dp")
    count = lax.axis_size("dp")
    member = device % MEMBERS
    clip = device // MEMBERS
    clips = count // MEMBERS
    micro = block_input.shape[0]
    tokens = micro * ROWS
    shard = D // count
    members = [list(range(c * MEMBERS, (c + 1) * MEMBERS)) for c in range(clips)]

    def chosen(first, second):
        return jnp.where(section == 1, second, first)

    cond_low = low(jax.nn.silu(high(conditioning)))
    cond_rows = lax.dynamic_slice_in_dim(cond_low, device * shard, shard, 2)
    sums = jnp.einsum("bck,kn->cbn", cond_rows, low(modulation[0]), preferred_element_type=HIGH)
    bit = clips // 2
    while bit:
        upper = clip // bit % 2 == 1
        halves = (sums[:bit], sums[bit:])
        sums = jnp.where(upper, halves[1], halves[0]) + swap(
            jnp.where(upper, halves[0], halves[1]), bit * MEMBERS
        )
        bit //= 2
    sums = sums[0]
    for bit in (1, 2, 4):
        sums = sums + swap(sums, bit)
    mods = (sums + modulation_bias[0]).reshape(micro, 6, 1, D)
    shift1, scale1, gate1, shift2, scale2, gate2 = [mods[:, i] for i in range(6)]

    def gathered(x):
        return lax.all_gather(low(x[0]), "dp", axis=0, tiled=True)

    w_in = gathered(self_input)
    w_query = gathered(cross_query)
    w_self_out = gathered(self_output)
    w_cross_out = gathered(cross_output)
    w_up = gathered(up_weight)
    w_down = gathered(down_weight)
    w_in_x = xor_blocks(w_in, 1, PAIR, member, 3)
    w_self_out_x = xor_blocks(w_self_out, 0, PAIR, member)

    keep = lax.dynamic_index_in_dim(text_keep, clip, 1, keepdims=False).astype(LOW)
    text = text_embed * keep[:, None, None]
    text = jnp.pad(text, ((0, 0), (0, TEXT_PAD - text.shape[1]), (0, 0)))
    real = jnp.arange(TEXT_PAD * MEMBERS) % TEXT_PAD < text_embed.shape[1]
    text_mask = jnp.where(real, 0.0, NEGATIVE).astype(HIGH).reshape(1, 1, -1)

    def collect(x):
        parts = jnp.stack([x] + [swap(x, k) for k in range(1, MEMBERS)])
        return parts[member ^ jnp.arange(MEMBERS)]

    text_all = jnp.swapaxes(collect(text), 0, 1).reshape(micro * MEMBERS * TEXT_PAD, D)
    w_memory = low(cross_memory[0]).reshape(shard, 2, MEMBERS, PAIR)
    w_memory = jnp.transpose(w_memory, (2, 0, 1, 3)).reshape(MEMBERS, shard, 2 * PAIR)
    w_memory = lax.all_to_all(jnp.tile(w_memory, (clips, 1, 1)), "dp", 0, 0, tiled=True)
    w_memory = w_memory.reshape(D, 2 * PAIR)
    memory = low(dot(text_all, w_memory)).reshape(micro, MEMBERS * TEXT_PAD, 2 * PAIR)
    memory = collect(memory).reshape(MEMBERS, micro, MEMBERS * TEXT_PAD, 2, PAIR)
    memory = jnp.transpose(memory, (1, 2, 3, 0, 4)).reshape(micro, MEMBERS * TEXT_PAD, 2 * D)

    within = jnp.arange(ROWS)
    mine, partner = places_of(member, within), places_of(member ^ 1, within)
    hot_q1 = place_hot(*mine)
    hot_k1 = jnp.concatenate([hot_q1, place_hot(*partner)])
    bias1 = bias_of(position_bias[0], hot_q1, hot_k1)
    spread = jnp.arange(MEMBERS * CELLS)
    frame_places = places_of(member ^ (spread // CELLS), spread % CELLS)
    hot0 = place_hot(*frame_places)
    own_table = lax.dynamic_slice_in_dim(position_bias[0], 2 * member, 2, 0)
    bias0 = bias_of(own_table, hot0, hot0)

    def heads_of_frames(x):
        width = x.shape[1] // MEMBERS
        parts = [x[:, k * width : (k + 1) * width] for k in range(MEMBERS)]
        parts = [parts[0]] + [swap(parts[k], k, (0,)) for k in range(1, MEMBERS)]
        parts = [part.reshape(micro * FRAMES, CELLS, width) for part in parts]
        return jnp.concatenate(parts, 1)

    def heads_back(x):
        width = x.shape[2]
        parts = [x[:, k * CELLS : (k + 1) * CELLS].reshape(tokens, width) for k in range(MEMBERS)]
        parts = [parts[0]] + [swap(parts[k], k, (0,)) for k in range(1, MEMBERS)]
        return jnp.concatenate(parts, 1)

    def forward(which, inputs):
        kept = {"x": inputs}
        hidden = low(layer_mod(inputs, shift1, scale1)).reshape(tokens, D)
        kept["hidden"] = hidden
        asked = low(dot(hidden, w_query)).reshape(micro, ROWS, D)
        kept["asked"] = asked
        if which == 0:
            joint = heads_of_frames(low(dot(hidden, w_in_x)))
            kept["joint"] = joint
            mixture = heads_back(attend((joint, 0), (joint, 1), (joint, 2), bias0, 2))
            w_out = w_self_out_x
        else:
            joint = low(dot(hidden, w_in)).reshape(micro, ROWS, 3 * D)
            pair = joint[:, :, D:]
            pair = jnp.concatenate([pair, swap(pair, 1, (1,))], 1)
            kept["joint"] = joint
            kept["pair"] = pair
            mixture = attend((joint, 0), (pair, 0), (pair, MEMBERS), bias1, HEADS).reshape(tokens, D)
            w_out = w_self_out
        mixture_text = attend((asked, 0), (memory, 0), (memory, MEMBERS), text_mask, HEADS)
        mixture_text = mixture_text.reshape(tokens, D)
        branch = (dot(mixture, w_out) + dot(mixture_text, w_cross_out)).reshape(micro, ROWS, D)
        middle = inputs + gate1 * branch
        second = low(layer_mod(middle, shift2, scale2)).reshape(tokens, D)
        upper = dot(second, w_up)
        active = low(jax.nn.gelu(upper))
        feed = dot(active, w_down).reshape(micro, ROWS, D)
        result = low(middle + gate2 * feed)
        kept.update(
            mixture=mixture,
            mixture_text=mixture_text,
            branch=branch,
            middle=middle,
            second=second,
            upper=upper,
            active=active,
            feed=feed,
        )
        return result, kept

    def back_feed(which, kept, grad_result):
        out = {}
        gate2_grad = jnp.sum(grad_result * kept["feed"], 1)
        feed_grad = low(gate2 * grad_result).reshape(tokens, D)
        active_grad = dot_right_t(feed_grad, w_down)
        upper_grad = low(jax.vjp(jax.nn.gelu, kept["upper"])[1](active_grad)[0])
        second_grad = dot_right_t(upper_grad, w_up).reshape(micro, ROWS, D)
        middle_norm, shift2_grad, scale2_grad = jax.vjp(layer_mod, kept["middle"], shift2, scale2)[1](second_grad)
        out["feed_grad"] = feed_grad
        out["upper_grad"] = upper_grad
        out["middle_grad"] = grad_result + middle_norm
        out["late"] = [shift2_grad[:, 0], scale2_grad[:, 0], gate2_grad]
        return out

    def back_attention(which, kept, out):
        middle_grad = out["middle_grad"]
        gate1_grad = jnp.sum(middle_grad * kept["branch"], 1)
        branch_grad = low(gate1 * middle_grad).reshape(tokens, D)
        out["branch_grad"] = branch_grad
        text_grad = low(dot_right_t(branch_grad, w_cross_out)).reshape(micro, ROWS, D)
        if which == 0:
            mixture_grad = heads_of_frames(low(dot_right_t(branch_grad, w_self_out_x)))
            joint = kept["joint"]
            dq, dk, dv, dbias = attend_back(
                (joint, 0), (joint, 1), (joint, 2), bias0, (mixture_grad, 0), 2
            )
            joint_grad = heads_back(jnp.concatenate([dq, dk, dv], 2))
            hidden_grad = dot_right_t(joint_grad, w_in_x)
            out["joint_grad"] = xor_blocks_back(joint_grad, 1, PAIR, member, 3)
            table = bias_grad(dbias, hot0, hot0)
            out["table"] = lax.dynamic_update_slice_in_dim(
                jnp.zeros((HEADS, REL), HIGH), table, 2 * member, 0
            )
            out["mixture"] = xor_blocks(kept["mixture"], 1, PAIR, member)
        else:
            mixture_grad = low(dot_right_t(branch_grad, w_self_out)).reshape(micro, ROWS, D)
            joint, pair = kept["joint"], kept["pair"]
            dq, dk, dv, dbias = attend_back(
                (joint, 0), (pair, 0), (pair, MEMBERS), bias1, (mixture_grad, 0), HEADS
            )
            pair_grad = jnp.concatenate([dk, dv], 2)
            arrived = swap(pair_grad[:, ROWS:], 1, (1,))
            own = low(high(pair_grad[:, :ROWS]) + high(arrived))
            joint_grad = jnp.concatenate([dq, own], 2).reshape(tokens, 3 * D)
            hidden_grad = dot_right_t(joint_grad, w_in)
            out["joint_grad"] = joint_grad
            out["table"] = bias_grad(dbias, hot_q1, hot_k1)
            out["mixture"] = kept["mixture"]
        dqt, dkt, dvt = attend_back(
            (kept["asked"], 0), (memory, 0), (memory, MEMBERS), text_mask, (text_grad, 0), HEADS
        )
        asked_grad = dqt.reshape(tokens, D)
        out["asked_grad"] = asked_grad
        out["memory_grad"] = jnp.concatenate([dkt, dvt], 2)
        hidden_grad = hidden_grad + dot_right_t(asked_grad, w_query)
        inputs_norm, shift1_grad, scale1_grad = jax.vjp(layer_mod, kept["x"], shift1, scale1)[1](
            hidden_grad.reshape(micro, ROWS, D)
        )
        out["mods"] = jnp.concatenate(
            [shift1_grad[:, 0], scale1_grad[:, 0], gate1_grad] + out["late"], 1
        )
        return low(middle_grad + inputs_norm)

    first_result, first_kept = forward(0, high(block_input))
    received = lax.ppermute(first_result, "section", [(0, 1)])
    second_result, second_kept = forward(1, high(received))
    second_out = back_feed(1, second_kept, high(cotangent))
    second_grad = back_attention(1, second_kept, second_out)
    returned = lax.ppermute(second_grad, "section", [(1, 0)])
    first_out = back_feed(0, first_kept, high(returned))

    def both(name):
        if name in first_out:
            return chosen(first_out[name], second_out[name])
        return chosen(first_kept[name], second_kept[name])

    def outer(left, right):
        return low(dot_left_t(left, right))

    grad_up = outer(both("second"), both("upper_grad"))
    grad_down = outer(both("active"), both("feed_grad"))
    (up_shard,), (down_shard,) = ring_sums([grad_up], [grad_down])

    first_grad = back_attention(0, first_kept, first_out)
    branch_grad = both("branch_grad")
    hidden = both("hidden")
    grad_self_out = outer(both("mixture"), branch_grad)
    grad_cross_out = outer(both("mixture_text"), branch_grad)
    grad_in = outer(hidden, both("joint_grad"))
    grad_query = outer(hidden, both("asked_grad"))
    (in_shard,), (out_shard, cross_shard, query_shard) = ring_sums(
        [grad_in], [grad_self_out, grad_cross_out, grad_query]
    )

    memory_grad = both("memory_grad").reshape(micro, MEMBERS * TEXT_PAD, 2, MEMBERS, PAIR)
    memory_grad = jnp.transpose(memory_grad, (3, 0, 1, 2, 4)).reshape(MEMBERS, -1, 2 * PAIR)
    memory_grad = lax.all_to_all(memory_grad, "dp", 0, 0, tiled=True, axis_index_groups=members)
    memory_grad = low(jnp.sum(high(memory_grad), 0))
    grad_memory = outer(text_all, memory_grad).reshape(count, shard, 2 * PAIR)
    grad_memory = lax.all_to_all(grad_memory, "dp", 0, 0, tiled=True)
    grad_memory = jnp.sum(high(grad_memory).reshape(clips, MEMBERS, shard, 2, PAIR), 0)
    memory_shard = jnp.transpose(grad_memory, (1, 2, 0, 3)).reshape(shard, 2 * D)

    mods_grad = both("mods").reshape(micro * 6 * D)
    table_grad = both("table").reshape(HEADS * REL)
    small = jnp.concatenate([mods_grad, table_grad])
    small = jnp.pad(small, (0, -small.shape[0] % 1024)).reshape(-1, 128)
    small = lax.all_gather(small, "dp", axis=0, tiled=False).reshape(count, -1)
    mods_all = small[:, : micro * 6 * D].reshape(count, micro, 6 * D)
    table_sum = jnp.sum(small[:, micro * 6 * D : micro * 6 * D + HEADS * REL], 0).reshape(HEADS, REL)
    conds = jnp.repeat(jnp.swapaxes(cond_rows, 0, 1), MEMBERS, axis=0)
    modul_shard = jnp.einsum(
        "nbk,nbc->kc", high(conds), mods_all, precision=lax.Precision.HIGHEST
    )
    bias_sum = jnp.sum(mods_all, (0, 1))

    outputs = chosen(first_result, second_result)
    input_grads = chosen(first_grad, second_grad)
    return tuple(
        x[None]
        for x in (
            outputs,
            input_grads,
            in_shard,
            out_shard,
            query_shard,
            memory_shard,
            cross_shard,
            up_shard,
            down_shard,
            modul_shard,
            bias_sum,
            table_sum,
        )
    )


def solution(mesh):
    weights = P("section", "dp", None)
    return jax.shard_map(
        per_device,
        mesh=mesh,
        in_specs=(
            P(None, "dp", None),
            P(),
            P(None, "dp", None),
            P(),
            P(None, "dp", None),
        )
        + (weights,) * 8
        + (P("section", None), P("section", None, None)),
        out_specs=(P("section", None, "dp", None),) * 2
        + (weights,) * 8
        + (P("section", None), P("section", None, None)),
        check_vma=False,
    )
```

```python
import functools

import jax
import jax.numpy as jnp
import numpy as np
from jax import lax
from jax.experimental import pallas as pl
from jax.experimental.pallas import tpu as pltpu
from jax.sharding import PartitionSpec as P

D = 1024
HEADS = 16
HEAD = 64
FF = 4096
FRAMES = 5
BH = 8
BW = 4
CELLS = BH * BW
ROWS = 160
REL = 71
MEMBERS = 8
PAIR = 2 * HEAD
EPSILON = 1e-06
LOW = jnp.bfloat16
HIGH = jnp.float32
MIB = 1024 * 1024
SHORT = pl.CostEstimate(flops=1, bytes_accessed=1, transcendentals=0)


def dot(left, right):
    return lax.dot_general(left, right, (((1,), (0,)), ((), ())), preferred_element_type=HIGH)


def dot_right_t(left, right):
    return lax.dot_general(left, right, (((1,), (1,)), ((), ())), preferred_element_type=HIGH)


def dot_left_t(left, right):
    return lax.dot_general(left, right, (((0,), (0,)), ((), ())), preferred_element_type=HIGH)


def low(v):
    return v.astype(LOW)


def high(v):
    return v.astype(HIGH)


def layer_mod(inputs, offset, factor):
    average = jnp.mean(inputs, axis=-1, keepdims=True)
    centred = inputs - average
    spread = jnp.mean(centred * centred, axis=-1, keepdims=True)
    return centred * lax.rsqrt(spread + EPSILON) * (1.0 + factor) + offset


def swap(x, bits, sections=(0, 1)):
    count = lax.axis_size("dp")
    route = [(s * count + i, s * count + (i ^ bits)) for s in sections for i in range(count)]
    return lax.ppermute(x, ("section", "dp"), route)


def head_masks():
    lane = lax.broadcasted_iota(jnp.int32, (1, PAIR), 1)
    first = (lane < HEAD).astype(LOW)
    return first, 1 - first


def by_head(first, second):
    lane = lax.broadcasted_iota(jnp.int32, (1, PAIR), 1)
    return low(jnp.where(lane < HEAD, first, second))


def pairs_forward(pairs):
    masks = [mask * LOW(HEAD ** (-0.5)) for mask in head_masks()]
    heads = [(q * mask, k, v, bias) for q, k, v, biases in pairs for mask, bias in zip(masks, biases)]
    scores = [dot_right_t(q, k) + bias for q, k, _, bias in heads]
    highest = [jnp.max(x, axis=-1, keepdims=True) for x in scores]
    exponents = [jnp.exp(x - y) for x, y in zip(scores, highest)]
    totals = [jnp.sum(x, axis=-1, keepdims=True) for x in exponents]
    mixed = [dot(low(x), head[2]) * (1.0 / total) for x, head, total in zip(exponents, heads, totals)]
    norms = [x + jnp.log(y) for x, y in zip(highest, totals)]
    return [(by_head(*mixed[i : i + 2]), norms[i : i + 2]) for i in range(0, len(heads), 2)]


def pairs_backward(pairs):
    masks = head_masks()
    heads = [
        (q * mask, k, v, do * mask, bias, norm)
        for q, k, v, do, biases, norms in pairs
        for mask, bias, norm in zip(masks, biases, norms)
    ]
    scale = HEAD ** (-0.5)
    soft = [jnp.exp(dot_right_t(q * LOW(scale), k) + bias - norm) for q, k, _, _, bias, norm in heads]
    grads = [dot_right_t(do, v) for _, _, v, do, _, _ in heads]
    means = [jnp.sum(x * y, axis=-1, keepdims=True) for x, y in zip(soft, grads)]
    grads = [x * (y - z) for x, y, z in zip(soft, grads, means)]
    raw = [low(x * scale) for x in grads]
    dq = [dot(x, head[1]) for x, head in zip(raw, heads)]
    dk = [dot_left_t(head[0], x) for x, head in zip(raw, heads)]
    dv = [dot_left_t(head[3], low(x)) for x, head in zip(soft, heads)]
    return [
        (by_head(*dq[i : i + 2]), low((dk[i] + dk[i + 1]).T), low((dv[i] + dv[i + 1]).T), grads[i : i + 2])
        for i in range(0, len(heads), 2)
    ]


def add_over_steps(ref, index, value, axis):
    @pl.when(pl.program_id(axis) == 0)
    def _():
        ref[index] = value

    @pl.when(pl.program_id(axis) > 0)
    def _():
        ref[index] += value


def part_of(block, part):
    return block[:, part * PAIR : (part + 1) * PAIR]


def frames_pairs(joint_ref, bias_ref):
    for w in range(joint_ref.shape[1]):
        x = joint_ref[:, w].reshape(MEMBERS * CELLS, 3 * PAIR)
        yield part_of(x, 0), part_of(x, 1), part_of(x, 2), (bias_ref[0], bias_ref[1])


def frames_forward(joint_ref, bias_ref, o_ref, norm_ref):
    for w, (o, norms) in enumerate(pairs_forward(list(frames_pairs(joint_ref, bias_ref)))):
        o_ref[:, w] = o.reshape(MEMBERS, CELLS, PAIR)
        norm_ref[w] = jnp.concatenate(norms, 1)


def frames_backward(joint_ref, bias_ref, norm_ref, do_ref, grad_ref, dbias_ref):
    pairs = []
    for w, (q, k, v, biases) in enumerate(frames_pairs(joint_ref, bias_ref)):
        do = do_ref[:, w].reshape(MEMBERS * CELLS, PAIR)
        pairs.append((q, k, v, do, biases, (norm_ref[w, :, 0:1], norm_ref[w, :, 1:2])))
    sums = [0.0, 0.0]
    for w, (dq, dk, dv, dbias) in enumerate(pairs_backward(pairs)):
        for part, value in enumerate((dq, dk, dv)):
            grad_ref[:, w, :, part * PAIR : (part + 1) * PAIR] = value.reshape(MEMBERS, CELLS, PAIR)
        sums = [s + d for s, d in zip(sums, dbias)]
    for a in range(2):
        add_over_steps(dbias_ref, a, sums[a], 0)


def window_pairs(own_ref, other_ref, bias_ref):
    for h in range(own_ref.shape[0]):
        own, other = own_ref[h], other_ref[h]
        k, v = [jnp.concatenate([part_of(own, p), part_of(other, p)], 0) for p in (1, 2)]
        yield part_of(own, 0), k, v, (bias_ref[2 * h], bias_ref[2 * h + 1])


def window_forward(own_ref, other_ref, bias_ref, o_ref, norm_ref):
    made = pairs_forward(list(window_pairs(own_ref, other_ref, bias_ref)))
    for h, (o, _) in enumerate(made):
        o_ref[h] = o
    norm_ref[0, 0] = jnp.concatenate([norm for _, norms in made for norm in norms], 1)


def window_backward(own_ref, other_ref, bias_ref, norm_ref, do_ref, own_grad_ref, other_grad_ref, dbias_ref):
    norms = norm_ref[0, 0]
    pairs = []
    for h, (q, k, v, biases) in enumerate(window_pairs(own_ref, other_ref, bias_ref)):
        pairs.append((q, k, v, do_ref[h], biases, (norms[:, 2 * h : 2 * h + 1], norms[:, 2 * h + 1 : 2 * h + 2])))
    for h, (dq, dk, dv, dbias) in enumerate(pairs_backward(pairs)):
        own_grad_ref[h] = jnp.concatenate([dq, dk[:ROWS], dv[:ROWS]], 1)
        other_grad_ref[h] = jnp.concatenate([dk[ROWS:], dv[ROWS:]], 1)
        for a in range(2):
            add_over_steps(dbias_ref, 2 * h + a, dbias[a], 1)


def text_pairs(q_ref, k_ref, v_ref):
    for h in range(q_ref.shape[1] // PAIR):
        yield part_of(q_ref[...], h), part_of(k_ref[0], h), part_of(v_ref[0], h), (0.0, 0.0)


def text_forward(q_ref, k_ref, v_ref, o_ref, norm_ref):
    made = pairs_forward(list(text_pairs(q_ref, k_ref, v_ref)))
    o_ref[...] = jnp.concatenate([o for o, _ in made], 1)
    norm_ref[0, 0] = jnp.concatenate([norm for _, norms in made for norm in norms], 1)


def text_backward(q_ref, k_ref, v_ref, norm_ref, do_ref, dq_ref, dk_ref, dv_ref):
    norms = norm_ref[0, 0]
    pairs = []
    for h, (q, k, v, biases) in enumerate(text_pairs(q_ref, k_ref, v_ref)):
        heads = (norms[:, 2 * h : 2 * h + 1], norms[:, 2 * h + 1 : 2 * h + 2])
        pairs.append((q, k, v, part_of(do_ref[...], h), biases, heads))
    made = pairs_backward(pairs)
    dq_ref[...], dk_ref[0], dv_ref[0] = [jnp.concatenate([x[i] for x in made], 1) for i in range(3)]


def call(kernel, grid, in_specs, out_specs, out_shape, operands, limit=20):
    return pl.pallas_call(
        kernel,
        grid=grid,
        in_specs=in_specs,
        out_specs=out_specs,
        out_shape=out_shape,
        cost_estimate=SHORT,
        compiler_params=pltpu.CompilerParams(vmem_limit_bytes=limit * MIB),
    )(*operands)


def shaped(shape, dtype=LOW):
    return jax.ShapeDtypeStruct(shape, dtype)


GROUP = 4
GROUPS = HEADS // 2 // GROUP


def frames_specs(joint):
    steps = joint.shape[1] // FRAMES
    wide = pl.BlockSpec((MEMBERS, FRAMES, CELLS, 3 * PAIR), lambda i: (0, i, 0, 0))
    narrow = pl.BlockSpec((MEMBERS, FRAMES, CELLS, PAIR), lambda i: (0, i, 0, 0))
    size = MEMBERS * CELLS
    bias = pl.BlockSpec((2, size, size), lambda i: (0, 0, 0))
    norm = pl.BlockSpec((FRAMES, size, 2), lambda i: (i, 0, 0))
    return steps, wide, narrow, bias, norm


def attend_frames(joint, bias):
    steps, wide, narrow, bias_spec, norm = frames_specs(joint)
    size = MEMBERS * CELLS
    return call(
        frames_forward,
        (steps,),
        [wide, bias_spec],
        [narrow, norm],
        [shaped(joint.shape[:3] + (PAIR,)), shaped((steps * FRAMES, size, 2), HIGH)],
        (joint, bias),
    )


def attend_frames_back(joint, bias, norms, do):
    steps, wide, narrow, bias_spec, norm = frames_specs(joint)
    size = MEMBERS * CELLS
    return call(
        frames_backward,
        (steps,),
        [wide, bias_spec, norm, narrow],
        [wide, bias_spec],
        [shaped(joint.shape), shaped((2, size, size), HIGH)],
        (joint, bias, norms, do),
    )


def window_specs(width):
    return pl.BlockSpec((GROUP, ROWS, width), lambda g, w: (g, w, 0))


BIAS_SPEC = pl.BlockSpec((2 * GROUP, ROWS, 2 * ROWS), lambda g, w: (g, 0, 0))
NORM_SPEC = pl.BlockSpec((1, 1, ROWS, 2 * GROUP), lambda g, w: (g, w, 0, 0))


def attend_window(own, other, bias):
    micro = own.shape[1] // ROWS
    return call(
        window_forward,
        (GROUPS, micro),
        [window_specs(3 * PAIR), window_specs(3 * PAIR), BIAS_SPEC],
        [window_specs(PAIR), NORM_SPEC],
        [shaped(own.shape[:2] + (PAIR,)), shaped((GROUPS, micro, ROWS, 2 * GROUP), HIGH)],
        (own, other, bias),
    )


def attend_window_back(own, other, bias, norms, do):
    micro = own.shape[1] // ROWS
    return call(
        window_backward,
        (GROUPS, micro),
        [window_specs(3 * PAIR), window_specs(3 * PAIR), BIAS_SPEC, NORM_SPEC, window_specs(PAIR)],
        [window_specs(3 * PAIR), window_specs(2 * PAIR), BIAS_SPEC],
        [shaped(own.shape), shaped(own.shape[:2] + (2 * PAIR,)), shaped(bias.shape, HIGH)],
        (own, other, bias, norms, do),
    )


def text_specs(keys):
    rows = pl.BlockSpec((ROWS, GROUP * PAIR), lambda g, w: (w, g))
    k = pl.BlockSpec((1, keys, GROUP * PAIR), lambda g, w: (w, 0, g))
    v = pl.BlockSpec((1, keys, GROUP * PAIR), lambda g, w: (w, 0, GROUPS + g))
    return rows, k, v


def attend_text(asked, memory):
    micro, keys = memory.shape[:2]
    rows, k, v = text_specs(keys)
    return call(
        text_forward,
        (GROUPS, micro),
        [rows, k, v],
        [rows, NORM_SPEC],
        [shaped(asked.shape), shaped((GROUPS, micro, ROWS, 2 * GROUP), HIGH)],
        (asked, memory, memory),
    )


def attend_text_back(asked, memory, norms, do):
    micro, keys = memory.shape[:2]
    rows, k, v = text_specs(keys)
    return call(
        text_backward,
        (GROUPS, micro),
        [rows, k, v, NORM_SPEC, rows],
        [rows, k, k],
        [shaped(asked.shape), shaped((micro, keys, D)), shaped((micro, keys, D))],
        (asked, memory, memory, norms, do),
    )


PARTS = 16
ROWS_OF_PART = D // PARTS
SET = 4 * PAIR
STRIP = FF // 8
LARGE = 40


def block_spec(first):
    return pl.BlockSpec((PARTS, ROWS_OF_PART, SET), lambda j: (0, first + (j >> 1), j & 1))


def joined(ref):
    return ref[...].reshape(-1, ref.shape[-1])


def rows_spec(shape):
    return pl.BlockSpec(shape, lambda j: (0,) * len(shape))


def project_kernel(hidden_ref, w_ref, joint_ref, asked_ref):
    made = low(dot(hidden_ref[...], joined(w_ref)))
    joint_ref[0] = made[:, : 3 * PAIR]
    asked_ref[...] = made[:, 3 * PAIR :]


def project(hidden, packed):
    tokens = hidden.shape[0]
    return call(
        project_kernel,
        (MEMBERS,),
        [rows_spec((tokens, D)), block_spec(0)],
        [pl.BlockSpec((1, tokens, 3 * PAIR), lambda m: (m, 0, 0)), pl.BlockSpec((tokens, PAIR), lambda m: (0, m))],
        [shaped((MEMBERS, tokens, 3 * PAIR)), shaped((tokens, D))],
        (hidden, packed),
    )


def project_back_kernel(joint_ref, asked_ref, w_ref, out_ref):
    grad = jnp.concatenate([joint_ref[0], asked_ref[...]], 1)
    add_over_steps(out_ref, slice(None), dot_right_t(grad, joined(w_ref)), 0)


def project_back(joint_grad, asked_grad, packed):
    tokens = asked_grad.shape[0]
    return call(
        project_back_kernel,
        (MEMBERS,),
        [
            pl.BlockSpec((1, tokens, 3 * PAIR), lambda m: (m, 0, 0)),
            pl.BlockSpec((tokens, PAIR), lambda m: (0, m)),
            block_spec(0),
        ],
        rows_spec((tokens, D)),
        shaped((tokens, D), HIGH),
        (joint_grad, asked_grad, packed),
    )


def text_project_kernel(text_ref, w_ref, out_ref):
    out_ref[...] = low(dot(text_ref[...], joined(w_ref)))


def text_project(text, packed):
    return call(
        text_project_kernel,
        (2 * D // SET,),
        [rows_spec(text.shape), block_spec(6)],
        pl.BlockSpec((text.shape[0], SET), lambda j: (0, j)),
        shaped((text.shape[0], 2 * D)),
        (text, packed),
        LARGE,
    )


def merge_kernel(o_ref, text_ref, w_self_ref, w_cross_ref, out_ref):
    o = jnp.concatenate([o_ref[m] for m in range(MEMBERS)], 1)
    out_ref[...] = dot(o, joined(w_self_ref)) + dot(text_ref[...], joined(w_cross_ref))


def merge(o, text, packed):
    tokens = text.shape[0]
    return call(
        merge_kernel,
        (D // SET,),
        [rows_spec((MEMBERS, tokens, PAIR)), rows_spec((tokens, D)), block_spec(0), block_spec(1)],
        pl.BlockSpec((tokens, SET), lambda j: (0, j)),
        shaped((tokens, D), HIGH),
        (o, text, packed, packed),
        LARGE,
    )


def merge_back_kernel(grad_ref, w_self_ref, w_cross_ref, o_ref, text_ref):
    made = low(dot_right_t(grad_ref[...], joined(w_self_ref)))
    for m in range(o_ref.shape[0]):
        o_ref[m] = part_of(made, m)
    text_ref[...] = low(dot_right_t(grad_ref[...], joined(w_cross_ref)))


def merge_back(grad, packed):
    tokens = grad.shape[0]
    height = 2 * PAIR
    parts = height // ROWS_OF_PART
    return call(
        merge_back_kernel,
        (D // height,),
        [
            rows_spec((tokens, D)),
            pl.BlockSpec((parts, ROWS_OF_PART, D), lambda j: (j, 0, 0)),
            pl.BlockSpec((parts, ROWS_OF_PART, D), lambda j: (j, 1, 0)),
        ],
        [pl.BlockSpec((2, tokens, PAIR), lambda j: (j, 0, 0)), pl.BlockSpec((tokens, height), lambda j: (0, j))],
        [shaped((MEMBERS, tokens, PAIR)), shaped((tokens, D))],
        (grad, packed, packed),
        LARGE,
    )


def feed_kernel(s_ref, up_ref, down_ref, upper_ref, active_ref, feed_ref):
    upper = dot(s_ref[...], joined(up_ref))
    active = low(jax.nn.gelu(upper))
    upper_ref[...] = upper
    active_ref[...] = active
    add_over_steps(feed_ref, slice(None), dot(active, joined(down_ref)), 0)


def feed_specs(tokens):
    strip = pl.BlockSpec((tokens, STRIP), lambda j: (0, j))
    down = pl.BlockSpec((STRIP // (FF // PARTS), FF // PARTS, D), lambda j: (j, 2, 0))
    return rows_spec((tokens, D)), strip, block_spec(2), down


def feed_call(second, packed):
    tokens = second.shape[0]
    full, strip, up, down = feed_specs(tokens)
    return call(
        feed_kernel,
        (FF // STRIP,),
        [full, up, down],
        [strip, strip, full],
        [shaped((tokens, FF), HIGH), shaped((tokens, FF)), shaped((tokens, D), HIGH)],
        (second, packed, packed),
        LARGE,
    )


def feed_back_kernel(f_ref, upper_ref, up_ref, down_ref, upper_grad_ref, second_grad_ref):
    active_grad = dot_right_t(f_ref[...], joined(down_ref))
    upper_grad = low(jax.vjp(jax.nn.gelu, upper_ref[...])[1](active_grad)[0])
    upper_grad_ref[...] = upper_grad
    add_over_steps(second_grad_ref, slice(None), dot_right_t(upper_grad, joined(up_ref)), 0)


def feed_back_call(feed_grad, upper, packed):
    tokens = feed_grad.shape[0]
    full, strip, up, down = feed_specs(tokens)
    return call(
        feed_back_kernel,
        (FF // STRIP,),
        [full, strip, up, down],
        [strip, full],
        [shaped((tokens, FF)), shaped((tokens, D), HIGH)],
        (feed_grad, upper, packed, packed),
        LARGE,
    )


def pack_columns(x):
    rows = x.shape[0]
    return jnp.swapaxes(x.reshape(rows, -1, D), 0, 1).reshape(-1, D)


def unpack_columns(x, blocks):
    return jnp.swapaxes(x.reshape(blocks, -1, D), 0, 1).reshape(-1, blocks * D)


SPANS = ((FRAMES, FRAMES - 1), (2 * BH, 2 * FRAMES - 1 + 2 * BH - 1), (4 * BW, 2 * FRAMES - 1 + 4 * BH - 1 + 4 * BW - 1))
SPAN = sum(size for size, _ in SPANS)


def table_picks():
    picks = np.zeros((SPAN, SPAN, REL), np.float32)
    start = 0
    for size, middle in SPANS:
        for i in range(size):
            for j in range(size):
                picks[start + i, start + j, middle + i - j] = 1
        start += size
    return picks


def place_hot(frame, row, column):
    marks = []
    for (size, _), place in zip(SPANS, (frame, row, column)):
        marks.append(place[:, None] == jnp.arange(size)[None, :])
    return jnp.concatenate(marks, 1).astype(HIGH)


def places_of(member, within):
    cell = within & (CELLS - 1)
    return (
        within // CELLS + 0 * member,
        (member >> 2) * BH + cell // BW,
        (member & 3) * BW + (cell & (BW - 1)),
    )


def bias_of(table, hot_q, hot_k):
    exact = lax.Precision.HIGHEST
    blocks = jnp.einsum("hn,abn->hab", table, table_picks(), precision=exact)
    left = jnp.einsum("ia,hab->hib", hot_q, blocks, precision=exact)
    return jnp.einsum("hib,jb->hij", left, hot_k, precision=exact)


def bias_grad(grad, hot_q, hot_k):
    exact = lax.Precision.HIGHEST
    right = jnp.einsum("hij,jb->hib", grad, hot_k, precision=exact)
    blocks = jnp.einsum("ia,hib->hab", hot_q, right, precision=exact)
    return jnp.einsum("hab,abn->hn", blocks, table_picks(), precision=exact)


RING = [0, 2, 4, 6, 7, 5, 3, 1]
WAYS = (1, -1)


def together(*values):
    return lax.optimization_barrier(values)


def device_ring():
    device = lax.axis_index("dp")
    chip = device >> 1
    half = len(RING) // 2
    place = jnp.where((chip & 1) == 1, 2 * half - 1 - (chip >> 1), chip >> 1)
    spots = (place + jnp.arange(2 * half)) & (2 * half - 1)
    return jnp.where(spots < half, 2 * spots, 4 * half - 1 - 2 * spots), device & 1


def hop(x, way):
    count = lax.axis_size("dp")
    chips = len(RING)
    route = []
    for s in range(2):
        for i in range(chips):
            for c in range(2):
                source = s * count + RING[i] * 2 + c
                route.append((source, s * count + RING[(i + way) % chips] * 2 + c))
    return lax.ppermute(x, ("section", "dp"), route)


def ring_gather(own):
    chips = len(RING)
    half = own.shape[0] // 2
    chunks = [own[:half], own[half:]]
    held = []
    side = ()
    for step in range(chips):
        last = step + 1 == chips
        if not last:
            following = [hop(chunk, way) for chunk, way in zip(chunks, WAYS)]
        held.append([list(chunks), [swap(chunk, 1) for chunk in chunks]])
        if not last:
            side = yield side
            before = [x for pair in held[:-1] for x in pair[1]]
            tied = together(*following, *before, *side)
            chunks = list(tied[:2])
            for i, pair in enumerate(held[:-1]):
                pair[1] = list(tied[2 + 2 * i : 4 + 2 * i])
            side = tied[2 + len(before) :]
        if step == EARLY:
            made = assembled(held, 0, None)
        if step == EARLY + 1:
            made, *chunks = together(made, *chunks)
    return assembled(held, EARLY, made), side


EARLY = 5


def assembled(held, start, made):
    held = held[start:EARLY] if made is None else held[start:]
    chips = len(RING)
    spots, core = device_ring()
    order = jnp.concatenate([spots, jnp.broadcast_to(core, (1,))]).astype(jnp.int32)
    flat = [x for own, other in held for x in own + other]
    half = flat[0].shape[0]
    shape = (chips, 2, 2 * half, D)

    def kernel(order_ref, *refs):
        sources, (sink, scratch, arrive, leave) = refs[: len(flat)], refs[-4:]
        arriving, leaving = [], []
        for i, ref in enumerate(sources):
            step, which, way = start + i // 4, i // 2 % 2, i % 2
            spot = order_ref[-WAYS[way] * step % chips]
            place = order_ref[chips] if which == 0 else 1 - order_ref[chips]
            where = (spot, place, pl.ds(way * half, half))
            arriving.append(pltpu.make_async_copy(ref, scratch.at[i], arrive.at[i]))
            leaving.append(pltpu.make_async_copy(scratch.at[i], sink.at[where], leave.at[i]))
        for copy in arriving:
            copy.start()
        for copy, onward in zip(arriving, leaving):
            copy.wait()
            onward.start()
        for copy in leaving:
            copy.wait()

    operands = flat if made is None else flat + [made]
    anywhere = pl.BlockSpec(memory_space=pl.ANY)
    made = pl.pallas_call(
        kernel,
        grid_spec=pltpu.PrefetchScalarGridSpec(
            num_scalar_prefetch=1,
            grid=(),
            in_specs=[anywhere] * len(operands),
            out_specs=anywhere,
            scratch_shapes=[pltpu.VMEM((len(flat),) + flat[0].shape, LOW)]
            + [pltpu.SemaphoreType.DMA((len(flat),))] * 2,
        ),
        out_shape=shaped(shape),
        input_output_aliases={} if made is None else {1 + len(flat): 0},
        cost_estimate=SHORT,
        compiler_params=pltpu.CompilerParams(vmem_limit_bytes=58 * MIB),
    )(order, *operands)
    return made if start == 0 else made.reshape(PARTS, 2 * half, D)


def ring_sums(right, left):
    def term(step):
        return [jnp.concatenate([high(x[step]) for x in arrays], 0) for arrays in (right, left)]

    totals = term(0)
    side = ()
    for step in range(1, len(RING)):
        arrived = [hop(low(total), way) for total, way in zip(totals, WAYS)]
        side = yield side
        tied = together(*arrived, *side)
        side = tied[2:]
        totals = [high(x) + y for x, y in zip(tied, term(step))]
    return totals, side


def no_ring(result):
    side = ()
    for _ in RING[1:]:
        side = yield side
    return result, side


class Stages:
    def __init__(self, generator):
        self.generator = generator
        self.result = None
        next(generator)

    def step(self, *side):
        try:
            return self.generator.send(side)
        except StopIteration as stop:
            self.result, side = stop.value
            return side


def ring_order():
    spots, core = device_ring()
    back = jnp.concatenate([spots[:0:-1], spots[:1]])
    ahead = jnp.concatenate([spots[1:], spots[:1]])
    return jnp.stack([back, ahead, jnp.broadcast_to(core, spots.shape)]).astype(jnp.int32)


def call_ordered(kernel, steps, in_specs, out_specs, out_shape, scratch, order, operands):
    return pl.pallas_call(
        kernel,
        grid_spec=pltpu.PrefetchScalarGridSpec(
            num_scalar_prefetch=1, grid=(steps,), in_specs=in_specs, out_specs=out_specs, scratch_shapes=scratch
        ),
        out_shape=out_shape,
        cost_estimate=SHORT,
        compiler_params=pltpu.CompilerParams(vmem_limit_bytes=24 * MIB),
    )(order, *operands)


def grad_spec(block):
    return pl.BlockSpec((len(RING), HEAD, SET), lambda j, order: (0, block(j) >> 1, block(j) & 1))


def packed_grad_kernel(order_ref, h_ref, o_ref, t_ref, w_ref, j_ref, j2_ref, a_ref, a2_ref, b_ref, b2_ref, k_ref, k2_ref, v_ref, v2_ref, right_ref, left_ref, rows_ref, grad_ref):
    step = pl.program_id(0)
    chips = len(RING)
    tokens, words = a_ref.shape[0], k_ref.shape[0]

    def pick(source_ref, way):
        width = source_ref.shape[1]
        for j in range(chips):
            start = pl.multiple_of((2 * order_ref[way, j] + order_ref[2, 0]) * HEAD, HEAD)
            rows_ref[j * HEAD : (j + 1) * HEAD, :width] = source_ref[pl.ds(start, HEAD)]

    pl.when(step == 0)(lambda: pick(h_ref, 0))
    pl.when(step == MEMBERS)(lambda: pick(o_ref, 1))
    pl.when(step == MEMBERS + 2)(lambda: pick(t_ref, 1))
    pl.when(step == MEMBERS + 4)(lambda: pick(w_ref, 1))

    @pl.when(step < MEMBERS)
    def _():
        for i, (joint, asked) in enumerate(((j_ref, a_ref), (j2_ref, a2_ref))):
            grad_ref[i * tokens : (i + 1) * tokens, : 3 * PAIR] = joint[0]
            grad_ref[i * tokens : (i + 1) * tokens, 3 * PAIR :] = asked[...]
        right_ref[...] = low(dot(rows_ref[...], grad_ref[...])).reshape(chips, HEAD, SET)

    @pl.when((step >= MEMBERS) & (step < MEMBERS + 4))
    def _():
        grad_ref[:tokens] = b_ref[...]
        grad_ref[tokens:] = b2_ref[...]
        left_ref[...] = low(dot(rows_ref[...], grad_ref[...])).reshape(chips, HEAD, SET)

    def memory(first, second):
        grad_ref[:words] = first[...]
        grad_ref[words : 2 * words] = second[...]
        made = dot(rows_ref[:, : 2 * words], grad_ref[: 2 * words])
        left_ref[...] = low(made).reshape(chips, HEAD, SET)

    pl.when((step >= MEMBERS + 4) & (step < MEMBERS + 6))(lambda: memory(k_ref, k2_ref))
    pl.when(step >= MEMBERS + 6)(lambda: memory(v_ref, v2_ref))


def packed_grads(order, hidden, o, text, words, joint_grad, asked_grad, branch_grad, keys_grad, values_grad):
    tokens = asked_grad[0].shape[0]
    chips = len(RING)

    def full(x):
        return pl.BlockSpec(x.shape, lambda j, order: (0, 0))

    def strips(x, first, last):
        return pl.BlockSpec((x.shape[0], SET), lambda j, order: (0, jnp.clip(j - first, 0, last)))

    joint = pl.BlockSpec((1, tokens, 3 * PAIR), lambda j, order: (jnp.minimum(j, MEMBERS - 1), 0, 0))
    asked = pl.BlockSpec((tokens, PAIR), lambda j, order: (0, jnp.minimum(j, MEMBERS - 1)))
    branch = pl.BlockSpec((tokens, SET), lambda j, order: (0, jnp.maximum(j - MEMBERS, 0) & 1))
    keys = strips(keys_grad[0], MEMBERS + 4, 1)
    values = strips(values_grad[0], MEMBERS + 6, 1)
    return call_ordered(
        packed_grad_kernel,
        2 * MEMBERS,
        [full(hidden), full(o), full(text), full(words), joint, joint, asked, asked, branch, branch]
        + [keys, keys, values, values],
        [
            grad_spec(lambda j: jnp.minimum(j, MEMBERS - 1)),
            grad_spec(lambda j: jnp.maximum(j - MEMBERS, 0)),
        ],
        [shaped((chips, 4 * HEAD, D))] * 2,
        [pltpu.VMEM((chips * HEAD, 2 * tokens), LOW), pltpu.VMEM((2 * tokens, SET), LOW)],
        order,
        (hidden, o, text, words) + joint_grad + asked_grad + branch_grad + keys_grad + values_grad,
    )


def turn_kernel(*refs):
    count = len(refs) // 3
    unit = (
        lax.broadcasted_iota(jnp.int32, (PAIR, PAIR), 0) == lax.broadcasted_iota(jnp.int32, (PAIR, PAIR), 1)
    ).astype(LOW)
    for i in range(count):
        own, other, out = refs[2 * i], refs[2 * i + 1], refs[2 * count + i]
        rows = own.shape[-2]
        for j, ref in enumerate((own, other)):
            out[:, j * rows : (j + 1) * rows] = low(dot_right_t(unit, ref[...].reshape(rows, PAIR)))


def turned(*pairs):
    def spec(x):
        if x.ndim == 3:
            return pl.BlockSpec((1, x.shape[1], PAIR), lambda j: (j, 0, 0))
        return pl.BlockSpec((x.shape[0], PAIR), lambda j: (0, j))

    rows = [pair[0].shape[-2] for pair in pairs]
    return call(
        turn_kernel,
        (D // PAIR,),
        [spec(x) for pair in pairs for x in pair],
        [pl.BlockSpec((PAIR, 2 * n), lambda j: (j, 0)) for n in rows],
        [shaped((D, 2 * n)) for n in rows],
        tuple(x for pair in pairs for x in pair),
    )


def feed_grad_kernel(order_ref, s_ref, u_ref, u2_ref, a_ref, a2_ref, f_ref, f2_ref, right_ref, left_ref, rows_ref):
    chips = len(RING)

    @pl.when(pl.program_id(0) == 0)
    def _():
        for j in range(chips):
            start = pl.multiple_of((2 * order_ref[0, j] + order_ref[2, 0]) * HEAD, HEAD)
            rows_ref[j * HEAD : (j + 1) * HEAD] = s_ref[pl.ds(start, HEAD)]

    grad = jnp.concatenate([u_ref[...], u2_ref[...]], 0)
    right_ref[...] = low(dot(rows_ref[...], grad)).reshape(chips, HEAD, STRIP)
    left_ref[0] = low(dot_left_t(a_ref[...], f_ref[...]) + dot_left_t(a2_ref[...], f2_ref[...]))


def feed_grads(order, second, upper_grad, active, feed_grad):
    tokens = upper_grad[0].shape[0]
    chips = len(RING)
    rows = FF // (2 * chips)
    strip = pl.BlockSpec((tokens, STRIP), lambda j, order: (0, j))
    hidden = pl.BlockSpec((tokens, rows), lambda j, order: (0, 2 * order[1, j] + order[2, 0]))
    full = pl.BlockSpec((tokens, D), lambda j, order: (0, 0))
    return call_ordered(
        feed_grad_kernel,
        chips,
        [pl.BlockSpec((D, 2 * tokens), lambda j, order: (0, 0)), strip, strip, hidden, hidden, full, full],
        [grad_spec(lambda j: j), pl.BlockSpec((1, rows, D), lambda j, order: (j, 0, 0))],
        [shaped((chips, 4 * HEAD, D)), shaped((chips, rows, D))],
        [pltpu.VMEM((chips * HEAD, 2 * tokens), LOW)],
        order,
        (second,) + upper_grad + active + feed_grad,
    )


def per_device(
    block_input,
    conditioning,
    text_embed,
    text_keep,
    cotangent,
    self_input,
    self_output,
    cross_query,
    cross_memory,
    cross_output,
    up_weight,
    down_weight,
    modulation,
    modulation_bias,
    position_bias,
):
    section = lax.axis_index("section")
    device = lax.axis_index("dp")
    count = lax.axis_size("dp")
    member = device & (MEMBERS - 1)
    clip = device >> 3
    clips = count // MEMBERS
    micro = block_input.shape[0]
    tokens = micro * ROWS
    shard = D // count
    words = MEMBERS * text_embed.shape[1]
    members = [list(range(c * MEMBERS, (c + 1) * MEMBERS)) for c in range(clips)]

    def chosen(first, second):
        return jnp.where(section == 1, second, first)

    def slice_at(x, start, size, axis):
        starts = [0] * x.ndim
        starts[axis] = start
        sizes = list(x.shape)
        sizes[axis] = size
        return lax.dynamic_slice(x, starts, sizes, allow_negative_indices=False)

    def trade(x):
        return lax.all_to_all(x, "dp", 0, 0, tiled=True, axis_index_groups=members)

    def collect(x):
        return trade(jnp.broadcast_to(x, (MEMBERS,) + x.shape))

    ringed = count == 2 * len(RING)

    def parts_of(x):
        x = x.reshape(-1, min(shard, ROWS_OF_PART), x.shape[1] // D, D)
        return jnp.swapaxes(x, 1, 2).reshape(-1, D)

    def gathered(pieces):
        full = [lax.all_gather(x, "dp", axis=0, tiled=True) for x in pieces]
        full = [jnp.swapaxes(x.reshape(PARTS, -1, x.shape[1] // D, D), 1, 2) for x in full]
        return jnp.concatenate([x.reshape(PARTS, -1, D) for x in full], 1)

    grouped = [x[0].reshape(shard, -1, MEMBERS, PAIR) for x in (self_input, cross_query)]
    grouped = jnp.swapaxes(low(jnp.concatenate(grouped, 1)), 1, 2).reshape(shard, 4 * D)
    ring = Stages(ring_gather(parts_of(grouped)) if ringed else no_ring(gathered([grouped])))

    cond_low = low(jax.nn.silu(high(conditioning)))
    cond_rows = slice_at(cond_low, device * shard, shard, 2)
    sums = jnp.einsum("bck,kn->cbn", cond_rows, low(modulation[0]), preferred_element_type=HIGH)
    keep = slice_at(text_keep, clip, 1, 1).astype(LOW)
    text = text_embed * keep[:, :, None]
    sums, text = ring.step(sums, text)

    bit = clips // 2
    while bit:
        upper = (clip & bit) > 0
        halves = (sums[:bit], sums[bit:])
        sums = jnp.where(upper, halves[1], halves[0]) + swap(
            jnp.where(upper, halves[0], halves[1]), bit * MEMBERS
        )
        bit //= 2
    sums = sums[0]
    (sums,) = ring.step(sums)

    text_all = collect(text)
    sums = sums + swap(sums, 1)
    (sums,) = ring.step(sums)

    sums = sums + swap(sums, 2)
    sums, text_all = ring.step(sums, text_all)

    sums = sums + swap(sums, 4)
    (sums,) = ring.step(sums)

    mods = (sums + modulation_bias[0]).reshape(micro, 6, 1, D)
    shift1, scale1, gate1, shift2, scale2, gate2 = [mods[:, i] for i in range(6)]
    hidden = low(layer_mod(high(block_input), shift1, scale1)).reshape(tokens, D)
    mods, hidden = ring.step(mods, hidden)
    shift1, scale1, gate1, shift2, scale2, gate2 = [mods[:, i] for i in range(6)]

    spread = jnp.arange(MEMBERS * CELLS)
    hot0 = place_hot(*places_of(spread // CELLS, spread % CELLS))
    own_table = slice_at(position_bias[0], 2 * member, 2, 0)
    bias0 = bias_of(own_table, hot0, hot0)
    pieces = [low(x[0]) for x in (self_output, cross_output, up_weight, cross_memory, down_weight)]
    hidden, bias0, *pieces = ring.step(hidden, bias0, *pieces)
    packed = ring.result

    def of_frames(x):
        return x.reshape(MEMBERS, -1, CELLS, x.shape[-1])

    def of_tokens(x):
        return x.reshape(MEMBERS, -1, x.shape[-1])

    def branch_and_norm(inputs, mixture, mixture_text):
        branch = merge(mixture, mixture_text, outer).reshape(micro, ROWS, D)
        middle = inputs + gate1 * branch
        second = low(layer_mod(middle, shift2, scale2)).reshape(tokens, D)
        return branch, middle, second

    def feed_forward(kept):
        upper, active, feed = feed_call(kept["second"], outer)
        feed = feed.reshape(micro, ROWS, D)
        kept.update(upper=upper, active=active, feed=feed)
        return low(kept["middle"] + gate2 * feed)

    if ringed:
        ring = Stages(ring_gather(jnp.concatenate([parts_of(x) for x in pieces], 0)))
    else:
        ring = Stages(no_ring(gathered(pieces)))
    joint, asked = project(hidden, packed)
    joint, asked = ring.step(joint, asked)
    joint = [joint[:, i * ROWS : (i + 1) * ROWS] for i in range(micro)]
    joint[0], *joint[1:] = ring.step(trade(joint[0]), *joint[1:])
    mixture, norm = [None] * micro, [None] * micro
    for i in range(micro):
        joint[i] = of_frames(joint[i])
        mixture[i], norm[i] = attend_frames(joint[i], bias0)
        mixture[i] = trade(of_tokens(mixture[i]))
        if i + 1 < micro:
            joint[i + 1], norm[i] = ring.step(trade(joint[i + 1]), norm[i])
    norm[-1], *mixture = ring.step(norm[-1], *mixture)
    mixture = jnp.concatenate(mixture, 1)
    within = jnp.arange(ROWS)
    mine, partner = places_of(member, within), places_of(member ^ 1, within)
    hot_q1 = place_hot(*mine)
    hot_k1 = jnp.concatenate([hot_q1, place_hot(*partner)])
    bias1 = bias_of(position_bias[0], hot_q1, hot_k1)
    bias1, mixture = ring.step(bias1, mixture)
    for _ in range(4 - micro):
        ring.step()
    outer = ring.result
    text_all = jnp.swapaxes(text_all, 0, 1).reshape(micro * words, D)
    memory = text_project(text_all, outer).reshape(micro, words, 2 * D)
    mixture_text, text_norm = attend_text(asked, memory)
    branch, middle, second = branch_and_norm(high(block_input), mixture, mixture_text)
    first = dict(
        x=high(block_input),
        hidden=hidden,
        joint=joint,
        asked=asked,
        norm=norm,
        mixture=mixture,
        mixture_text=mixture_text,
        text_norm=text_norm,
        branch=branch,
        middle=middle,
        second=second,
    )
    first_result = feed_forward(first)

    def back_feed(kept, grad_result):
        gate2_grad = jnp.sum(grad_result * kept["feed"], 1)
        feed_grad = low(gate2 * grad_result).reshape(tokens, D)
        upper_grad, second_grad = feed_back_call(feed_grad, kept["upper"], outer)
        kept.update(feed_grad=feed_grad, upper_grad=upper_grad, second_grad=second_grad, gate2_grad=gate2_grad)

    def back_norm2(kept, grad_result):
        second_grad = kept["second_grad"].reshape(micro, ROWS, D)
        middle_norm, shift2_grad, scale2_grad = jax.vjp(layer_mod, kept["middle"], shift2, scale2)[1](second_grad)
        middle_grad = grad_result + middle_norm
        gate1_grad = jnp.sum(middle_grad * kept["branch"], 1)
        branch_grad = low(gate1 * middle_grad).reshape(tokens, D)
        kept.update(
            middle_grad=middle_grad,
            branch_grad=branch_grad,
            late=[gate1_grad, shift2_grad[:, 0], scale2_grad[:, 0], kept["gate2_grad"]],
        )
        return merge_back(branch_grad, outer)

    def back_norm1(kept):
        hidden_grad = project_back(kept["joint_grad"], kept["asked_grad"], packed)
        inputs_norm, shift1_grad, scale1_grad = jax.vjp(layer_mod, kept["x"], shift1, scale1)[1](
            hidden_grad.reshape(micro, ROWS, D)
        )
        kept["mods"] = jnp.concatenate([shift1_grad[:, 0], scale1_grad[:, 0]] + kept["late"], 1)
        return low(kept["middle_grad"] + inputs_norm)

    received = lax.ppermute(first_result, "section", [(0, 1)])
    received, bias1 = together(received, bias1)
    inputs = high(received)
    hidden = low(layer_mod(inputs, shift1, scale1)).reshape(tokens, D)
    joint, asked = project(hidden, packed)
    other = swap(joint, 1, (1,))
    mixture_text, text_norm = attend_text(asked, memory)
    mixture, norm = attend_window(joint, other, bias1)
    branch, middle, second = branch_and_norm(inputs, mixture, mixture_text)
    latter = dict(
        x=inputs, hidden=hidden, mixture=mixture, mixture_text=mixture_text, branch=branch, middle=middle, second=second
    )
    second_result = feed_forward(latter)
    grad_result = high(cotangent)
    back_feed(latter, grad_result)
    mixture_grad, text_grad = back_norm2(latter, grad_result)
    own, sent, dbias1 = attend_window_back(joint, other, bias1, norm, mixture_grad)
    arrived = swap(sent, 1, (1,))
    latter["asked_grad"], dkt1, dvt1 = attend_text_back(asked, memory, text_norm, text_grad)
    keys = low(high(own[:, :, PAIR:]) + high(arrived))
    latter["joint_grad"] = jnp.concatenate([own[:, :, :PAIR], keys], 2)
    second_grad = back_norm1(latter)
    returned = lax.ppermute(second_grad, "section", [(1, 0)])
    names = ("second", "active", "hidden", "mixture", "mixture_text")
    second_grad, dkt1, dvt1, *kept = together(second_grad, dkt1, dvt1, *[latter[name] for name in names])
    latter.update(zip(names, kept))

    def both(name):
        return chosen(first[name], latter[name])

    ready = [both(name) for name in names]
    apart = count != 2 * len(RING)
    order = None if apart else ring_order()

    def paired(x):
        return (x, x if apart else swap(x, 1))

    def summed(x):
        return high(lax.psum_scatter(x, "dp", scatter_dimension=0, tiled=True))

    second_all, active_all, hidden_all, mixture_all, text_all2 = ready
    columns = [paired(x) for x in (hidden_all, mixture_all, text_all2)] + [(text_all, text_all), paired(second_all)]
    columns = turned(*columns)
    returned, *flat = together(returned, *columns, *paired(active_all))
    columns, active2 = flat[:5], tuple(flat[5:])

    grad_result = high(returned)
    back_feed(first, grad_result)
    upper2, feed2 = paired(both("upper_grad")), paired(both("feed_grad"))
    mixture_grad, text_grad = back_norm2(first, grad_result)
    mixture_grad = of_frames(trade(mixture_grad))
    first["asked_grad"], dkt, dvt = attend_text_back(first["asked"], memory, first["text_norm"], text_grad)
    mixture_grad, dkt, dvt = together(mixture_grad, dkt, dvt)

    def frames_back(i):
        frames = mixture_grad[:, i * FRAMES : (i + 1) * FRAMES]
        grad, dbias = attend_frames_back(first["joint"][i], bias0, first["norm"][i], frames)
        return of_tokens(grad), dbias

    joint_grad, dbias0 = frames_back(0)
    feeds = () if apart else feed_grads(order, columns[4], upper2, active2, feed2)
    traded, *feeds = together(trade(joint_grad), *feeds)
    joint_grad = [traded]
    ring = Stages(no_ring(None) if apart else ring_sums(feeds[:1], feeds[1:]))
    asked2, branch2 = paired(both("asked_grad")), paired(both("branch_grad"))
    keys2, values2 = [paired(chosen(x, y).reshape(micro * words, D)) for x, y in ((dkt, dkt1), (dvt, dvt1))]
    for i in range(1, micro):
        grad, dbias = frames_back(i)
        dbias0 = dbias0 + dbias
        grad, dbias0 = ring.step(trade(grad), dbias0)
        joint_grad.append(grad)
    flat = ring.step(*asked2, *branch2, *keys2, *values2)
    asked2, branch2, keys2, values2 = [tuple(flat[2 * i : 2 * i + 2]) for i in range(4)]
    first["joint_grad"] = jnp.concatenate(joint_grad, 1)
    joint2 = paired(both("joint_grad"))
    if apart:
        joint_all = [jnp.swapaxes(joint2[0], 0, 1), asked2[0].reshape(tokens, MEMBERS, PAIR)]
        joint_all = jnp.concatenate(joint_all, 2).reshape(tokens, 4 * D)
        rights = (joint_all, branch2[0], branch2[0], keys2[0], values2[0], upper2[0], feed2[0])
        lefts = [x[:, :tokens] for x in columns[:3]] + [text_all.T] * 2 + [columns[4][:, :tokens], active2[0].T]
        grads = [summed(low(dot(x, y))) for x, y in zip(lefts, rights)]
    else:
        grads = packed_grads(order, *columns[:4], joint2, asked2, branch2, keys2, values2)
    first["joint_grad"], dbias0, dbias1, *grads = ring.step(first["joint_grad"], dbias0, dbias1, *grads)
    for _ in range(6 - micro):
        ring.step()
    feed_part = ring.result
    ring = Stages(no_ring(grads) if apart else ring_sums(grads[:1], grads[1:]))
    first_grad = back_norm1(first)
    (first_grad,) = ring.step(first_grad)

    table0 = lax.dynamic_update_slice(
        jnp.zeros((HEADS, REL), HIGH), bias_grad(dbias0, hot0, hot0), (2 * member, 0), allow_negative_indices=False
    )
    table = chosen(table0, bias_grad(dbias1, hot_q1, hot_k1))
    small = jnp.concatenate([both("mods").reshape(micro * 6 * D), table.reshape(HEADS * REL)])
    small = jnp.pad(small, (0, -small.shape[0] % 1024)).reshape(1, -1, 128)
    (small,) = ring.step(small)
    small = small + swap(small, 1)
    (small,) = ring.step(small)
    small = small + swap(small, 2)
    (small,) = ring.step(small)
    small = small + swap(small, 4)
    (small,) = ring.step(small)
    bit = 1
    while bit < clips:
        far = swap(small, bit * MEMBERS)
        upper = (clip & bit) > 0
        small = jnp.concatenate([jnp.where(upper, far, small), jnp.where(upper, small, far)])
        bit *= 2
    (small,) = ring.step(small)
    small = small.reshape(clips, -1)
    mods_all = small[:, : micro * 6 * D].reshape(clips, micro, 6 * D)
    table_sum = jnp.sum(small[:, micro * 6 * D : micro * 6 * D + HEADS * REL], 0).reshape(HEADS, REL)
    modul_shard = jnp.einsum("bck,cbn->kn", high(cond_rows), mods_all, precision=lax.Precision.HIGHEST)
    bias_sum = jnp.sum(mods_all, (0, 1))
    modul_shard, bias_sum, table_sum = ring.step(modul_shard, bias_sum, table_sum)

    if apart:
        grouped, out_shard, cross_shard, keys, values, up_shard, down_shard = ring.result
        memory_shard = jnp.concatenate([keys, values], 1)
    else:
        (grouped, outputs), (up_shard, down_shard) = ring.result, feed_part
        grouped, up_shard = [
            jnp.swapaxes(x.reshape(4, shard, D), 0, 1).reshape(shard, 4 * D) for x in (grouped, up_shard)
        ]
        out_shard, cross_shard = outputs[:shard], outputs[shard : 2 * shard]
        memory_shard = jnp.concatenate([outputs[2 * shard : 3 * shard], outputs[3 * shard :]], 1)
    grouped = jnp.swapaxes(grouped.reshape(shard, MEMBERS, 4, PAIR), 1, 2).reshape(shard, 4 * D)
    in_shard, query_shard = grouped[:, : 3 * D], grouped[:, 3 * D :]
    outputs = chosen(first_result, second_result)
    input_grads = chosen(first_grad, second_grad)
    return tuple(
        x[None]
        for x in (
            outputs,
            input_grads,
            in_shard,
            out_shard,
            query_shard,
            memory_shard,
            cross_shard,
            up_shard,
            down_shard,
            modul_shard,
            bias_sum,
            table_sum,
        )
    )


def solution(mesh):
    weights = P("section", "dp", None)
    return jax.shard_map(
        per_device,
        mesh=mesh,
        in_specs=(
            P(None, "dp", None),
            P(),
            P(None, "dp", None),
            P(),
            P(None, "dp", None),
        )
        + (weights,) * 8
        + (P("section", None), P("section", None, None)),
        out_specs=(P("section", None, "dp", None),) * 2
        + (weights,) * 8
        + (P("section", None), P("section", None, None)),
        check_vma=False,
    )
```

```python
import functools

import jax
import jax.numpy as jnp
import numpy as np
from jax import lax
from jax.experimental import pallas as pl
from jax.experimental.pallas import tpu as pltpu
from jax.sharding import PartitionSpec as P

D = 1024
HEADS = 16
HEAD = 64
FF = 4096
FRAMES = 5
BH = 8
BW = 4
CELLS = BH * BW
ROWS = 160
REL = 71
MEMBERS = 8
PAIR = 2 * HEAD
EPSILON = 1e-06
LOW = jnp.bfloat16
HIGH = jnp.float32
MIB = 1024 * 1024
SHORT = pl.CostEstimate(flops=1, bytes_accessed=1, transcendentals=0)


def dot(left, right):
    return lax.dot_general(left, right, (((1,), (0,)), ((), ())), preferred_element_type=HIGH)


def dot_right_t(left, right):
    return lax.dot_general(left, right, (((1,), (1,)), ((), ())), preferred_element_type=HIGH)


def dot_left_t(left, right):
    return lax.dot_general(left, right, (((0,), (0,)), ((), ())), preferred_element_type=HIGH)


def low(v):
    return v.astype(LOW)


def high(v):
    return v.astype(HIGH)


def layer_mod(inputs, offset, factor):
    average = jnp.mean(inputs, axis=-1, keepdims=True)
    centred = inputs - average
    spread = jnp.mean(centred * centred, axis=-1, keepdims=True)
    return centred * lax.rsqrt(spread + EPSILON) * (1.0 + factor) + offset


def swap(x, bits, sections=(0, 1)):
    count = lax.axis_size("dp")
    route = [(s * count + i, s * count + (i ^ bits)) for s in sections for i in range(count)]
    return lax.ppermute(x, ("section", "dp"), route)


def head_masks():
    lane = lax.broadcasted_iota(jnp.int32, (1, PAIR), 1)
    first = (lane < HEAD).astype(LOW)
    return first, 1 - first


def by_head(first, second):
    lane = lax.broadcasted_iota(jnp.int32, (1, PAIR), 1)
    return low(jnp.where(lane < HEAD, first, second))


def pairs_forward(pairs):
    masks = [mask * LOW(HEAD ** (-0.5)) for mask in head_masks()]
    heads = [(q * mask, k, v, bias) for q, k, v, biases in pairs for mask, bias in zip(masks, biases)]
    scores = [dot_right_t(q, k) + bias for q, k, _, bias in heads]
    highest = [jnp.max(x, axis=-1, keepdims=True) for x in scores]
    exponents = [jnp.exp(x - y) for x, y in zip(scores, highest)]
    totals = [jnp.sum(x, axis=-1, keepdims=True) for x in exponents]
    mixed = [dot(low(x), head[2]) * (1.0 / total) for x, head, total in zip(exponents, heads, totals)]
    norms = [x + jnp.log(y) for x, y in zip(highest, totals)]
    return [(by_head(*mixed[i : i + 2]), norms[i : i + 2]) for i in range(0, len(heads), 2)]


def pairs_backward(pairs):
    masks = head_masks()
    heads = [
        (q * mask, k, v, do * mask, bias, norm)
        for q, k, v, do, biases, norms in pairs
        for mask, bias, norm in zip(masks, biases, norms)
    ]
    scale = HEAD ** (-0.5)
    soft = [jnp.exp(dot_right_t(q * LOW(scale), k) + bias - norm) for q, k, _, _, bias, norm in heads]
    grads = [dot_right_t(do, v) for _, _, v, do, _, _ in heads]
    means = [jnp.sum(x * y, axis=-1, keepdims=True) for x, y in zip(soft, grads)]
    grads = [x * (y - z) for x, y, z in zip(soft, grads, means)]
    raw = [low(x * scale) for x in grads]
    dq = [dot(x, head[1]) for x, head in zip(raw, heads)]
    dk = [dot_left_t(head[0], x) for x, head in zip(raw, heads)]
    dv = [dot_left_t(head[3], low(x)) for x, head in zip(soft, heads)]
    return [
        (by_head(*dq[i : i + 2]), low((dk[i] + dk[i + 1]).T), low((dv[i] + dv[i + 1]).T), grads[i : i + 2])
        for i in range(0, len(heads), 2)
    ]


def add_over_steps(ref, index, value, axis):
    @pl.when(pl.program_id(axis) == 0)
    def _():
        ref[index] = value

    @pl.when(pl.program_id(axis) > 0)
    def _():
        ref[index] += value


def part_of(block, part):
    return block[:, part * PAIR : (part + 1) * PAIR]


def frames_pairs(joint_ref, bias_ref):
    for w in range(joint_ref.shape[1]):
        x = joint_ref[:, w].reshape(MEMBERS * CELLS, 3 * PAIR)
        yield part_of(x, 0), part_of(x, 1), part_of(x, 2), (bias_ref[0], bias_ref[1])


def frames_forward(joint_ref, bias_ref, o_ref, norm_ref):
    for w, (o, norms) in enumerate(pairs_forward(list(frames_pairs(joint_ref, bias_ref)))):
        o_ref[:, w] = o.reshape(MEMBERS, CELLS, PAIR)
        norm_ref[w] = jnp.concatenate(norms, 1)


def frames_backward(joint_ref, bias_ref, norm_ref, do_ref, grad_ref, dbias_ref):
    pairs = []
    for w, (q, k, v, biases) in enumerate(frames_pairs(joint_ref, bias_ref)):
        do = do_ref[:, w].reshape(MEMBERS * CELLS, PAIR)
        pairs.append((q, k, v, do, biases, (norm_ref[w, :, 0:1], norm_ref[w, :, 1:2])))
    sums = [0.0, 0.0]
    for w, (dq, dk, dv, dbias) in enumerate(pairs_backward(pairs)):
        for part, value in enumerate((dq, dk, dv)):
            grad_ref[:, w, :, part * PAIR : (part + 1) * PAIR] = value.reshape(MEMBERS, CELLS, PAIR)
        sums = [s + d for s, d in zip(sums, dbias)]
    for a in range(2):
        add_over_steps(dbias_ref, a, sums[a], 0)


def window_pairs(own_ref, other_ref, bias_ref):
    for h in range(own_ref.shape[0]):
        own, other = own_ref[h], other_ref[h]
        k, v = [jnp.concatenate([part_of(own, p), part_of(other, p)], 0) for p in (1, 2)]
        yield part_of(own, 0), k, v, (bias_ref[2 * h], bias_ref[2 * h + 1])


def window_forward(own_ref, other_ref, bias_ref, o_ref, norm_ref):
    made = pairs_forward(list(window_pairs(own_ref, other_ref, bias_ref)))
    for h, (o, _) in enumerate(made):
        o_ref[h] = o
    norm_ref[0, 0] = jnp.concatenate([norm for _, norms in made for norm in norms], 1)


def window_backward(own_ref, other_ref, bias_ref, norm_ref, do_ref, own_grad_ref, other_grad_ref, dbias_ref):
    norms = norm_ref[0, 0]
    pairs = []
    for h, (q, k, v, biases) in enumerate(window_pairs(own_ref, other_ref, bias_ref)):
        pairs.append((q, k, v, do_ref[h], biases, (norms[:, 2 * h : 2 * h + 1], norms[:, 2 * h + 1 : 2 * h + 2])))
    for h, (dq, dk, dv, dbias) in enumerate(pairs_backward(pairs)):
        own_grad_ref[h] = jnp.concatenate([dq, dk[:ROWS], dv[:ROWS]], 1)
        other_grad_ref[h] = jnp.concatenate([dk[ROWS:], dv[ROWS:]], 1)
        for a in range(2):
            add_over_steps(dbias_ref, 2 * h + a, dbias[a], 1)


def text_pairs(q_ref, k_ref, v_ref):
    for h in range(q_ref.shape[1] // PAIR):
        yield part_of(q_ref[...], h), part_of(k_ref[0], h), part_of(v_ref[0], h), (0.0, 0.0)


def text_forward(q_ref, k_ref, v_ref, o_ref, norm_ref):
    made = pairs_forward(list(text_pairs(q_ref, k_ref, v_ref)))
    o_ref[...] = jnp.concatenate([o for o, _ in made], 1)
    norm_ref[0, 0] = jnp.concatenate([norm for _, norms in made for norm in norms], 1)


def text_backward(q_ref, k_ref, v_ref, norm_ref, do_ref, dq_ref, dk_ref, dv_ref):
    norms = norm_ref[0, 0]
    pairs = []
    for h, (q, k, v, biases) in enumerate(text_pairs(q_ref, k_ref, v_ref)):
        heads = (norms[:, 2 * h : 2 * h + 1], norms[:, 2 * h + 1 : 2 * h + 2])
        pairs.append((q, k, v, part_of(do_ref[...], h), biases, heads))
    made = pairs_backward(pairs)
    dq_ref[...], dk_ref[0], dv_ref[0] = [jnp.concatenate([x[i] for x in made], 1) for i in range(3)]


def call(kernel, grid, in_specs, out_specs, out_shape, operands, limit=20):
    return pl.pallas_call(
        kernel,
        grid=grid,
        in_specs=in_specs,
        out_specs=out_specs,
        out_shape=out_shape,
        cost_estimate=SHORT,
        compiler_params=pltpu.CompilerParams(vmem_limit_bytes=limit * MIB),
    )(*operands)


def shaped(shape, dtype=LOW):
    return jax.ShapeDtypeStruct(shape, dtype)


GROUP = 4
GROUPS = HEADS // 2 // GROUP


def frames_specs(joint):
    steps = joint.shape[1] // FRAMES
    wide = pl.BlockSpec((MEMBERS, FRAMES, CELLS, 3 * PAIR), lambda i: (0, i, 0, 0))
    narrow = pl.BlockSpec((MEMBERS, FRAMES, CELLS, PAIR), lambda i: (0, i, 0, 0))
    size = MEMBERS * CELLS
    bias = pl.BlockSpec((2, size, size), lambda i: (0, 0, 0))
    norm = pl.BlockSpec((FRAMES, size, 2), lambda i: (i, 0, 0))
    return steps, wide, narrow, bias, norm


def attend_frames(joint, bias):
    steps, wide, narrow, bias_spec, norm = frames_specs(joint)
    size = MEMBERS * CELLS
    return call(
        frames_forward,
        (steps,),
        [wide, bias_spec],
        [narrow, norm],
        [shaped(joint.shape[:3] + (PAIR,)), shaped((steps * FRAMES, size, 2), HIGH)],
        (joint, bias),
    )


def attend_frames_back(joint, bias, norms, do):
    steps, wide, narrow, bias_spec, norm = frames_specs(joint)
    size = MEMBERS * CELLS
    return call(
        frames_backward,
        (steps,),
        [wide, bias_spec, norm, narrow],
        [wide, bias_spec],
        [shaped(joint.shape), shaped((2, size, size), HIGH)],
        (joint, bias, norms, do),
    )


def window_specs(width):
    return pl.BlockSpec((GROUP, ROWS, width), lambda g, w: (g, w, 0))


BIAS_SPEC = pl.BlockSpec((2 * GROUP, ROWS, 2 * ROWS), lambda g, w: (g, 0, 0))
NORM_SPEC = pl.BlockSpec((1, 1, ROWS, 2 * GROUP), lambda g, w: (g, w, 0, 0))


def attend_window(own, other, bias):
    micro = own.shape[1] // ROWS
    return call(
        window_forward,
        (GROUPS, micro),
        [window_specs(3 * PAIR), window_specs(3 * PAIR), BIAS_SPEC],
        [window_specs(PAIR), NORM_SPEC],
        [shaped(own.shape[:2] + (PAIR,)), shaped((GROUPS, micro, ROWS, 2 * GROUP), HIGH)],
        (own, other, bias),
    )


def attend_window_back(own, other, bias, norms, do):
    micro = own.shape[1] // ROWS
    return call(
        window_backward,
        (GROUPS, micro),
        [window_specs(3 * PAIR), window_specs(3 * PAIR), BIAS_SPEC, NORM_SPEC, window_specs(PAIR)],
        [window_specs(3 * PAIR), window_specs(2 * PAIR), BIAS_SPEC],
        [shaped(own.shape), shaped(own.shape[:2] + (2 * PAIR,)), shaped(bias.shape, HIGH)],
        (own, other, bias, norms, do),
    )


def text_specs(keys):
    rows = pl.BlockSpec((ROWS, GROUP * PAIR), lambda g, w: (w, g))
    k = pl.BlockSpec((1, keys, GROUP * PAIR), lambda g, w: (w, 0, g))
    v = pl.BlockSpec((1, keys, GROUP * PAIR), lambda g, w: (w, 0, GROUPS + g))
    return rows, k, v


def attend_text(asked, memory):
    micro, keys = memory.shape[:2]
    rows, k, v = text_specs(keys)
    return call(
        text_forward,
        (GROUPS, micro),
        [rows, k, v],
        [rows, NORM_SPEC],
        [shaped(asked.shape), shaped((GROUPS, micro, ROWS, 2 * GROUP), HIGH)],
        (asked, memory, memory),
    )


def attend_text_back(asked, memory, norms, do):
    micro, keys = memory.shape[:2]
    rows, k, v = text_specs(keys)
    return call(
        text_backward,
        (GROUPS, micro),
        [rows, k, v, NORM_SPEC, rows],
        [rows, k, k],
        [shaped(asked.shape), shaped((micro, keys, D)), shaped((micro, keys, D))],
        (asked, memory, memory, norms, do),
    )


PARTS = 16
ROWS_OF_PART = D // PARTS
SET = 4 * PAIR
STRIP = D
LARGE = 40


def block_spec(first):
    return pl.BlockSpec((PARTS, ROWS_OF_PART, SET), lambda j: (0, first + (j >> 1), j & 1))


def joined(ref):
    return ref[...].reshape(-1, ref.shape[-1])


def wide_spec(first):
    return pl.BlockSpec((PARTS, ROWS_OF_PART, D), lambda j: (0, first + j, 0))


def rows_spec(shape):
    return pl.BlockSpec(shape, lambda j: (0,) * len(shape))


SETS = D // SET


def project_kernel(hidden_ref, w_ref, joint_ref, asked_ref):
    made = low(dot(hidden_ref[...], joined(w_ref)))
    for i in range(SETS):
        joint_ref[i] = made[:, i * SET : i * SET + 3 * PAIR]
        asked_ref[:, i * PAIR : (i + 1) * PAIR] = made[:, i * SET + 3 * PAIR : (i + 1) * SET]


def project_specs(tokens):
    joint = pl.BlockSpec((SETS, tokens, 3 * PAIR), lambda m: (m, 0, 0))
    asked = pl.BlockSpec((tokens, SETS * PAIR), lambda m: (0, m))
    return joint, asked


def project(hidden, packed):
    tokens = hidden.shape[0]
    return call(
        project_kernel,
        (MEMBERS // SETS,),
        [rows_spec((tokens, D)), wide_spec(0)],
        list(project_specs(tokens)),
        [shaped((MEMBERS, tokens, 3 * PAIR)), shaped((tokens, D))],
        (hidden, packed),
    )


def joint_columns(joint_ref, asked_ref):
    pieces = [x for i in range(SETS) for x in (joint_ref[i], part_of(asked_ref[...], i))]
    return jnp.concatenate(pieces, 1)


def project_back_kernel(joint_ref, asked_ref, w_ref, out_ref):
    grad = joint_columns(joint_ref, asked_ref)
    add_over_steps(out_ref, slice(None), dot_right_t(grad, joined(w_ref)), 0)


def project_back(joint_grad, asked_grad, packed):
    tokens = asked_grad.shape[0]
    return call(
        project_back_kernel,
        (MEMBERS // SETS,),
        [*project_specs(tokens), wide_spec(0)],
        rows_spec((tokens, D)),
        shaped((tokens, D), HIGH),
        (joint_grad, asked_grad, packed),
    )


def text_project_kernel(text_ref, w_ref, out_ref):
    out_ref[...] = low(dot(text_ref[...], joined(w_ref)))


def text_project(text, packed):
    return call(
        text_project_kernel,
        (2 * D // SET,),
        [rows_spec(text.shape), block_spec(6)],
        pl.BlockSpec((text.shape[0], SET), lambda j: (0, j)),
        shaped((text.shape[0], 2 * D)),
        (text, packed),
        LARGE,
    )


def merge_kernel(o_ref, text_ref, w_self_ref, w_cross_ref, out_ref):
    o = jnp.concatenate([o_ref[m] for m in range(MEMBERS)], 1)
    out_ref[...] = dot(o, joined(w_self_ref)) + dot(text_ref[...], joined(w_cross_ref))


def merge(o, text, packed):
    tokens = text.shape[0]
    return call(
        merge_kernel,
        (D // SET,),
        [rows_spec((MEMBERS, tokens, PAIR)), rows_spec((tokens, D)), block_spec(0), block_spec(1)],
        pl.BlockSpec((tokens, SET), lambda j: (0, j)),
        shaped((tokens, D), HIGH),
        (o, text, packed, packed),
        LARGE,
    )


def merge_back_kernel(grad_ref, w_self_ref, w_cross_ref, o_ref, text_ref):
    made = low(dot_right_t(grad_ref[...], joined(w_self_ref)))
    for m in range(o_ref.shape[0]):
        o_ref[m] = part_of(made, m)
    text_ref[...] = low(dot_right_t(grad_ref[...], joined(w_cross_ref)))


def merge_back(grad, packed):
    tokens = grad.shape[0]
    height = 2 * PAIR
    parts = height // ROWS_OF_PART
    return call(
        merge_back_kernel,
        (D // height,),
        [
            rows_spec((tokens, D)),
            pl.BlockSpec((parts, ROWS_OF_PART, D), lambda j: (j, 0, 0)),
            pl.BlockSpec((parts, ROWS_OF_PART, D), lambda j: (j, 1, 0)),
        ],
        [pl.BlockSpec((2, tokens, PAIR), lambda j: (j, 0, 0)), pl.BlockSpec((tokens, height), lambda j: (0, j))],
        [shaped((MEMBERS, tokens, PAIR)), shaped((tokens, D))],
        (grad, packed, packed),
        LARGE,
    )


def slices(count):
    width = STRIP // count
    return [slice(i * width, (i + 1) * width) for i in range(count)]


def feed_kernel(s_ref, up_ref, down_ref, upper_ref, active_ref, feed_ref):
    up, down = joined(up_ref), joined(down_ref)
    uppers = [dot(s_ref[...], up[:, at]) for at in slices(4)]
    actives = [low(jax.nn.gelu(x)) for x in uppers]
    for at, upper, active in zip(slices(4), uppers, actives):
        upper_ref[:, at] = low(upper)
        active_ref[:, at] = active
    add_over_steps(feed_ref, slice(None), sum(dot(x, down[at]) for at, x in zip(slices(4), actives)), 0)


def feed_specs(tokens):
    strip = pl.BlockSpec((tokens, STRIP), lambda j: (0, j))
    down = pl.BlockSpec((STRIP // (FF // PARTS), FF // PARTS, D), lambda j: (j, 2, 0))
    return rows_spec((tokens, D)), strip, wide_spec(2), down


def feed_call(second, packed):
    tokens = second.shape[0]
    full, strip, up, down = feed_specs(tokens)
    return call(
        feed_kernel,
        (FF // STRIP,),
        [full, up, down],
        [strip, strip, full],
        [shaped((tokens, FF)), shaped((tokens, FF)), shaped((tokens, D), HIGH)],
        (second, packed, packed),
        LARGE,
    )


def feed_back_kernel(f_ref, upper_ref, up_ref, down_ref, upper_grad_ref, second_grad_ref):
    up, down = joined(up_ref), joined(down_ref)
    grads = [dot_right_t(f_ref[...], down[at]) for at in slices(4)]
    grads = [low(jax.vjp(jax.nn.gelu, high(upper_ref[:, at]))[1](x)[0]) for at, x in zip(slices(4), grads)]
    for at, x in zip(slices(4), grads):
        upper_grad_ref[:, at] = x
    add_over_steps(second_grad_ref, slice(None), sum(dot_right_t(x, up[:, at]) for at, x in zip(slices(4), grads)), 0)


def feed_back_call(feed_grad, upper, packed):
    tokens = feed_grad.shape[0]
    full, strip, up, down = feed_specs(tokens)
    return call(
        feed_back_kernel,
        (FF // STRIP,),
        [full, strip, up, down],
        [strip, full],
        [shaped((tokens, FF)), shaped((tokens, D), HIGH)],
        (feed_grad, upper, packed, packed),
        LARGE,
    )


def pack_columns(x):
    rows = x.shape[0]
    return jnp.swapaxes(x.reshape(rows, -1, D), 0, 1).reshape(-1, D)


def unpack_columns(x, blocks):
    return jnp.swapaxes(x.reshape(blocks, -1, D), 0, 1).reshape(-1, blocks * D)


SPANS = ((FRAMES, FRAMES - 1), (2 * BH, 2 * FRAMES - 1 + 2 * BH - 1), (4 * BW, 2 * FRAMES - 1 + 4 * BH - 1 + 4 * BW - 1))
SPAN = sum(size for size, _ in SPANS)


def table_picks():
    picks = np.zeros((SPAN, SPAN, REL), np.float32)
    start = 0
    for size, middle in SPANS:
        for i in range(size):
            for j in range(size):
                picks[start + i, start + j, middle + i - j] = 1
        start += size
    return picks


def place_hot(frame, row, column):
    marks = []
    for (size, _), place in zip(SPANS, (frame, row, column)):
        marks.append(place[:, None] == jnp.arange(size)[None, :])
    return jnp.concatenate(marks, 1).astype(HIGH)


def places_of(member, within):
    cell = within & (CELLS - 1)
    return (
        within // CELLS + 0 * member,
        (member >> 2) * BH + cell // BW,
        (member & 3) * BW + (cell & (BW - 1)),
    )


def bias_of(table, hot_q, hot_k):
    exact = lax.Precision.HIGHEST
    blocks = jnp.einsum("hn,abn->hab", table, table_picks(), precision=exact)
    left = jnp.einsum("ia,hab->hib", hot_q, blocks, precision=exact)
    return jnp.einsum("hib,jb->hij", left, hot_k, precision=exact)


def bias_grad(grad, hot_q, hot_k):
    exact = lax.Precision.HIGHEST
    right = jnp.einsum("hij,jb->hib", grad, hot_k, precision=exact)
    blocks = jnp.einsum("ia,hib->hab", hot_q, right, precision=exact)
    return jnp.einsum("hab,abn->hn", blocks, table_picks(), precision=exact)


RING = [0, 2, 4, 6, 7, 5, 3, 1]
WAYS = (1, -1)


def together(*values):
    return lax.optimization_barrier(values)


def device_ring():
    device = lax.axis_index("dp")
    chip = device >> 1
    half = len(RING) // 2
    place = jnp.where((chip & 1) == 1, 2 * half - 1 - (chip >> 1), chip >> 1)
    spots = (place + jnp.arange(2 * half)) & (2 * half - 1)
    return jnp.where(spots < half, 2 * spots, 4 * half - 1 - 2 * spots), device & 1


def hop(x, way):
    count = lax.axis_size("dp")
    chips = len(RING)
    route = []
    for s in range(2):
        for i in range(chips):
            for c in range(2):
                source = s * count + RING[i] * 2 + c
                route.append((source, s * count + RING[(i + way) % chips] * 2 + c))
    return lax.ppermute(x, ("section", "dp"), route)


def ring_gather(own):
    chips = len(RING)
    half = own.shape[0] // 2
    chunks = [own[:half], own[half:]]
    held = []
    side = ()
    for step in range(chips):
        last = step + 1 == chips
        if not last:
            following = [hop(chunk, way) for chunk, way in zip(chunks, WAYS)]
        held.append([list(chunks), [swap(chunk, 1) for chunk in chunks]])
        if not last:
            side = yield side
            before = [x for pair in held[:-1] for x in pair[1]]
            tied = together(*following, *before, *side)
            chunks = list(tied[:2])
            for i, pair in enumerate(held[:-1]):
                pair[1] = list(tied[2 + 2 * i : 4 + 2 * i])
            side = tied[2 + len(before) :]
        if step == EARLY:
            made = assembled(held, 0, None)
        if step == EARLY + 1:
            made, *chunks = together(made, *chunks)
    return assembled(held, EARLY, made), side


EARLY = 4


def assembled(held, start, made):
    held = held[start:EARLY] if made is None else held[start:]
    chips = len(RING)
    spots, core = device_ring()
    order = jnp.concatenate([spots, jnp.broadcast_to(core, (1,))]).astype(jnp.int32)
    flat = [x for own, other in held for x in own + other]
    half = flat[0].shape[0]
    shape = (chips, 2, 2 * half, D)

    def kernel(order_ref, *refs):
        sources, (sink, scratch, arrive, leave) = refs[: len(flat)], refs[-4:]
        arriving, leaving = [], []
        for i, ref in enumerate(sources):
            step, which, way = start + i // 4, i // 2 % 2, i % 2
            spot = order_ref[-WAYS[way] * step % chips]
            place = order_ref[chips] if which == 0 else 1 - order_ref[chips]
            where = (spot, place, pl.ds(way * half, half))
            arriving.append(pltpu.make_async_copy(ref, scratch.at[i], arrive.at[i]))
            leaving.append(pltpu.make_async_copy(scratch.at[i], sink.at[where], leave.at[i]))
        for copy in arriving:
            copy.start()
        for copy, onward in zip(arriving, leaving):
            copy.wait()
            onward.start()
        for copy in leaving:
            copy.wait()

    operands = flat if made is None else flat + [made]
    anywhere = pl.BlockSpec(memory_space=pl.ANY)
    made = pl.pallas_call(
        kernel,
        grid_spec=pltpu.PrefetchScalarGridSpec(
            num_scalar_prefetch=1,
            grid=(),
            in_specs=[anywhere] * len(operands),
            out_specs=anywhere,
            scratch_shapes=[pltpu.VMEM((len(flat),) + flat[0].shape, LOW)]
            + [pltpu.SemaphoreType.DMA((len(flat),))] * 2,
        ),
        out_shape=shaped(shape),
        input_output_aliases={} if made is None else {1 + len(flat): 0},
        cost_estimate=SHORT,
        compiler_params=pltpu.CompilerParams(vmem_limit_bytes=58 * MIB),
    )(order, *operands)
    return made if start == 0 else made.reshape(PARTS, 2 * half, D)


def ring_sums(right, left):
    def term(step):
        return [jnp.concatenate([high(x[step]) for x in arrays], 0) for arrays in (right, left)]

    totals = term(0)
    side = ()
    for step in range(1, len(RING)):
        arrived = [hop(low(total), way) for total, way in zip(totals, WAYS)]
        side = yield side
        tied = together(*arrived, *side)
        side = tied[2:]
        totals = [high(x) + y for x, y in zip(tied, term(step))]
    return totals, side


def no_ring(result):
    side = ()
    for _ in RING[1:]:
        side = yield side
    return result, side


class Stages:
    def __init__(self, generator):
        self.generator = generator
        self.result = None
        next(generator)

    def step(self, *side):
        try:
            return self.generator.send(side)
        except StopIteration as stop:
            self.result, side = stop.value
            return side


def ring_order():
    spots, core = device_ring()
    back = jnp.concatenate([spots[:0:-1], spots[:1]])
    ahead = jnp.concatenate([spots[1:], spots[:1]])
    return jnp.stack([back, ahead, jnp.broadcast_to(core, spots.shape)]).astype(jnp.int32)


def call_ordered(kernel, steps, in_specs, out_specs, out_shape, scratch, order, operands):
    return pl.pallas_call(
        kernel,
        grid_spec=pltpu.PrefetchScalarGridSpec(
            num_scalar_prefetch=1, grid=(steps,), in_specs=in_specs, out_specs=out_specs, scratch_shapes=scratch
        ),
        out_shape=out_shape,
        cost_estimate=SHORT,
        compiler_params=pltpu.CompilerParams(vmem_limit_bytes=24 * MIB),
    )(order, *operands)


def grad_spec(block):
    return pl.BlockSpec((len(RING), HEAD, SET), lambda j, order: (0, block(j) >> 1, block(j) & 1))


def packed_grad_kernel(order_ref, h_ref, o_ref, t_ref, w_ref, j_ref, j2_ref, a_ref, a2_ref, b_ref, b2_ref, k_ref, k2_ref, v_ref, v2_ref, right_ref, left_ref, rows_ref, grad_ref):
    step = pl.program_id(0)
    chips = len(RING)
    tokens, words = a_ref.shape[0], k_ref.shape[0]

    def pick(source_ref, way):
        width = source_ref.shape[1]
        for j in range(chips):
            start = pl.multiple_of((2 * order_ref[way, j] + order_ref[2, 0]) * HEAD, HEAD)
            rows_ref[j * HEAD : (j + 1) * HEAD, :width] = source_ref[pl.ds(start, HEAD)]

    pl.when(step == 0)(lambda: pick(h_ref, 0))
    pl.when(step == MEMBERS)(lambda: pick(o_ref, 1))
    pl.when(step == MEMBERS + 2)(lambda: pick(t_ref, 1))
    pl.when(step == MEMBERS + 4)(lambda: pick(w_ref, 1))

    @pl.when(step < MEMBERS)
    def _():
        for i, (joint, asked) in enumerate(((j_ref, a_ref), (j2_ref, a2_ref))):
            grad_ref[i * tokens : (i + 1) * tokens, : 3 * PAIR] = joint[0]
            grad_ref[i * tokens : (i + 1) * tokens, 3 * PAIR :] = asked[...]
        right_ref[...] = low(dot(rows_ref[...], grad_ref[...])).reshape(chips, HEAD, SET)

    @pl.when((step >= MEMBERS) & (step < MEMBERS + 4))
    def _():
        grad_ref[:tokens] = b_ref[...]
        grad_ref[tokens:] = b2_ref[...]
        left_ref[...] = low(dot(rows_ref[...], grad_ref[...])).reshape(chips, HEAD, SET)

    def memory(first, second):
        grad_ref[:words] = first[...]
        grad_ref[words : 2 * words] = second[...]
        made = dot(rows_ref[:, : 2 * words], grad_ref[: 2 * words])
        left_ref[...] = low(made).reshape(chips, HEAD, SET)

    pl.when((step >= MEMBERS + 4) & (step < MEMBERS + 6))(lambda: memory(k_ref, k2_ref))
    pl.when(step >= MEMBERS + 6)(lambda: memory(v_ref, v2_ref))


def packed_grads(order, hidden, o, text, words, joint_grad, asked_grad, branch_grad, keys_grad, values_grad):
    tokens = asked_grad[0].shape[0]
    chips = len(RING)

    def full(x):
        return pl.BlockSpec(x.shape, lambda j, order: (0, 0))

    def strips(x, first, last):
        return pl.BlockSpec((x.shape[0], SET), lambda j, order: (0, jnp.clip(j - first, 0, last)))

    joint = pl.BlockSpec((1, tokens, 3 * PAIR), lambda j, order: (jnp.minimum(j, MEMBERS - 1), 0, 0))
    asked = pl.BlockSpec((tokens, PAIR), lambda j, order: (0, jnp.minimum(j, MEMBERS - 1)))
    branch = pl.BlockSpec((tokens, SET), lambda j, order: (0, jnp.maximum(j - MEMBERS, 0) & 1))
    keys = strips(keys_grad[0], MEMBERS + 4, 1)
    values = strips(values_grad[0], MEMBERS + 6, 1)
    return call_ordered(
        packed_grad_kernel,
        2 * MEMBERS,
        [full(hidden), full(o), full(text), full(words), joint, joint, asked, asked, branch, branch]
        + [keys, keys, values, values],
        [
            grad_spec(lambda j: jnp.minimum(j, MEMBERS - 1)),
            grad_spec(lambda j: jnp.maximum(j - MEMBERS, 0)),
        ],
        [shaped((chips, 4 * HEAD, D))] * 2,
        [pltpu.VMEM((chips * HEAD, 2 * tokens), LOW), pltpu.VMEM((2 * tokens, SET), LOW)],
        order,
        (hidden, o, text, words) + joint_grad + asked_grad + branch_grad + keys_grad + values_grad,
    )


def turn_kernel(*refs):
    count = len(refs) // 3
    unit = (
        lax.broadcasted_iota(jnp.int32, (PAIR, PAIR), 0) == lax.broadcasted_iota(jnp.int32, (PAIR, PAIR), 1)
    ).astype(LOW)
    for i in range(count):
        own, other, out = refs[2 * i], refs[2 * i + 1], refs[2 * count + i]
        rows = own.shape[-2]
        for j, ref in enumerate((own, other)):
            out[:, j * rows : (j + 1) * rows] = low(dot_right_t(unit, ref[...].reshape(rows, PAIR)))


def turned(*pairs):
    def spec(x):
        if x.ndim == 3:
            return pl.BlockSpec((1, x.shape[1], PAIR), lambda j: (j, 0, 0))
        return pl.BlockSpec((x.shape[0], PAIR), lambda j: (0, j))

    rows = [pair[0].shape[-2] for pair in pairs]
    return call(
        turn_kernel,
        (D // PAIR,),
        [spec(x) for pair in pairs for x in pair],
        [pl.BlockSpec((PAIR, 2 * n), lambda j: (j, 0)) for n in rows],
        [shaped((D, 2 * n)) for n in rows],
        tuple(x for pair in pairs for x in pair),
    )


def feed_grad_kernel(order_ref, s_ref, u_ref, u2_ref, a_ref, a2_ref, f_ref, f2_ref, right_ref, left_ref, rows_ref):
    chips = len(RING)

    @pl.when(pl.program_id(0) == 0)
    def _():
        for j in range(chips):
            start = pl.multiple_of((2 * order_ref[0, j] + order_ref[2, 0]) * HEAD, HEAD)
            rows_ref[j * HEAD : (j + 1) * HEAD] = s_ref[pl.ds(start, HEAD)]

    grad = jnp.concatenate([u_ref[...], u2_ref[...]], 0)
    right_ref[...] = low(dot(rows_ref[...], grad)).reshape(chips, HEAD, SET)
    left_ref[0] = low(dot_left_t(a_ref[...], f_ref[...]) + dot_left_t(a2_ref[...], f2_ref[...]))


def feed_grads(order, second, upper_grad, active, feed_grad):
    tokens = upper_grad[0].shape[0]
    chips = len(RING)
    rows = FF // (2 * chips)
    strip = pl.BlockSpec((tokens, SET), lambda j, order: (0, j))
    hidden = pl.BlockSpec((tokens, rows), lambda j, order: (0, 2 * order[1, j] + order[2, 0]))
    full = pl.BlockSpec((tokens, D), lambda j, order: (0, 0))
    return call_ordered(
        feed_grad_kernel,
        chips,
        [pl.BlockSpec((D, 2 * tokens), lambda j, order: (0, 0)), strip, strip, hidden, hidden, full, full],
        [grad_spec(lambda j: j), pl.BlockSpec((1, rows, D), lambda j, order: (j, 0, 0))],
        [shaped((chips, 4 * HEAD, D)), shaped((chips, rows, D))],
        [pltpu.VMEM((chips * HEAD, 2 * tokens), LOW)],
        order,
        (second,) + upper_grad + active + feed_grad,
    )


def per_device(
    block_input,
    conditioning,
    text_embed,
    text_keep,
    cotangent,
    self_input,
    self_output,
    cross_query,
    cross_memory,
    cross_output,
    up_weight,
    down_weight,
    modulation,
    modulation_bias,
    position_bias,
):
    section = lax.axis_index("section")
    device = lax.axis_index("dp")
    count = lax.axis_size("dp")
    member = device & (MEMBERS - 1)
    clip = device >> 3
    clips = count // MEMBERS
    micro = block_input.shape[0]
    tokens = micro * ROWS
    shard = D // count
    words = MEMBERS * text_embed.shape[1]
    members = [list(range(c * MEMBERS, (c + 1) * MEMBERS)) for c in range(clips)]

    def chosen(first, second):
        return jnp.where(section == 1, second, first)

    def slice_at(x, start, size, axis):
        starts = [0] * x.ndim
        starts[axis] = start
        sizes = list(x.shape)
        sizes[axis] = size
        return lax.dynamic_slice(x, starts, sizes, allow_negative_indices=False)

    def trade(x):
        return lax.all_to_all(x, "dp", 0, 0, tiled=True, axis_index_groups=members)

    def collect(x):
        return trade(jnp.broadcast_to(x, (MEMBERS,) + x.shape))

    ringed = count == 2 * len(RING)

    def parts_of(x):
        x = x.reshape(-1, min(shard, ROWS_OF_PART), x.shape[1] // D, D)
        return jnp.swapaxes(x, 1, 2).reshape(-1, D)

    def gathered(pieces):
        full = [lax.all_gather(x, "dp", axis=0, tiled=True) for x in pieces]
        full = [jnp.swapaxes(x.reshape(PARTS, -1, x.shape[1] // D, D), 1, 2) for x in full]
        return jnp.concatenate([x.reshape(PARTS, -1, D) for x in full], 1)

    grouped = [x[0].reshape(shard, -1, MEMBERS, PAIR) for x in (self_input, cross_query)]
    grouped = jnp.swapaxes(low(jnp.concatenate(grouped, 1)), 1, 2).reshape(shard, 4 * D)
    ring = Stages(ring_gather(parts_of(grouped)) if ringed else no_ring(gathered([grouped])))

    cond_low = low(jax.nn.silu(high(conditioning)))
    cond_rows = slice_at(cond_low, device * shard, shard, 2)
    sums = jnp.einsum("bck,kn->cbn", cond_rows, low(modulation[0]), preferred_element_type=HIGH)
    keep = slice_at(text_keep, clip, 1, 1).astype(LOW)
    text = text_embed * keep[:, :, None]
    sums, text = ring.step(sums, text)

    bit = clips // 2
    while bit:
        upper = (clip & bit) > 0
        halves = (sums[:bit], sums[bit:])
        sums = jnp.where(upper, halves[1], halves[0]) + swap(
            jnp.where(upper, halves[0], halves[1]), bit * MEMBERS
        )
        bit //= 2
    sums = sums[0]
    (sums,) = ring.step(sums)

    text_all = collect(text)
    sums = sums + swap(sums, 1)
    (sums,) = ring.step(sums)

    sums = sums + swap(sums, 2)
    sums, text_all = ring.step(sums, text_all)

    sums = sums + swap(sums, 4)
    (sums,) = ring.step(sums)

    mods = (sums + modulation_bias[0]).reshape(micro, 6, 1, D)
    shift1, scale1, gate1, shift2, scale2, gate2 = [mods[:, i] for i in range(6)]
    hidden = low(layer_mod(high(block_input), shift1, scale1)).reshape(tokens, D)
    mods, hidden = ring.step(mods, hidden)
    shift1, scale1, gate1, shift2, scale2, gate2 = [mods[:, i] for i in range(6)]

    spread = jnp.arange(MEMBERS * CELLS)
    hot0 = place_hot(*places_of(spread // CELLS, spread % CELLS))
    own_table = slice_at(position_bias[0], 2 * member, 2, 0)
    bias0 = bias_of(own_table, hot0, hot0)
    pieces = [low(x[0]) for x in (self_output, cross_output, up_weight, cross_memory, down_weight)]
    hidden, bias0, *pieces = ring.step(hidden, bias0, *pieces)
    packed = ring.result

    def of_frames(x):
        return x.reshape(MEMBERS, -1, CELLS, x.shape[-1])

    def of_tokens(x):
        return x.reshape(MEMBERS, -1, x.shape[-1])

    def branch_and_norm(inputs, mixture, mixture_text):
        branch = merge(mixture, mixture_text, outer).reshape(micro, ROWS, D)
        middle = inputs + gate1 * branch
        second = low(layer_mod(middle, shift2, scale2)).reshape(tokens, D)
        return branch, middle, second

    def feed_forward(kept):
        upper, active, feed = feed_call(kept["second"], outer)
        feed = feed.reshape(micro, ROWS, D)
        kept.update(upper=upper, active=active, feed=feed)
        return low(kept["middle"] + gate2 * feed)

    if ringed:
        ring = Stages(ring_gather(jnp.concatenate([parts_of(x) for x in pieces], 0)))
    else:
        ring = Stages(no_ring(gathered(pieces)))
    joint, asked = project(hidden, packed)
    joint, asked = ring.step(joint, asked)
    joint = [joint[:, i * ROWS : (i + 1) * ROWS] for i in range(micro)]
    joint[0], *joint[1:] = ring.step(trade(joint[0]), *joint[1:])
    mixture, norm = [None] * micro, [None] * micro
    for i in range(micro):
        joint[i] = of_frames(joint[i])
        mixture[i], norm[i] = attend_frames(joint[i], bias0)
        mixture[i] = trade(of_tokens(mixture[i]))
        if i + 1 < micro:
            joint[i + 1], norm[i] = ring.step(trade(joint[i + 1]), norm[i])
    norm[-1], *mixture = ring.step(norm[-1], *mixture)
    mixture = jnp.concatenate(mixture, 1)
    within = jnp.arange(ROWS)
    mine, partner = places_of(member, within), places_of(member ^ 1, within)
    hot_q1 = place_hot(*mine)
    hot_k1 = jnp.concatenate([hot_q1, place_hot(*partner)])
    bias1 = bias_of(position_bias[0], hot_q1, hot_k1)
    bias1, mixture = ring.step(bias1, mixture)
    for _ in range(4 - micro):
        ring.step()
    outer = ring.result
    text_all = jnp.swapaxes(text_all, 0, 1).reshape(micro * words, D)
    memory = text_project(text_all, outer).reshape(micro, words, 2 * D)
    mixture_text, text_norm = attend_text(asked, memory)
    branch, middle, second = branch_and_norm(high(block_input), mixture, mixture_text)
    first = dict(
        x=high(block_input),
        hidden=hidden,
        joint=joint,
        asked=asked,
        norm=norm,
        mixture=mixture,
        mixture_text=mixture_text,
        text_norm=text_norm,
        branch=branch,
        middle=middle,
        second=second,
    )
    first_result = feed_forward(first)

    def back_feed(kept, grad_result):
        gate2_grad = jnp.sum(grad_result * kept["feed"], 1)
        feed_grad = low(gate2 * grad_result).reshape(tokens, D)
        upper_grad, second_grad = feed_back_call(feed_grad, kept["upper"], outer)
        kept.update(feed_grad=feed_grad, upper_grad=upper_grad, second_grad=second_grad, gate2_grad=gate2_grad)

    def back_norm2(kept, grad_result):
        second_grad = kept["second_grad"].reshape(micro, ROWS, D)
        middle_norm, shift2_grad, scale2_grad = jax.vjp(layer_mod, kept["middle"], shift2, scale2)[1](second_grad)
        middle_grad = grad_result + middle_norm
        gate1_grad = jnp.sum(middle_grad * kept["branch"], 1)
        branch_grad = low(gate1 * middle_grad).reshape(tokens, D)
        kept.update(
            middle_grad=middle_grad,
            branch_grad=branch_grad,
            late=[gate1_grad, shift2_grad[:, 0], scale2_grad[:, 0], kept["gate2_grad"]],
        )
        return merge_back(branch_grad, outer)

    def back_norm1(kept):
        hidden_grad = project_back(kept["joint_grad"], kept["asked_grad"], packed)
        inputs_norm, shift1_grad, scale1_grad = jax.vjp(layer_mod, kept["x"], shift1, scale1)[1](
            hidden_grad.reshape(micro, ROWS, D)
        )
        kept["mods"] = jnp.concatenate([shift1_grad[:, 0], scale1_grad[:, 0]] + kept["late"], 1)
        return low(kept["middle_grad"] + inputs_norm)

    received = lax.ppermute(first_result, "section", [(0, 1)])
    received, bias1 = together(received, bias1)
    inputs = high(received)
    hidden = low(layer_mod(inputs, shift1, scale1)).reshape(tokens, D)
    joint, asked = project(hidden, packed)
    other = swap(joint, 1, (1,))
    mixture_text, text_norm = attend_text(asked, memory)
    mixture, norm = attend_window(joint, other, bias1)
    branch, middle, second = branch_and_norm(inputs, mixture, mixture_text)
    latter = dict(
        x=inputs, hidden=hidden, mixture=mixture, mixture_text=mixture_text, branch=branch, middle=middle, second=second
    )
    second_result = feed_forward(latter)
    grad_result = high(cotangent)
    back_feed(latter, grad_result)
    mixture_grad, text_grad = back_norm2(latter, grad_result)
    own, sent, dbias1 = attend_window_back(joint, other, bias1, norm, mixture_grad)
    arrived = swap(sent, 1, (1,))
    latter["asked_grad"], dkt1, dvt1 = attend_text_back(asked, memory, text_norm, text_grad)
    keys = low(high(own[:, :, PAIR:]) + high(arrived))
    latter["joint_grad"] = jnp.concatenate([own[:, :, :PAIR], keys], 2)
    second_grad = back_norm1(latter)
    returned = lax.ppermute(second_grad, "section", [(1, 0)])
    names = ("second", "active", "hidden", "mixture", "mixture_text")
    second_grad, dkt1, dvt1, *kept = together(second_grad, dkt1, dvt1, *[latter[name] for name in names])
    latter.update(zip(names, kept))

    def both(name):
        return chosen(first[name], latter[name])

    ready = [both(name) for name in names]
    apart = count != 2 * len(RING)
    order = None if apart else ring_order()

    def paired(x):
        return (x, x if apart else swap(x, 1))

    def summed(x):
        return high(lax.psum_scatter(x, "dp", scatter_dimension=0, tiled=True))

    second_all, active_all, hidden_all, mixture_all, text_all2 = ready
    columns = [paired(x) for x in (hidden_all, mixture_all, text_all2)] + [(text_all, text_all), paired(second_all)]
    columns = turned(*columns)
    returned, *flat = together(returned, *columns, *paired(active_all))
    columns, active2 = flat[:5], tuple(flat[5:])

    grad_result = high(returned)
    back_feed(first, grad_result)
    upper2, feed2 = paired(both("upper_grad")), paired(both("feed_grad"))
    mixture_grad, text_grad = back_norm2(first, grad_result)
    mixture_grad = of_frames(trade(mixture_grad))
    first["asked_grad"], dkt, dvt = attend_text_back(first["asked"], memory, first["text_norm"], text_grad)
    mixture_grad, dkt, dvt = together(mixture_grad, dkt, dvt)

    def frames_back(i):
        frames = mixture_grad[:, i * FRAMES : (i + 1) * FRAMES]
        grad, dbias = attend_frames_back(first["joint"][i], bias0, first["norm"][i], frames)
        return of_tokens(grad), dbias

    joint_grad, dbias0 = frames_back(0)
    feeds = () if apart else feed_grads(order, columns[4], upper2, active2, feed2)
    traded, *feeds = together(trade(joint_grad), *feeds)
    joint_grad = [traded]
    ring = Stages(no_ring(None) if apart else ring_sums(feeds[:1], feeds[1:]))
    asked2, branch2 = paired(both("asked_grad")), paired(both("branch_grad"))
    keys2, values2 = [paired(chosen(x, y).reshape(micro * words, D)) for x, y in ((dkt, dkt1), (dvt, dvt1))]
    for i in range(1, micro):
        grad, dbias = frames_back(i)
        dbias0 = dbias0 + dbias
        grad, dbias0 = ring.step(trade(grad), dbias0)
        joint_grad.append(grad)
    flat = ring.step(*asked2, *branch2, *keys2, *values2)
    asked2, branch2, keys2, values2 = [tuple(flat[2 * i : 2 * i + 2]) for i in range(4)]
    first["joint_grad"] = jnp.concatenate(joint_grad, 1)
    joint2 = paired(both("joint_grad"))
    if apart:
        joint_all = [jnp.swapaxes(joint2[0], 0, 1), asked2[0].reshape(tokens, MEMBERS, PAIR)]
        joint_all = jnp.concatenate(joint_all, 2).reshape(tokens, 4 * D)
        rights = (joint_all, branch2[0], branch2[0], keys2[0], values2[0], upper2[0], feed2[0])
        lefts = [x[:, :tokens] for x in columns[:3]] + [text_all.T] * 2 + [columns[4][:, :tokens], active2[0].T]
        grads = [summed(low(dot(x, y))) for x, y in zip(lefts, rights)]
    else:
        grads = packed_grads(order, *columns[:4], joint2, asked2, branch2, keys2, values2)
    first["joint_grad"], dbias0, dbias1, *grads = ring.step(first["joint_grad"], dbias0, dbias1, *grads)
    for _ in range(6 - micro):
        ring.step()
    feed_part = ring.result
    ring = Stages(no_ring(grads) if apart else ring_sums(grads[:1], grads[1:]))
    first_grad = back_norm1(first)
    (first_grad,) = ring.step(first_grad)

    table0 = lax.dynamic_update_slice(
        jnp.zeros((HEADS, REL), HIGH), bias_grad(dbias0, hot0, hot0), (2 * member, 0), allow_negative_indices=False
    )
    table = chosen(table0, bias_grad(dbias1, hot_q1, hot_k1))
    small = jnp.concatenate([both("mods").reshape(micro * 6 * D), table.reshape(HEADS * REL)])
    small = jnp.pad(small, (0, -small.shape[0] % 1024)).reshape(1, -1, 128)
    (small,) = ring.step(small)
    small = small + swap(small, 1)
    (small,) = ring.step(small)
    small = small + swap(small, 2)
    (small,) = ring.step(small)
    small = small + swap(small, 4)
    (small,) = ring.step(small)
    bit = 1
    while bit < clips:
        far = swap(small, bit * MEMBERS)
        upper = (clip & bit) > 0
        small = jnp.concatenate([jnp.where(upper, far, small), jnp.where(upper, small, far)])
        bit *= 2
    (small,) = ring.step(small)
    small = small.reshape(clips, -1)
    mods_all = small[:, : micro * 6 * D].reshape(clips, micro, 6 * D)
    table_sum = jnp.sum(small[:, micro * 6 * D : micro * 6 * D + HEADS * REL], 0).reshape(HEADS, REL)
    modul_shard = jnp.einsum("bck,cbn->kn", high(cond_rows), mods_all, precision=lax.Precision.HIGHEST)
    bias_sum = jnp.sum(mods_all, (0, 1))
    if apart:
        up_shard = down_shard = bias_sum
    else:
        up_shard, down_shard = feed_part
        up_shard = jnp.swapaxes(up_shard.reshape(4, shard, D), 0, 1).reshape(shard, 4 * D)
    modul_shard, bias_sum, table_sum, up_shard, down_shard = ring.step(
        modul_shard, bias_sum, table_sum, up_shard, down_shard
    )

    if apart:
        grouped, out_shard, cross_shard, keys, values, up_shard, down_shard = ring.result
        memory_shard = jnp.concatenate([keys, values], 1)
    else:
        grouped, outputs = ring.result
        grouped = jnp.swapaxes(grouped.reshape(4, shard, D), 0, 1).reshape(shard, 4 * D)
        out_shard, cross_shard = outputs[:shard], outputs[shard : 2 * shard]
        memory_shard = jnp.concatenate([outputs[2 * shard : 3 * shard], outputs[3 * shard :]], 1)
    grouped = jnp.swapaxes(grouped.reshape(shard, MEMBERS, 4, PAIR), 1, 2).reshape(shard, 4 * D)
    in_shard, query_shard = grouped[:, : 3 * D], grouped[:, 3 * D :]
    outputs = chosen(first_result, second_result)
    input_grads = chosen(first_grad, second_grad)
    return tuple(
        x[None]
        for x in (
            outputs,
            input_grads,
            in_shard,
            out_shard,
            query_shard,
            memory_shard,
            cross_shard,
            up_shard,
            down_shard,
            modul_shard,
            bias_sum,
            table_sum,
        )
    )


def solution(mesh):
    weights = P("section", "dp", None)
    return jax.shard_map(
        per_device,
        mesh=mesh,
        in_specs=(
            P(None, "dp", None),
            P(),
            P(None, "dp", None),
            P(),
            P(None, "dp", None),
        )
        + (weights,) * 8
        + (P("section", None), P("section", None, None)),
        out_specs=(P("section", None, "dp", None),) * 2
        + (weights,) * 8
        + (P("section", None), P("section", None, None)),
        check_vma=False,
    )
```

```python
import functools

import jax
import jax.numpy as jnp
import numpy as np
from jax import lax
from jax.experimental import pallas as pl
from jax.experimental.pallas import tpu as pltpu
from jax.sharding import PartitionSpec as P

D = 1024
HEADS = 16
HEAD = 64
FF = 4096
FRAMES = 5
BH = 8
BW = 4
CELLS = BH * BW
ROWS = 160
REL = 71
MEMBERS = 8
PAIR = 2 * HEAD
EPSILON = 1e-06
LOW = jnp.bfloat16
HIGH = jnp.float32
MIB = 1024 * 1024
SHORT = pl.CostEstimate(flops=1, bytes_accessed=1, transcendentals=0)


def dot(left, right):
    return lax.dot_general(left, right, (((1,), (0,)), ((), ())), preferred_element_type=HIGH)


def dot_right_t(left, right):
    return lax.dot_general(left, right, (((1,), (1,)), ((), ())), preferred_element_type=HIGH)


def dot_left_t(left, right):
    return lax.dot_general(left, right, (((0,), (0,)), ((), ())), preferred_element_type=HIGH)


def low(v):
    return v.astype(LOW)


def high(v):
    return v.astype(HIGH)


def layer_mod(inputs, offset, factor):
    average = jnp.mean(inputs, axis=-1, keepdims=True)
    centred = inputs - average
    spread = jnp.mean(centred * centred, axis=-1, keepdims=True)
    return centred * lax.rsqrt(spread + EPSILON) * (1.0 + factor) + offset


def swap(x, bits, sections=(0, 1)):
    count = lax.axis_size("dp")
    route = [(s * count + i, s * count + (i ^ bits)) for s in sections for i in range(count)]
    return lax.ppermute(x, ("section", "dp"), route)


def head_masks():
    lane = lax.broadcasted_iota(jnp.int32, (1, PAIR), 1)
    first = (lane < HEAD).astype(LOW)
    return first, 1 - first


def by_head(first, second):
    lane = lax.broadcasted_iota(jnp.int32, (1, PAIR), 1)
    return low(jnp.where(lane < HEAD, first, second))


def pairs_forward(pairs):
    masks = [mask * LOW(HEAD ** (-0.5)) for mask in head_masks()]
    heads = [(q * mask, k, v, bias) for q, k, v, biases in pairs for mask, bias in zip(masks, biases)]
    scores = [dot_right_t(q, k) + bias for q, k, _, bias in heads]
    highest = [jnp.max(x, axis=-1, keepdims=True) for x in scores]
    exponents = [jnp.exp(x - y) for x, y in zip(scores, highest)]
    totals = [jnp.sum(x, axis=-1, keepdims=True) for x in exponents]
    mixed = [dot(low(x), head[2]) * (1.0 / total) for x, head, total in zip(exponents, heads, totals)]
    norms = [x + jnp.log(y) for x, y in zip(highest, totals)]
    return [(by_head(*mixed[i : i + 2]), norms[i : i + 2]) for i in range(0, len(heads), 2)]


def pairs_backward(pairs):
    masks = head_masks()
    heads = [
        (q * mask, k, v, do * mask, bias, norm)
        for q, k, v, do, biases, norms in pairs
        for mask, bias, norm in zip(masks, biases, norms)
    ]
    scale = HEAD ** (-0.5)
    soft = [jnp.exp(dot_right_t(q * LOW(scale), k) + bias - norm) for q, k, _, _, bias, norm in heads]
    grads = [dot_right_t(do, v) for _, _, v, do, _, _ in heads]
    means = [jnp.sum(x * y, axis=-1, keepdims=True) for x, y in zip(soft, grads)]
    grads = [x * (y - z) for x, y, z in zip(soft, grads, means)]
    raw = [low(x * scale) for x in grads]
    dq = [dot(x, head[1]) for x, head in zip(raw, heads)]
    dk = [dot_left_t(head[0], x) for x, head in zip(raw, heads)]
    dv = [dot_left_t(head[3], low(x)) for x, head in zip(soft, heads)]
    return [
        (by_head(*dq[i : i + 2]), low((dk[i] + dk[i + 1]).T), low((dv[i] + dv[i + 1]).T), grads[i : i + 2])
        for i in range(0, len(heads), 2)
    ]


def add_over_steps(ref, index, value, axis):
    @pl.when(pl.program_id(axis) == 0)
    def _():
        ref[index] = value

    @pl.when(pl.program_id(axis) > 0)
    def _():
        ref[index] += value


def part_of(block, part):
    return block[:, part * PAIR : (part + 1) * PAIR]


def frames_pairs(joint_ref, bias_ref):
    for w in range(joint_ref.shape[1]):
        x = joint_ref[:, w].reshape(MEMBERS * CELLS, 3 * PAIR)
        yield part_of(x, 0), part_of(x, 1), part_of(x, 2), (bias_ref[0], bias_ref[1])


def frames_forward(joint_ref, bias_ref, o_ref, norm_ref):
    for w, (o, norms) in enumerate(pairs_forward(list(frames_pairs(joint_ref, bias_ref)))):
        o_ref[:, w] = o.reshape(MEMBERS, CELLS, PAIR)
        norm_ref[w] = jnp.concatenate(norms, 1)


def frames_backward(joint_ref, bias_ref, norm_ref, do_ref, grad_ref, dbias_ref):
    pairs = []
    for w, (q, k, v, biases) in enumerate(frames_pairs(joint_ref, bias_ref)):
        do = do_ref[:, w].reshape(MEMBERS * CELLS, PAIR)
        pairs.append((q, k, v, do, biases, (norm_ref[w, :, 0:1], norm_ref[w, :, 1:2])))
    sums = [0.0, 0.0]
    for w, (dq, dk, dv, dbias) in enumerate(pairs_backward(pairs)):
        for part, value in enumerate((dq, dk, dv)):
            grad_ref[:, w, :, part * PAIR : (part + 1) * PAIR] = value.reshape(MEMBERS, CELLS, PAIR)
        sums = [s + d for s, d in zip(sums, dbias)]
    for a in range(2):
        add_over_steps(dbias_ref, a, sums[a], 0)


def window_pairs(own_ref, other_ref, bias_ref):
    for h in range(own_ref.shape[0]):
        own, other = own_ref[h], other_ref[h]
        k, v = [jnp.concatenate([part_of(own, p), part_of(other, p)], 0) for p in (1, 2)]
        yield part_of(own, 0), k, v, (bias_ref[2 * h], bias_ref[2 * h + 1])


def window_forward(own_ref, other_ref, bias_ref, o_ref, norm_ref):
    made = pairs_forward(list(window_pairs(own_ref, other_ref, bias_ref)))
    for h, (o, _) in enumerate(made):
        o_ref[h] = o
    norm_ref[0, 0] = jnp.concatenate([norm for _, norms in made for norm in norms], 1)


def window_backward(own_ref, other_ref, bias_ref, norm_ref, do_ref, own_grad_ref, other_grad_ref, dbias_ref):
    norms = norm_ref[0, 0]
    pairs = []
    for h, (q, k, v, biases) in enumerate(window_pairs(own_ref, other_ref, bias_ref)):
        pairs.append((q, k, v, do_ref[h], biases, (norms[:, 2 * h : 2 * h + 1], norms[:, 2 * h + 1 : 2 * h + 2])))
    for h, (dq, dk, dv, dbias) in enumerate(pairs_backward(pairs)):
        own_grad_ref[h] = jnp.concatenate([dq, dk[:ROWS], dv[:ROWS]], 1)
        other_grad_ref[h] = jnp.concatenate([dk[ROWS:], dv[ROWS:]], 1)
        for a in range(2):
            add_over_steps(dbias_ref, 2 * h + a, dbias[a], 1)


def text_pairs(q_ref, k_ref, v_ref):
    for h in range(q_ref.shape[1] // PAIR):
        yield part_of(q_ref[...], h), part_of(k_ref[0], h), part_of(v_ref[0], h), (0.0, 0.0)


def text_forward(q_ref, k_ref, v_ref, o_ref, norm_ref):
    made = pairs_forward(list(text_pairs(q_ref, k_ref, v_ref)))
    o_ref[...] = jnp.concatenate([o for o, _ in made], 1)
    norm_ref[0, 0] = jnp.concatenate([norm for _, norms in made for norm in norms], 1)


def text_backward(q_ref, k_ref, v_ref, norm_ref, do_ref, dq_ref, dk_ref, dv_ref):
    norms = norm_ref[0, 0]
    pairs = []
    for h, (q, k, v, biases) in enumerate(text_pairs(q_ref, k_ref, v_ref)):
        heads = (norms[:, 2 * h : 2 * h + 1], norms[:, 2 * h + 1 : 2 * h + 2])
        pairs.append((q, k, v, part_of(do_ref[...], h), biases, heads))
    made = pairs_backward(pairs)
    dq_ref[...], dk_ref[0], dv_ref[0] = [jnp.concatenate([x[i] for x in made], 1) for i in range(3)]


def call(kernel, grid, in_specs, out_specs, out_shape, operands, limit=20):
    return pl.pallas_call(
        kernel,
        grid=grid,
        in_specs=in_specs,
        out_specs=out_specs,
        out_shape=out_shape,
        cost_estimate=SHORT,
        compiler_params=pltpu.CompilerParams(vmem_limit_bytes=limit * MIB),
    )(*operands)


def shaped(shape, dtype=LOW):
    return jax.ShapeDtypeStruct(shape, dtype)


GROUP = 4
GROUPS = HEADS // 2 // GROUP


def frames_specs(joint):
    steps = joint.shape[1] // FRAMES
    wide = pl.BlockSpec((MEMBERS, FRAMES, CELLS, 3 * PAIR), lambda i: (0, i, 0, 0))
    narrow = pl.BlockSpec((MEMBERS, FRAMES, CELLS, PAIR), lambda i: (0, i, 0, 0))
    size = MEMBERS * CELLS
    bias = pl.BlockSpec((2, size, size), lambda i: (0, 0, 0))
    norm = pl.BlockSpec((FRAMES, size, 2), lambda i: (i, 0, 0))
    return steps, wide, narrow, bias, norm


def attend_frames(joint, bias):
    steps, wide, narrow, bias_spec, norm = frames_specs(joint)
    size = MEMBERS * CELLS
    return call(
        frames_forward,
        (steps,),
        [wide, bias_spec],
        [narrow, norm],
        [shaped(joint.shape[:3] + (PAIR,)), shaped((steps * FRAMES, size, 2), HIGH)],
        (joint, bias),
    )


def attend_frames_back(joint, bias, norms, do):
    steps, wide, narrow, bias_spec, norm = frames_specs(joint)
    size = MEMBERS * CELLS
    return call(
        frames_backward,
        (steps,),
        [wide, bias_spec, norm, narrow],
        [wide, bias_spec],
        [shaped(joint.shape), shaped((2, size, size), HIGH)],
        (joint, bias, norms, do),
    )


def window_specs(width):
    return pl.BlockSpec((GROUP, ROWS, width), lambda g, w: (g, w, 0))


BIAS_SPEC = pl.BlockSpec((2 * GROUP, ROWS, 2 * ROWS), lambda g, w: (g, 0, 0))
NORM_SPEC = pl.BlockSpec((1, 1, ROWS, 2 * GROUP), lambda g, w: (g, w, 0, 0))


def attend_window(own, other, bias):
    micro = own.shape[1] // ROWS
    return call(
        window_forward,
        (GROUPS, micro),
        [window_specs(3 * PAIR), window_specs(3 * PAIR), BIAS_SPEC],
        [window_specs(PAIR), NORM_SPEC],
        [shaped(own.shape[:2] + (PAIR,)), shaped((GROUPS, micro, ROWS, 2 * GROUP), HIGH)],
        (own, other, bias),
    )


def attend_window_back(own, other, bias, norms, do):
    micro = own.shape[1] // ROWS
    return call(
        window_backward,
        (GROUPS, micro),
        [window_specs(3 * PAIR), window_specs(3 * PAIR), BIAS_SPEC, NORM_SPEC, window_specs(PAIR)],
        [window_specs(3 * PAIR), window_specs(2 * PAIR), BIAS_SPEC],
        [shaped(own.shape), shaped(own.shape[:2] + (2 * PAIR,)), shaped(bias.shape, HIGH)],
        (own, other, bias, norms, do),
    )


def text_specs(keys):
    rows = pl.BlockSpec((ROWS, GROUP * PAIR), lambda g, w: (w, g))
    k = pl.BlockSpec((1, keys, GROUP * PAIR), lambda g, w: (w, 0, g))
    v = pl.BlockSpec((1, keys, GROUP * PAIR), lambda g, w: (w, 0, GROUPS + g))
    return rows, k, v


def attend_text(asked, memory):
    micro, keys = memory.shape[:2]
    rows, k, v = text_specs(keys)
    return call(
        text_forward,
        (GROUPS, micro),
        [rows, k, v],
        [rows, NORM_SPEC],
        [shaped(asked.shape), shaped((GROUPS, micro, ROWS, 2 * GROUP), HIGH)],
        (asked, memory, memory),
    )


def attend_text_back(asked, memory, norms, do):
    micro, keys = memory.shape[:2]
    rows, k, v = text_specs(keys)
    return call(
        text_backward,
        (GROUPS, micro),
        [rows, k, v, NORM_SPEC, rows],
        [rows, k, k],
        [shaped(asked.shape), shaped((micro, keys, D)), shaped((micro, keys, D))],
        (asked, memory, memory, norms, do),
    )


PARTS = 16
ROWS_OF_PART = D // PARTS
SET = 4 * PAIR
STRIP = D
LARGE = 40


def block_spec(first):
    return pl.BlockSpec((PARTS, ROWS_OF_PART, SET), lambda j: (0, first + (j >> 1), j & 1))


def joined(ref):
    return ref[...].reshape(-1, ref.shape[-1])


def wide_spec(first):
    return pl.BlockSpec((PARTS, ROWS_OF_PART, D), lambda j: (0, first + j, 0))


def rows_spec(shape):
    return pl.BlockSpec(shape, lambda j: (0,) * len(shape))


SETS = D // SET


def project_kernel(hidden_ref, w_ref, joint_ref, asked_ref):
    made = low(dot(hidden_ref[...], joined(w_ref)))
    for i in range(SETS):
        joint_ref[i] = made[:, i * SET : i * SET + 3 * PAIR]
        asked_ref[:, i * PAIR : (i + 1) * PAIR] = made[:, i * SET + 3 * PAIR : (i + 1) * SET]


def project_specs(tokens):
    joint = pl.BlockSpec((SETS, tokens, 3 * PAIR), lambda m: (m, 0, 0))
    asked = pl.BlockSpec((tokens, SETS * PAIR), lambda m: (0, m))
    return joint, asked


def project(hidden, packed):
    tokens = hidden.shape[0]
    return call(
        project_kernel,
        (MEMBERS // SETS,),
        [rows_spec((tokens, D)), wide_spec(0)],
        list(project_specs(tokens)),
        [shaped((MEMBERS, tokens, 3 * PAIR)), shaped((tokens, D))],
        (hidden, packed),
    )


def joint_columns(joint_ref, asked_ref):
    pieces = [x for i in range(SETS) for x in (joint_ref[i], part_of(asked_ref[...], i))]
    return jnp.concatenate(pieces, 1)


def project_back_kernel(joint_ref, asked_ref, w_ref, out_ref):
    grad = joint_columns(joint_ref, asked_ref)
    add_over_steps(out_ref, slice(None), dot_right_t(grad, joined(w_ref)), 0)


def project_back(joint_grad, asked_grad, packed):
    tokens = asked_grad.shape[0]
    return call(
        project_back_kernel,
        (MEMBERS // SETS,),
        [*project_specs(tokens), wide_spec(0)],
        rows_spec((tokens, D)),
        shaped((tokens, D), HIGH),
        (joint_grad, asked_grad, packed),
    )


def text_project_kernel(text_ref, w_ref, out_ref):
    out_ref[...] = low(dot(text_ref[...], joined(w_ref)))


def text_project(text, packed):
    return call(
        text_project_kernel,
        (2 * D // SET,),
        [rows_spec(text.shape), block_spec(4)],
        pl.BlockSpec((text.shape[0], SET), lambda j: (0, j)),
        shaped((text.shape[0], 2 * D)),
        (text, packed),
    )


def merge_kernel(o_ref, text_ref, w_self_ref, w_cross_ref, out_ref):
    o = jnp.concatenate([o_ref[m] for m in range(MEMBERS)], 1)
    out_ref[...] = dot(o, joined(w_self_ref)) + dot(text_ref[...], joined(w_cross_ref))


def merge(o, text, packed):
    tokens = text.shape[0]
    return call(
        merge_kernel,
        (D // SET,),
        [rows_spec((MEMBERS, tokens, PAIR)), rows_spec((tokens, D)), block_spec(8), block_spec(9)],
        pl.BlockSpec((tokens, SET), lambda j: (0, j)),
        shaped((tokens, D), HIGH),
        (o, text, packed, packed),
        LARGE,
    )


def merge_back_kernel(grad_ref, w_self_ref, w_cross_ref, o_ref, text_ref):
    made = low(dot_right_t(grad_ref[...], joined(w_self_ref)))
    for m in range(o_ref.shape[0]):
        o_ref[m] = part_of(made, m)
    text_ref[...] = low(dot_right_t(grad_ref[...], joined(w_cross_ref)))


def merge_back(grad, packed):
    tokens = grad.shape[0]
    height = 2 * PAIR
    parts = height // ROWS_OF_PART
    return call(
        merge_back_kernel,
        (D // height,),
        [
            rows_spec((tokens, D)),
            pl.BlockSpec((parts, ROWS_OF_PART, D), lambda j: (j, 8, 0)),
            pl.BlockSpec((parts, ROWS_OF_PART, D), lambda j: (j, 9, 0)),
        ],
        [pl.BlockSpec((2, tokens, PAIR), lambda j: (j, 0, 0)), pl.BlockSpec((tokens, height), lambda j: (0, j))],
        [shaped((MEMBERS, tokens, PAIR)), shaped((tokens, D))],
        (grad, packed, packed),
        LARGE,
    )


def slices(count):
    width = STRIP // count
    return [slice(i * width, (i + 1) * width) for i in range(count)]


def feed_kernel(s_ref, up_ref, down_ref, upper_ref, active_ref, feed_ref):
    up, down = joined(up_ref), joined(down_ref)
    uppers = [dot(s_ref[...], up[:, at]) for at in slices(4)]
    actives = [low(jax.nn.gelu(x)) for x in uppers]
    for at, upper, active in zip(slices(4), uppers, actives):
        upper_ref[:, at] = low(upper)
        active_ref[:, at] = active
    add_over_steps(feed_ref, slice(None), sum(dot(x, down[at]) for at, x in zip(slices(4), actives)), 0)


def feed_specs(tokens):
    strip = pl.BlockSpec((tokens, STRIP), lambda j: (0, j))
    down = pl.BlockSpec((STRIP // (FF // PARTS), FF // PARTS, D), lambda j: (j, 0, 0))
    return rows_spec((tokens, D)), strip, wide_spec(4), down


def feed_call(second, packed):
    tokens = second.shape[0]
    full, strip, up, down = feed_specs(tokens)
    return call(
        feed_kernel,
        (FF // STRIP,),
        [full, up, down],
        [strip, strip, full],
        [shaped((tokens, FF)), shaped((tokens, FF)), shaped((tokens, D), HIGH)],
        (second, packed, packed),
        LARGE,
    )


def feed_back_kernel(f_ref, upper_ref, up_ref, down_ref, upper_grad_ref, second_grad_ref):
    up, down = joined(up_ref), joined(down_ref)
    grads = [dot_right_t(f_ref[...], down[at]) for at in slices(4)]
    grads = [low(jax.vjp(jax.nn.gelu, high(upper_ref[:, at]))[1](x)[0]) for at, x in zip(slices(4), grads)]
    for at, x in zip(slices(4), grads):
        upper_grad_ref[:, at] = x
    add_over_steps(second_grad_ref, slice(None), sum(dot_right_t(x, up[:, at]) for at, x in zip(slices(4), grads)), 0)


def feed_back_call(feed_grad, upper, packed):
    tokens = feed_grad.shape[0]
    full, strip, up, down = feed_specs(tokens)
    return call(
        feed_back_kernel,
        (FF // STRIP,),
        [full, strip, up, down],
        [strip, full],
        [shaped((tokens, FF)), shaped((tokens, D), HIGH)],
        (feed_grad, upper, packed, packed),
        LARGE,
    )


def pack_columns(x):
    rows = x.shape[0]
    return jnp.swapaxes(x.reshape(rows, -1, D), 0, 1).reshape(-1, D)


def unpack_columns(x, blocks):
    return jnp.swapaxes(x.reshape(blocks, -1, D), 0, 1).reshape(-1, blocks * D)


SPANS = ((FRAMES, FRAMES - 1), (2 * BH, 2 * FRAMES - 1 + 2 * BH - 1), (4 * BW, 2 * FRAMES - 1 + 4 * BH - 1 + 4 * BW - 1))
SPAN = sum(size for size, _ in SPANS)


def table_picks():
    picks = np.zeros((SPAN, SPAN, REL), np.float32)
    start = 0
    for size, middle in SPANS:
        for i in range(size):
            for j in range(size):
                picks[start + i, start + j, middle + i - j] = 1
        start += size
    return picks


def place_hot(frame, row, column):
    marks = []
    for (size, _), place in zip(SPANS, (frame, row, column)):
        marks.append(place[:, None] == jnp.arange(size)[None, :])
    return jnp.concatenate(marks, 1).astype(HIGH)


def places_of(member, within):
    cell = within & (CELLS - 1)
    return (
        within // CELLS + 0 * member,
        (member >> 2) * BH + cell // BW,
        (member & 3) * BW + (cell & (BW - 1)),
    )


def bias_of(table, hot_q, hot_k):
    exact = lax.Precision.HIGHEST
    blocks = jnp.einsum("hn,abn->hab", table, table_picks(), precision=exact)
    left = jnp.einsum("ia,hab->hib", hot_q, blocks, precision=exact)
    return jnp.einsum("hib,jb->hij", left, hot_k, precision=exact)


def bias_grad(grad, hot_q, hot_k):
    exact = lax.Precision.HIGHEST
    right = jnp.einsum("hij,jb->hib", grad, hot_k, precision=exact)
    blocks = jnp.einsum("ia,hib->hab", hot_q, right, precision=exact)
    return jnp.einsum("hab,abn->hn", blocks, table_picks(), precision=exact)


RING = [0, 2, 4, 6, 7, 5, 3, 1]
WAYS = (1, -1)


def together(*values):
    return lax.optimization_barrier(values)


def device_ring():
    device = lax.axis_index("dp")
    chip = device >> 1
    half = len(RING) // 2
    place = jnp.where((chip & 1) == 1, 2 * half - 1 - (chip >> 1), chip >> 1)
    spots = (place + jnp.arange(2 * half)) & (2 * half - 1)
    return jnp.where(spots < half, 2 * spots, 4 * half - 1 - 2 * spots), device & 1


def hop(x, way):
    count = lax.axis_size("dp")
    chips = len(RING)
    route = []
    for s in range(2):
        for i in range(chips):
            for c in range(2):
                source = s * count + RING[i] * 2 + c
                route.append((source, s * count + RING[(i + way) % chips] * 2 + c))
    return lax.ppermute(x, ("section", "dp"), route)


def ring_gather(own, early):
    chips = len(RING)
    half = own.shape[0] // 2
    chunks = [own[:half], own[half:]]
    held = []
    side = ()
    for step in range(chips):
        last = step + 1 == chips
        if not last:
            following = [hop(chunk, way) for chunk, way in zip(chunks, WAYS)]
        held.append([list(chunks), [swap(chunk, 1) for chunk in chunks]])
        if not last:
            side = yield side
            before = [x for pair in held[:-1] for x in pair[1]]
            tied = together(*following, *before, *side)
            chunks = list(tied[:2])
            for i, pair in enumerate(held[:-1]):
                pair[1] = list(tied[2 + 2 * i : 4 + 2 * i])
            side = tied[2 + len(before) :]
        if step == early:
            made = assembled(held, 0, early, None)
        if step == early + 1:
            made, *chunks = together(made, *chunks)
    return assembled(held, early, chips, made), side


def assembled(held, start, end, made):
    chips = len(RING)
    held = held[start:end]
    spots, core = device_ring()
    order = jnp.concatenate([spots, jnp.broadcast_to(core, (1,))]).astype(jnp.int32)
    flat = [x for own, other in held for x in own + other]
    half = flat[0].shape[0]
    shape = (chips, 2, 2 * half, D)

    def kernel(order_ref, *refs):
        sources, (sink, scratch, arrive, leave) = refs[: len(flat)], refs[-4:]
        arriving, leaving = [], []
        for i, ref in enumerate(sources):
            step, which, way = start + i // 4, i // 2 % 2, i % 2
            spot = order_ref[-WAYS[way] * step % chips]
            place = order_ref[chips] if which == 0 else 1 - order_ref[chips]
            where = (spot, place, pl.ds(way * half, half))
            arriving.append(pltpu.make_async_copy(ref, scratch.at[i], arrive.at[i]))
            leaving.append(pltpu.make_async_copy(scratch.at[i], sink.at[where], leave.at[i]))
        for copy in arriving:
            copy.start()
        for copy, onward in zip(arriving, leaving):
            copy.wait()
            onward.start()
        for copy in leaving:
            copy.wait()

    operands = flat if made is None else flat + [made]
    anywhere = pl.BlockSpec(memory_space=pl.ANY)
    made = pl.pallas_call(
        kernel,
        grid_spec=pltpu.PrefetchScalarGridSpec(
            num_scalar_prefetch=1,
            grid=(),
            in_specs=[anywhere] * len(operands),
            out_specs=anywhere,
            scratch_shapes=[pltpu.VMEM((len(flat),) + flat[0].shape, LOW)]
            + [pltpu.SemaphoreType.DMA((len(flat),))] * 2,
        ),
        out_shape=shaped(shape),
        input_output_aliases={} if made is None else {1 + len(flat): 0},
        cost_estimate=SHORT,
        compiler_params=pltpu.CompilerParams(vmem_limit_bytes=58 * MIB),
    )(order, *operands)
    return made if start == 0 else made.reshape(PARTS, 2 * half, D)


def ring_sums(right, left):
    def term(step):
        return [jnp.concatenate([high(x[step]) for x in arrays], 0) for arrays in (right, left)]

    totals = term(0)
    side = ()
    for step in range(1, len(RING)):
        arrived = [hop(low(total), way) for total, way in zip(totals, WAYS)]
        side = yield side
        tied = together(*arrived, *side)
        side = tied[2:]
        totals = [high(x) + y for x, y in zip(tied, term(step))]
    return totals, side


def no_ring(result):
    side = ()
    for _ in RING[1:]:
        side = yield side
    return result, side


class Stages:
    def __init__(self, generator):
        self.generator = generator
        self.result = None
        next(generator)

    def step(self, *side):
        try:
            return self.generator.send(side)
        except StopIteration as stop:
            self.result, side = stop.value
            return side


def ring_order():
    spots, core = device_ring()
    back = jnp.concatenate([spots[:0:-1], spots[:1]])
    ahead = jnp.concatenate([spots[1:], spots[:1]])
    return jnp.stack([back, ahead, jnp.broadcast_to(core, spots.shape)]).astype(jnp.int32)


def call_ordered(kernel, steps, in_specs, out_specs, out_shape, scratch, order, operands):
    return pl.pallas_call(
        kernel,
        grid_spec=pltpu.PrefetchScalarGridSpec(
            num_scalar_prefetch=1, grid=(steps,), in_specs=in_specs, out_specs=out_specs, scratch_shapes=scratch
        ),
        out_shape=out_shape,
        cost_estimate=SHORT,
        compiler_params=pltpu.CompilerParams(vmem_limit_bytes=24 * MIB),
    )(order, *operands)


def grad_spec(block):
    return pl.BlockSpec((len(RING), HEAD, SET), lambda j, order: (0, block(j) >> 1, block(j) & 1))


def packed_grad_kernel(order_ref, h_ref, o_ref, t_ref, w_ref, j_ref, j2_ref, a_ref, a2_ref, b_ref, b2_ref, k_ref, k2_ref, v_ref, v2_ref, right_ref, left_ref, rows_ref, grad_ref):
    step = pl.program_id(0)
    chips = len(RING)
    tokens, words = a_ref.shape[0], k_ref.shape[0]

    def pick(source_ref, way):
        width = source_ref.shape[1]
        for j in range(chips):
            start = pl.multiple_of((2 * order_ref[way, j] + order_ref[2, 0]) * HEAD, HEAD)
            rows_ref[j * HEAD : (j + 1) * HEAD, :width] = source_ref[pl.ds(start, HEAD)]

    pl.when(step == 0)(lambda: pick(h_ref, 0))
    pl.when(step == MEMBERS)(lambda: pick(o_ref, 1))
    pl.when(step == MEMBERS + 2)(lambda: pick(t_ref, 1))
    pl.when(step == MEMBERS + 4)(lambda: pick(w_ref, 1))

    @pl.when(step < MEMBERS)
    def _():
        for i, (joint, asked) in enumerate(((j_ref, a_ref), (j2_ref, a2_ref))):
            grad_ref[i * tokens : (i + 1) * tokens, : 3 * PAIR] = joint[0]
            grad_ref[i * tokens : (i + 1) * tokens, 3 * PAIR :] = asked[...]
        right_ref[...] = low(dot(rows_ref[...], grad_ref[...])).reshape(chips, HEAD, SET)

    @pl.when((step >= MEMBERS) & (step < MEMBERS + 4))
    def _():
        grad_ref[:tokens] = b_ref[...]
        grad_ref[tokens:] = b2_ref[...]
        left_ref[...] = low(dot(rows_ref[...], grad_ref[...])).reshape(chips, HEAD, SET)

    def memory(first, second):
        grad_ref[:words] = first[...]
        grad_ref[words : 2 * words] = second[...]
        made = dot(rows_ref[:, : 2 * words], grad_ref[: 2 * words])
        left_ref[...] = low(made).reshape(chips, HEAD, SET)

    pl.when((step >= MEMBERS + 4) & (step < MEMBERS + 6))(lambda: memory(k_ref, k2_ref))
    pl.when(step >= MEMBERS + 6)(lambda: memory(v_ref, v2_ref))


def packed_grads(order, hidden, o, text, words, joint_grad, asked_grad, branch_grad, keys_grad, values_grad):
    tokens = asked_grad[0].shape[0]
    chips = len(RING)

    def full(x):
        return pl.BlockSpec(x.shape, lambda j, order: (0, 0))

    def strips(x, first, last):
        return pl.BlockSpec((x.shape[0], SET), lambda j, order: (0, jnp.clip(j - first, 0, last)))

    joint = pl.BlockSpec((1, tokens, 3 * PAIR), lambda j, order: (jnp.minimum(j, MEMBERS - 1), 0, 0))
    asked = pl.BlockSpec((tokens, PAIR), lambda j, order: (0, jnp.minimum(j, MEMBERS - 1)))
    branch = pl.BlockSpec((tokens, SET), lambda j, order: (0, jnp.maximum(j - MEMBERS, 0) & 1))
    keys = strips(keys_grad[0], MEMBERS + 4, 1)
    values = strips(values_grad[0], MEMBERS + 6, 1)
    return call_ordered(
        packed_grad_kernel,
        2 * MEMBERS,
        [full(hidden), full(o), full(text), full(words), joint, joint, asked, asked, branch, branch]
        + [keys, keys, values, values],
        [
            grad_spec(lambda j: jnp.minimum(j, MEMBERS - 1)),
            grad_spec(lambda j: jnp.maximum(j - MEMBERS, 0)),
        ],
        [shaped((chips, 4 * HEAD, D))] * 2,
        [pltpu.VMEM((chips * HEAD, 2 * tokens), LOW), pltpu.VMEM((2 * tokens, SET), LOW)],
        order,
        (hidden, o, text, words) + joint_grad + asked_grad + branch_grad + keys_grad + values_grad,
    )


def turn_kernel(*refs):
    count = len(refs) // 3
    unit = (
        lax.broadcasted_iota(jnp.int32, (PAIR, PAIR), 0) == lax.broadcasted_iota(jnp.int32, (PAIR, PAIR), 1)
    ).astype(LOW)
    for i in range(count):
        own, other, out = refs[2 * i], refs[2 * i + 1], refs[2 * count + i]
        rows = own.shape[-2]
        for j, ref in enumerate((own, other)):
            out[:, j * rows : (j + 1) * rows] = low(dot_right_t(unit, ref[...].reshape(rows, PAIR)))


def turned(*pairs):
    def spec(x):
        if x.ndim == 3:
            return pl.BlockSpec((1, x.shape[1], PAIR), lambda j: (j, 0, 0))
        return pl.BlockSpec((x.shape[0], PAIR), lambda j: (0, j))

    rows = [pair[0].shape[-2] for pair in pairs]
    return call(
        turn_kernel,
        (D // PAIR,),
        [spec(x) for pair in pairs for x in pair],
        [pl.BlockSpec((PAIR, 2 * n), lambda j: (j, 0)) for n in rows],
        [shaped((D, 2 * n)) for n in rows],
        tuple(x for pair in pairs for x in pair),
    )


def feed_grad_kernel(order_ref, s_ref, u_ref, u2_ref, a_ref, a2_ref, f_ref, f2_ref, right_ref, left_ref, rows_ref):
    chips = len(RING)

    @pl.when(pl.program_id(0) == 0)
    def _():
        for j in range(chips):
            start = pl.multiple_of((2 * order_ref[0, j] + order_ref[2, 0]) * HEAD, HEAD)
            rows_ref[j * HEAD : (j + 1) * HEAD] = s_ref[pl.ds(start, HEAD)]

    grad = jnp.concatenate([u_ref[...], u2_ref[...]], 0)
    right_ref[...] = low(dot(rows_ref[...], grad)).reshape(chips, HEAD, SET)
    left_ref[0] = low(dot_left_t(a_ref[...], f_ref[...]) + dot_left_t(a2_ref[...], f2_ref[...]))


def feed_grads(order, second, upper_grad, active, feed_grad):
    tokens = upper_grad[0].shape[0]
    chips = len(RING)
    rows = FF // (2 * chips)
    strip = pl.BlockSpec((tokens, SET), lambda j, order: (0, j))
    hidden = pl.BlockSpec((tokens, rows), lambda j, order: (0, 2 * order[1, j] + order[2, 0]))
    full = pl.BlockSpec((tokens, D), lambda j, order: (0, 0))
    return call_ordered(
        feed_grad_kernel,
        chips,
        [pl.BlockSpec((D, 2 * tokens), lambda j, order: (0, 0)), strip, strip, hidden, hidden, full, full],
        [grad_spec(lambda j: j), pl.BlockSpec((1, rows, D), lambda j, order: (j, 0, 0))],
        [shaped((chips, 4 * HEAD, D)), shaped((chips, rows, D))],
        [pltpu.VMEM((chips * HEAD, 2 * tokens), LOW)],
        order,
        (second,) + upper_grad + active + feed_grad,
    )


def per_device(
    block_input,
    conditioning,
    text_embed,
    text_keep,
    cotangent,
    self_input,
    self_output,
    cross_query,
    cross_memory,
    cross_output,
    up_weight,
    down_weight,
    modulation,
    modulation_bias,
    position_bias,
):
    section = lax.axis_index("section")
    device = lax.axis_index("dp")
    count = lax.axis_size("dp")
    member = device & (MEMBERS - 1)
    clip = device >> 3
    clips = count // MEMBERS
    micro = block_input.shape[0]
    tokens = micro * ROWS
    shard = D // count
    words = MEMBERS * text_embed.shape[1]
    members = [list(range(c * MEMBERS, (c + 1) * MEMBERS)) for c in range(clips)]

    def chosen(first, second):
        return jnp.where(section == 1, second, first)

    def slice_at(x, start, size, axis):
        starts = [0] * x.ndim
        starts[axis] = start
        sizes = list(x.shape)
        sizes[axis] = size
        return lax.dynamic_slice(x, starts, sizes, allow_negative_indices=False)

    def trade(x):
        return lax.all_to_all(x, "dp", 0, 0, tiled=True, axis_index_groups=members)

    def collect(x):
        return trade(jnp.broadcast_to(x, (MEMBERS,) + x.shape))

    ringed = count == 2 * len(RING)

    def parts_of(x):
        x = x.reshape(-1, min(shard, ROWS_OF_PART), x.shape[1] // D, D)
        return jnp.swapaxes(x, 1, 2).reshape(-1, D)

    def gathered(pieces):
        full = [lax.all_gather(x, "dp", axis=0, tiled=True) for x in pieces]
        full = [jnp.swapaxes(x.reshape(PARTS, -1, x.shape[1] // D, D), 1, 2) for x in full]
        return jnp.concatenate([x.reshape(PARTS, -1, D) for x in full], 1)

    grouped = [x[0].reshape(shard, -1, MEMBERS, PAIR) for x in (self_input, cross_query)]
    grouped = jnp.swapaxes(low(jnp.concatenate(grouped, 1)), 1, 2).reshape(shard, 4 * D)
    pieces = [grouped, low(cross_memory[0])]
    if ringed:
        ring = Stages(ring_gather(jnp.concatenate([parts_of(x) for x in pieces], 0), 4))
    else:
        ring = Stages(no_ring(gathered(pieces)))

    cond_low = low(jax.nn.silu(high(conditioning)))
    cond_rows = slice_at(cond_low, device * shard, shard, 2)
    sums = jnp.einsum("bck,kn->cbn", cond_rows, low(modulation[0]), preferred_element_type=HIGH)
    keep = slice_at(text_keep, clip, 1, 1).astype(LOW)
    text = text_embed * keep[:, :, None]
    sums, text = ring.step(sums, text)

    bit = clips // 2
    while bit:
        upper = (clip & bit) > 0
        halves = (sums[:bit], sums[bit:])
        sums = jnp.where(upper, halves[1], halves[0]) + swap(
            jnp.where(upper, halves[0], halves[1]), bit * MEMBERS
        )
        bit //= 2
    sums = sums[0]
    (sums,) = ring.step(sums)

    sums = sums + swap(sums, 1)
    (sums,) = ring.step(sums)

    sums = sums + swap(sums, 2)
    (sums,) = ring.step(sums)

    sums = sums + swap(sums, 4)
    (sums,) = ring.step(sums)

    mods = (sums + modulation_bias[0]).reshape(micro, 6, 1, D)
    shift1, scale1, gate1, shift2, scale2, gate2 = [mods[:, i] for i in range(6)]
    hidden = low(layer_mod(high(block_input), shift1, scale1)).reshape(tokens, D)
    mods, hidden = ring.step(mods, hidden)
    shift1, scale1, gate1, shift2, scale2, gate2 = [mods[:, i] for i in range(6)]

    spread = jnp.arange(MEMBERS * CELLS)
    hot0 = place_hot(*places_of(spread // CELLS, spread % CELLS))
    own_table = slice_at(position_bias[0], 2 * member, 2, 0)
    bias0 = bias_of(own_table, hot0, hot0)
    pieces = [low(x[0]) for x in (down_weight, up_weight, self_output, cross_output)]
    hidden, bias0, *pieces = ring.step(hidden, bias0, *pieces)
    packed = ring.result

    def of_frames(x):
        return x.reshape(MEMBERS, -1, CELLS, x.shape[-1])

    def of_tokens(x):
        return x.reshape(MEMBERS, -1, x.shape[-1])

    def branch_and_norm(inputs, mixture, mixture_text):
        branch = merge(mixture, mixture_text, outer).reshape(micro, ROWS, D)
        middle = inputs + gate1 * branch
        second = low(layer_mod(middle, shift2, scale2)).reshape(tokens, D)
        return branch, middle, second

    def feed_forward(kept):
        upper, active, feed = feed_call(kept["second"], outer)
        feed = feed.reshape(micro, ROWS, D)
        kept.update(upper=upper, active=active, feed=feed)
        return low(kept["middle"] + gate2 * feed)

    if ringed:
        ring = Stages(ring_gather(jnp.concatenate([parts_of(x) for x in pieces], 0), 5))
    else:
        ring = Stages(no_ring(gathered(pieces)))
    joint, asked = project(hidden, packed)
    joint, asked = ring.step(joint, asked)
    joint = [joint[:, i * ROWS : (i + 1) * ROWS] for i in range(micro)]
    joint[0], *joint[1:] = ring.step(trade(joint[0]), *joint[1:])
    mixture, norm = [None] * micro, [None] * micro
    for i in range(micro):
        joint[i] = of_frames(joint[i])
        mixture[i], norm[i] = attend_frames(joint[i], bias0)
        mixture[i] = trade(of_tokens(mixture[i]))
        if i + 1 < micro:
            joint[i + 1], norm[i] = ring.step(trade(joint[i + 1]), norm[i])
    norm[-1], *mixture = ring.step(norm[-1], *mixture)
    mixture = jnp.concatenate(mixture, 1)
    within = jnp.arange(ROWS)
    mine, partner = places_of(member, within), places_of(member ^ 1, within)
    hot_q1 = place_hot(*mine)
    hot_k1 = jnp.concatenate([hot_q1, place_hot(*partner)])
    bias1 = bias_of(position_bias[0], hot_q1, hot_k1)
    text_all = collect(text)
    bias1, mixture, text_all = ring.step(bias1, mixture, text_all)
    text_all = jnp.swapaxes(text_all, 0, 1).reshape(micro * words, D)
    memory = text_project(text_all, packed).reshape(micro, words, 2 * D)
    mixture_text, text_norm = attend_text(asked, memory)
    text_all, memory, mixture_text, text_norm = ring.step(text_all, memory, mixture_text, text_norm)
    for _ in range(3 - micro):
        ring.step()
    outer = ring.result
    branch, middle, second = branch_and_norm(high(block_input), mixture, mixture_text)
    first = dict(
        x=high(block_input),
        hidden=hidden,
        joint=joint,
        asked=asked,
        norm=norm,
        mixture=mixture,
        mixture_text=mixture_text,
        text_norm=text_norm,
        branch=branch,
        middle=middle,
        second=second,
    )
    first_result = feed_forward(first)

    def back_feed(kept, grad_result):
        gate2_grad = jnp.sum(grad_result * kept["feed"], 1)
        feed_grad = low(gate2 * grad_result).reshape(tokens, D)
        upper_grad, second_grad = feed_back_call(feed_grad, kept["upper"], outer)
        kept.update(feed_grad=feed_grad, upper_grad=upper_grad, second_grad=second_grad, gate2_grad=gate2_grad)

    def back_norm2(kept, grad_result):
        second_grad = kept["second_grad"].reshape(micro, ROWS, D)
        middle_norm, shift2_grad, scale2_grad = jax.vjp(layer_mod, kept["middle"], shift2, scale2)[1](second_grad)
        middle_grad = grad_result + middle_norm
        gate1_grad = jnp.sum(middle_grad * kept["branch"], 1)
        branch_grad = low(gate1 * middle_grad).reshape(tokens, D)
        kept.update(
            middle_grad=middle_grad,
            branch_grad=branch_grad,
            late=[gate1_grad, shift2_grad[:, 0], scale2_grad[:, 0], kept["gate2_grad"]],
        )
        return merge_back(branch_grad, outer)

    def back_norm1(kept):
        hidden_grad = project_back(kept["joint_grad"], kept["asked_grad"], packed)
        inputs_norm, shift1_grad, scale1_grad = jax.vjp(layer_mod, kept["x"], shift1, scale1)[1](
            hidden_grad.reshape(micro, ROWS, D)
        )
        kept["mods"] = jnp.concatenate([shift1_grad[:, 0], scale1_grad[:, 0]] + kept["late"], 1)
        return low(kept["middle_grad"] + inputs_norm)

    received = lax.ppermute(first_result, "section", [(0, 1)])
    first["joint"], first["norm"] = jnp.concatenate(first["joint"], 1), jnp.concatenate(first["norm"], 0)
    received, bias1, first["joint"], first["norm"] = together(received, bias1, first["joint"], first["norm"])
    inputs = high(received)
    hidden = low(layer_mod(inputs, shift1, scale1)).reshape(tokens, D)
    joint, asked = project(hidden, packed)
    other = swap(joint, 1, (1,))
    mixture_text, text_norm = attend_text(asked, memory)
    mixture, norm = attend_window(joint, other, bias1)
    branch, middle, second = branch_and_norm(inputs, mixture, mixture_text)
    latter = dict(
        x=inputs, hidden=hidden, mixture=mixture, mixture_text=mixture_text, branch=branch, middle=middle, second=second
    )
    second_result = feed_forward(latter)
    grad_result = high(cotangent)
    back_feed(latter, grad_result)
    mixture_grad, text_grad = back_norm2(latter, grad_result)
    own, sent, dbias1 = attend_window_back(joint, other, bias1, norm, mixture_grad)
    arrived = swap(sent, 1, (1,))
    latter["asked_grad"], dkt1, dvt1 = attend_text_back(asked, memory, text_norm, text_grad)
    keys = low(high(own[:, :, PAIR:]) + high(arrived))
    latter["joint_grad"] = jnp.concatenate([own[:, :, :PAIR], keys], 2)
    second_grad = back_norm1(latter)
    returned = lax.ppermute(second_grad, "section", [(1, 0)])
    names = ("second", "active", "hidden", "mixture", "mixture_text")
    second_grad, dkt1, dvt1, *kept = together(second_grad, dkt1, dvt1, *[latter[name] for name in names])
    latter.update(zip(names, kept))

    def both(name):
        return chosen(first[name], latter[name])

    ready = [both(name) for name in names]
    apart = count != 2 * len(RING)
    order = None if apart else ring_order()

    def paired(x):
        return (x, x if apart else swap(x, 1))

    def summed(x):
        return high(lax.psum_scatter(x, "dp", scatter_dimension=0, tiled=True))

    second_all, active_all, hidden_all, mixture_all, text_all2 = ready
    columns = [paired(x) for x in (hidden_all, mixture_all, text_all2)] + [(text_all, text_all), paired(second_all)]
    columns = turned(*columns)
    returned, *flat = together(returned, *columns, *paired(active_all))
    columns, active2 = flat[:5], tuple(flat[5:])

    grad_result = high(returned)
    back_feed(first, grad_result)
    upper2, feed2 = paired(both("upper_grad")), paired(both("feed_grad"))
    mixture_grad, text_grad = back_norm2(first, grad_result)
    mixture_grad = of_frames(trade(mixture_grad))
    first["asked_grad"], dkt, dvt = attend_text_back(first["asked"], memory, first["text_norm"], text_grad)
    mixture_grad, dkt, dvt, *flat = together(mixture_grad, dkt, dvt, *upper2, *feed2)
    upper2, feed2 = tuple(flat[:2]), tuple(flat[2:])

    joint_grad, dbias0 = attend_frames_back(
        first["joint"], bias0, first["norm"], mixture_grad
    )
    feeds = () if apart else feed_grads(order, columns[4], upper2, active2, feed2)
    first["joint_grad"], *feeds = together(trade(of_tokens(joint_grad)), *feeds)
    ring = Stages(no_ring(None) if apart else ring_sums(feeds[:1], feeds[1:]))
    items = [paired(both(x)) for x in ("asked_grad", "branch_grad", "joint_grad")]
    items += [paired(chosen(x, y).reshape(micro * words, D)) for x, y in ((dkt, dkt1), (dvt, dvt1))]
    flat = ring.step(*[x for pair in items for x in pair])
    asked2, branch2, joint2, keys2, values2 = [tuple(flat[2 * i : 2 * i + 2]) for i in range(5)]
    if apart:
        joint_all = [jnp.swapaxes(joint2[0], 0, 1), asked2[0].reshape(tokens, MEMBERS, PAIR)]
        joint_all = jnp.concatenate(joint_all, 2).reshape(tokens, 4 * D)
        rights = (joint_all, branch2[0], branch2[0], keys2[0], values2[0], upper2[0], feed2[0])
        lefts = [x[:, :tokens] for x in columns[:3]] + [text_all.T] * 2 + [columns[4][:, :tokens], active2[0].T]
        grads = [summed(low(dot(x, y))) for x, y in zip(lefts, rights)]
    else:
        grads = packed_grads(order, *columns[:4], joint2, asked2, branch2, keys2, values2)
    first["joint_grad"], dbias0, dbias1, *grads = ring.step(first["joint_grad"], dbias0, dbias1, *grads)
    for _ in range(5):
        ring.step()
    feed_part = ring.result
    ring = Stages(no_ring(grads) if apart else ring_sums(grads[:1], grads[1:]))
    first_grad = back_norm1(first)
    (first_grad,) = ring.step(first_grad)

    table0 = lax.dynamic_update_slice(
        jnp.zeros((HEADS, REL), HIGH), bias_grad(dbias0, hot0, hot0), (2 * member, 0), allow_negative_indices=False
    )
    table = chosen(table0, bias_grad(dbias1, hot_q1, hot_k1))
    small = jnp.concatenate([both("mods").reshape(micro * 6 * D), table.reshape(HEADS * REL)])
    small = jnp.pad(small, (0, -small.shape[0] % 1024)).reshape(1, -1, 128)
    (small,) = ring.step(small)
    small = small + swap(small, 1)
    (small,) = ring.step(small)
    small = small + swap(small, 2)
    (small,) = ring.step(small)
    small = small + swap(small, 4)
    (small,) = ring.step(small)
    bit = 1
    while bit < clips:
        far = swap(small, bit * MEMBERS)
        upper = (clip & bit) > 0
        small = jnp.concatenate([jnp.where(upper, far, small), jnp.where(upper, small, far)])
        bit *= 2
    (small,) = ring.step(small)
    small = small.reshape(clips, -1)
    mods_all = small[:, : micro * 6 * D].reshape(clips, micro, 6 * D)
    table_sum = jnp.sum(small[:, micro * 6 * D : micro * 6 * D + HEADS * REL], 0).reshape(HEADS, REL)
    modul_shard = jnp.einsum("bck,cbn->kn", high(cond_rows), mods_all, precision=lax.Precision.HIGHEST)
    bias_sum = jnp.sum(mods_all, (0, 1))
    if apart:
        up_shard = down_shard = bias_sum
    else:
        up_shard, down_shard = feed_part
        up_shard = jnp.swapaxes(up_shard.reshape(4, shard, D), 0, 1).reshape(shard, 4 * D)
    modul_shard, bias_sum, table_sum, up_shard, down_shard = ring.step(
        modul_shard, bias_sum, table_sum, up_shard, down_shard
    )

    if apart:
        grouped, out_shard, cross_shard, keys, values, up_shard, down_shard = ring.result
        memory_shard = jnp.concatenate([keys, values], 1)
    else:
        grouped, outputs = ring.result
        grouped = jnp.swapaxes(grouped.reshape(4, shard, D), 0, 1).reshape(shard, 4 * D)
        out_shard, cross_shard = outputs[:shard], outputs[shard : 2 * shard]
        memory_shard = jnp.concatenate([outputs[2 * shard : 3 * shard], outputs[3 * shard :]], 1)
    grouped = jnp.swapaxes(grouped.reshape(shard, MEMBERS, 4, PAIR), 1, 2).reshape(shard, 4 * D)
    in_shard, query_shard = grouped[:, : 3 * D], grouped[:, 3 * D :]
    outputs = chosen(first_result, second_result)
    input_grads = chosen(first_grad, second_grad)
    return tuple(
        x[None]
        for x in (
            outputs,
            input_grads,
            in_shard,
            out_shard,
            query_shard,
            memory_shard,
            cross_shard,
            up_shard,
            down_shard,
            modul_shard,
            bias_sum,
            table_sum,
        )
    )


def solution(mesh):
    weights = P("section", "dp", None)
    return jax.shard_map(
        per_device,
        mesh=mesh,
        in_specs=(
            P(None, "dp", None),
            P(),
            P(None, "dp", None),
            P(),
            P(None, "dp", None),
        )
        + (weights,) * 8
        + (P("section", None), P("section", None, None)),
        out_specs=(P("section", None, "dp", None),) * 2
        + (weights,) * 8
        + (P("section", None), P("section", None, None)),
        check_vma=False,
    )
```

```python
import functools

import jax
import jax.numpy as jnp
import numpy as np
from jax import lax
from jax.experimental import pallas as pl
from jax.experimental.pallas import tpu as pltpu
from jax.sharding import PartitionSpec as P

D = 1024
HEADS = 16
HEAD = 64
FF = 4096
FRAMES = 5
BH = 8
BW = 4
CELLS = BH * BW
ROWS = 160
REL = 71
MEMBERS = 8
PAIR = 2 * HEAD
EPSILON = 1e-06
LOW = jnp.bfloat16
HIGH = jnp.float32
MIB = 1024 * 1024
SHORT = pl.CostEstimate(flops=1, bytes_accessed=1, transcendentals=0)


def dot(left, right):
    return lax.dot_general(left, right, (((1,), (0,)), ((), ())), preferred_element_type=HIGH)


def dot_right_t(left, right):
    return lax.dot_general(left, right, (((1,), (1,)), ((), ())), preferred_element_type=HIGH)


def dot_left_t(left, right):
    return lax.dot_general(left, right, (((0,), (0,)), ((), ())), preferred_element_type=HIGH)


def low(v):
    return v.astype(LOW)


def high(v):
    return v.astype(HIGH)


def layer_mod(inputs, offset, factor):
    average = jnp.mean(inputs, axis=-1, keepdims=True)
    centred = inputs - average
    spread = jnp.mean(centred * centred, axis=-1, keepdims=True)
    return centred * lax.rsqrt(spread + EPSILON) * (1.0 + factor) + offset


def swap(x, bits, sections=(0, 1)):
    count = lax.axis_size("dp")
    route = [(s * count + i, s * count + (i ^ bits)) for s in sections for i in range(count)]
    return lax.ppermute(x, ("section", "dp"), route)


def head_masks():
    lane = lax.broadcasted_iota(jnp.int32, (1, PAIR), 1)
    first = (lane < HEAD).astype(LOW)
    return first, 1 - first


def by_head(first, second):
    lane = lax.broadcasted_iota(jnp.int32, (1, PAIR), 1)
    return low(jnp.where(lane < HEAD, first, second))


def pairs_forward(pairs):
    masks = [mask * LOW(HEAD ** (-0.5)) for mask in head_masks()]
    heads = [(q * mask, k, v, bias) for q, k, v, biases in pairs for mask, bias in zip(masks, biases)]
    scores = [dot_right_t(q, k) + bias for q, k, _, bias in heads]
    highest = [jnp.max(x, axis=-1, keepdims=True) for x in scores]
    exponents = [jnp.exp(x - y) for x, y in zip(scores, highest)]
    totals = [jnp.sum(x, axis=-1, keepdims=True) for x in exponents]
    mixed = [dot(low(x), head[2]) * (1.0 / total) for x, head, total in zip(exponents, heads, totals)]
    norms = [x + jnp.log(y) for x, y in zip(highest, totals)]
    return [(by_head(*mixed[i : i + 2]), norms[i : i + 2]) for i in range(0, len(heads), 2)]


def pairs_backward(pairs):
    masks = head_masks()
    heads = [
        (q * mask, k, v, do * mask, bias, norm)
        for q, k, v, do, biases, norms in pairs
        for mask, bias, norm in zip(masks, biases, norms)
    ]
    scale = HEAD ** (-0.5)
    soft = [jnp.exp(dot_right_t(q * LOW(scale), k) + bias - norm) for q, k, _, _, bias, norm in heads]
    grads = [dot_right_t(do, v) for _, _, v, do, _, _ in heads]
    means = [jnp.sum(x * y, axis=-1, keepdims=True) for x, y in zip(soft, grads)]
    grads = [x * (y - z) for x, y, z in zip(soft, grads, means)]
    raw = [low(x * scale) for x in grads]
    dq = [dot(x, head[1]) for x, head in zip(raw, heads)]
    dk = [dot_left_t(head[0], x) for x, head in zip(raw, heads)]
    dv = [dot_left_t(head[3], low(x)) for x, head in zip(soft, heads)]
    return [
        (by_head(*dq[i : i + 2]), low((dk[i] + dk[i + 1]).T), low((dv[i] + dv[i + 1]).T), grads[i : i + 2])
        for i in range(0, len(heads), 2)
    ]


def add_over_steps(ref, index, value, axis):
    @pl.when(pl.program_id(axis) == 0)
    def _():
        ref[index] = value

    @pl.when(pl.program_id(axis) > 0)
    def _():
        ref[index] += value


def part_of(block, part):
    return block[:, part * PAIR : (part + 1) * PAIR]


def frames_pairs(joint_ref, bias_ref):
    for w in range(joint_ref.shape[1]):
        x = joint_ref[:, w].reshape(MEMBERS * CELLS, 3 * PAIR)
        yield part_of(x, 0), part_of(x, 1), part_of(x, 2), (bias_ref[0], bias_ref[1])


def frames_forward(joint_ref, bias_ref, o_ref, norm_ref):
    for w, (o, norms) in enumerate(pairs_forward(list(frames_pairs(joint_ref, bias_ref)))):
        o_ref[:, w] = o.reshape(MEMBERS, CELLS, PAIR)
        norm_ref[w] = jnp.concatenate(norms, 1)


def frames_backward(joint_ref, bias_ref, norm_ref, do_ref, grad_ref, dbias_ref):
    pairs = []
    for w, (q, k, v, biases) in enumerate(frames_pairs(joint_ref, bias_ref)):
        do = do_ref[:, w].reshape(MEMBERS * CELLS, PAIR)
        pairs.append((q, k, v, do, biases, (norm_ref[w, :, 0:1], norm_ref[w, :, 1:2])))
    sums = [0.0, 0.0]
    for w, (dq, dk, dv, dbias) in enumerate(pairs_backward(pairs)):
        for part, value in enumerate((dq, dk, dv)):
            grad_ref[:, w, :, part * PAIR : (part + 1) * PAIR] = value.reshape(MEMBERS, CELLS, PAIR)
        sums = [s + d for s, d in zip(sums, dbias)]
    for a in range(2):
        add_over_steps(dbias_ref, a, sums[a], 0)


def window_pairs(own_ref, other_ref, bias_ref):
    for h in range(own_ref.shape[0]):
        own, other = own_ref[h], other_ref[h]
        k, v = [jnp.concatenate([part_of(own, p), part_of(other, p)], 0) for p in (1, 2)]
        yield part_of(own, 0), k, v, (bias_ref[2 * h], bias_ref[2 * h + 1])


def window_forward(own_ref, other_ref, bias_ref, o_ref, norm_ref):
    made = pairs_forward(list(window_pairs(own_ref, other_ref, bias_ref)))
    for h, (o, _) in enumerate(made):
        o_ref[h] = o
    norm_ref[0, 0] = jnp.concatenate([norm for _, norms in made for norm in norms], 1)


def window_backward(own_ref, other_ref, bias_ref, norm_ref, do_ref, own_grad_ref, other_grad_ref, dbias_ref):
    norms = norm_ref[0, 0]
    pairs = []
    for h, (q, k, v, biases) in enumerate(window_pairs(own_ref, other_ref, bias_ref)):
        pairs.append((q, k, v, do_ref[h], biases, (norms[:, 2 * h : 2 * h + 1], norms[:, 2 * h + 1 : 2 * h + 2])))
    for h, (dq, dk, dv, dbias) in enumerate(pairs_backward(pairs)):
        own_grad_ref[h] = jnp.concatenate([dq, dk[:ROWS], dv[:ROWS]], 1)
        other_grad_ref[h] = jnp.concatenate([dk[ROWS:], dv[ROWS:]], 1)
        for a in range(2):
            add_over_steps(dbias_ref, 2 * h + a, dbias[a], 1)


def text_pairs(q_ref, k_ref, v_ref):
    for h in range(q_ref.shape[1] // PAIR):
        yield part_of(q_ref[...], h), part_of(k_ref[0], h), part_of(v_ref[0], h), (0.0, 0.0)


def text_forward(q_ref, k_ref, v_ref, o_ref, norm_ref):
    made = pairs_forward(list(text_pairs(q_ref, k_ref, v_ref)))
    o_ref[...] = jnp.concatenate([o for o, _ in made], 1)
    norm_ref[0, 0] = jnp.concatenate([norm for _, norms in made for norm in norms], 1)


def text_backward(q_ref, k_ref, v_ref, norm_ref, do_ref, dq_ref, dk_ref, dv_ref):
    norms = norm_ref[0, 0]
    pairs = []
    for h, (q, k, v, biases) in enumerate(text_pairs(q_ref, k_ref, v_ref)):
        heads = (norms[:, 2 * h : 2 * h + 1], norms[:, 2 * h + 1 : 2 * h + 2])
        pairs.append((q, k, v, part_of(do_ref[...], h), biases, heads))
    made = pairs_backward(pairs)
    dq_ref[...], dk_ref[0], dv_ref[0] = [jnp.concatenate([x[i] for x in made], 1) for i in range(3)]


def call(kernel, grid, in_specs, out_specs, out_shape, operands, limit=20):
    return pl.pallas_call(
        kernel,
        grid=grid,
        in_specs=in_specs,
        out_specs=out_specs,
        out_shape=out_shape,
        cost_estimate=SHORT,
        compiler_params=pltpu.CompilerParams(vmem_limit_bytes=limit * MIB),
    )(*operands)


def shaped(shape, dtype=LOW):
    return jax.ShapeDtypeStruct(shape, dtype)


GROUP = 4
GROUPS = HEADS // 2 // GROUP


def frames_specs(joint):
    steps = joint.shape[1] // FRAMES
    wide = pl.BlockSpec((MEMBERS, FRAMES, CELLS, 3 * PAIR), lambda i: (0, i, 0, 0))
    narrow = pl.BlockSpec((MEMBERS, FRAMES, CELLS, PAIR), lambda i: (0, i, 0, 0))
    size = MEMBERS * CELLS
    bias = pl.BlockSpec((2, size, size), lambda i: (0, 0, 0))
    norm = pl.BlockSpec((FRAMES, size, 2), lambda i: (i, 0, 0))
    return steps, wide, narrow, bias, norm


def attend_frames(joint, bias):
    steps, wide, narrow, bias_spec, norm = frames_specs(joint)
    size = MEMBERS * CELLS
    return call(
        frames_forward,
        (steps,),
        [wide, bias_spec],
        [narrow, norm],
        [shaped(joint.shape[:3] + (PAIR,)), shaped((steps * FRAMES, size, 2), HIGH)],
        (joint, bias),
    )


def attend_frames_back(joint, bias, norms, do):
    steps, wide, narrow, bias_spec, norm = frames_specs(joint)
    size = MEMBERS * CELLS
    return call(
        frames_backward,
        (steps,),
        [wide, bias_spec, norm, narrow],
        [wide, bias_spec],
        [shaped(joint.shape), shaped((2, size, size), HIGH)],
        (joint, bias, norms, do),
    )


def window_specs(width):
    return pl.BlockSpec((GROUP, ROWS, width), lambda g, w: (g, w, 0))


BIAS_SPEC = pl.BlockSpec((2 * GROUP, ROWS, 2 * ROWS), lambda g, w: (g, 0, 0))
NORM_SPEC = pl.BlockSpec((1, 1, ROWS, 2 * GROUP), lambda g, w: (g, w, 0, 0))


def attend_window(own, other, bias):
    micro = own.shape[1] // ROWS
    return call(
        window_forward,
        (GROUPS, micro),
        [window_specs(3 * PAIR), window_specs(3 * PAIR), BIAS_SPEC],
        [window_specs(PAIR), NORM_SPEC],
        [shaped(own.shape[:2] + (PAIR,)), shaped((GROUPS, micro, ROWS, 2 * GROUP), HIGH)],
        (own, other, bias),
    )


def attend_window_back(own, other, bias, norms, do):
    micro = own.shape[1] // ROWS
    return call(
        window_backward,
        (GROUPS, micro),
        [window_specs(3 * PAIR), window_specs(3 * PAIR), BIAS_SPEC, NORM_SPEC, window_specs(PAIR)],
        [window_specs(3 * PAIR), window_specs(2 * PAIR), BIAS_SPEC],
        [shaped(own.shape), shaped(own.shape[:2] + (2 * PAIR,)), shaped(bias.shape, HIGH)],
        (own, other, bias, norms, do),
    )


def text_specs(keys):
    rows = pl.BlockSpec((ROWS, GROUP * PAIR), lambda g, w: (w, g))
    k = pl.BlockSpec((1, keys, GROUP * PAIR), lambda g, w: (w, 0, g))
    v = pl.BlockSpec((1, keys, GROUP * PAIR), lambda g, w: (w, 0, GROUPS + g))
    return rows, k, v


def attend_text(asked, memory):
    micro, keys = memory.shape[:2]
    rows, k, v = text_specs(keys)
    return call(
        text_forward,
        (GROUPS, micro),
        [rows, k, v],
        [rows, NORM_SPEC],
        [shaped(asked.shape), shaped((GROUPS, micro, ROWS, 2 * GROUP), HIGH)],
        (asked, memory, memory),
    )


def attend_text_back(asked, memory, norms, do):
    micro, keys = memory.shape[:2]
    rows, k, v = text_specs(keys)
    return call(
        text_backward,
        (GROUPS, micro),
        [rows, k, v, NORM_SPEC, rows],
        [rows, k, k],
        [shaped(asked.shape), shaped((micro, keys, D)), shaped((micro, keys, D))],
        (asked, memory, memory, norms, do),
    )


PARTS = 16
ROWS_OF_PART = D // PARTS
SET = 4 * PAIR
STRIP = D
LARGE = 40


def block_spec(first):
    return pl.BlockSpec((PARTS, ROWS_OF_PART, SET), lambda j: (0, first + (j >> 1), j & 1))


def joined(ref):
    return ref[...].reshape(-1, ref.shape[-1])


def wide_spec(first):
    return pl.BlockSpec((PARTS, ROWS_OF_PART, D), lambda j: (0, first + j, 0))


def rows_spec(shape):
    return pl.BlockSpec(shape, lambda j: (0,) * len(shape))


SETS = D // SET


def project_kernel(hidden_ref, w_ref, joint_ref, asked_ref):
    made = low(dot(hidden_ref[...], joined(w_ref)))
    for i in range(SETS):
        joint_ref[i] = made[:, i * SET : i * SET + 3 * PAIR]
        asked_ref[:, i * PAIR : (i + 1) * PAIR] = made[:, i * SET + 3 * PAIR : (i + 1) * SET]


def project_specs(tokens):
    joint = pl.BlockSpec((SETS, tokens, 3 * PAIR), lambda m: (m, 0, 0))
    asked = pl.BlockSpec((tokens, SETS * PAIR), lambda m: (0, m))
    return joint, asked


def project(hidden, packed):
    tokens = hidden.shape[0]
    return call(
        project_kernel,
        (MEMBERS // SETS,),
        [rows_spec((tokens, D)), wide_spec(0)],
        list(project_specs(tokens)),
        [shaped((MEMBERS, tokens, 3 * PAIR)), shaped((tokens, D))],
        (hidden, packed),
    )


def joint_columns(joint_ref, asked_ref):
    pieces = [x for i in range(SETS) for x in (joint_ref[i], part_of(asked_ref[...], i))]
    return jnp.concatenate(pieces, 1)


def project_back_kernel(joint_ref, asked_ref, w_ref, out_ref):
    grad = joint_columns(joint_ref, asked_ref)
    add_over_steps(out_ref, slice(None), dot_right_t(grad, joined(w_ref)), 0)


def project_back(joint_grad, asked_grad, packed):
    tokens = asked_grad.shape[0]
    return call(
        project_back_kernel,
        (MEMBERS // SETS,),
        [*project_specs(tokens), wide_spec(0)],
        rows_spec((tokens, D)),
        shaped((tokens, D), HIGH),
        (joint_grad, asked_grad, packed),
        LARGE + 12,
    )


def text_project_kernel(text_ref, w_ref, out_ref):
    out_ref[...] = low(dot(text_ref[...], joined(w_ref)))


def text_project(text, packed):
    return call(
        text_project_kernel,
        (2 * D // SET,),
        [rows_spec(text.shape), block_spec(4)],
        pl.BlockSpec((text.shape[0], SET), lambda j: (0, j)),
        shaped((text.shape[0], 2 * D)),
        (text, packed),
    )


def merge_kernel(o_ref, text_ref, w_self_ref, w_cross_ref, out_ref):
    o = jnp.concatenate([o_ref[m] for m in range(MEMBERS)], 1)
    out_ref[...] = dot(o, joined(w_self_ref)) + dot(text_ref[...], joined(w_cross_ref))


def merge(o, text, packed):
    tokens = text.shape[0]
    return call(
        merge_kernel,
        (D // SET,),
        [rows_spec((MEMBERS, tokens, PAIR)), rows_spec((tokens, D)), block_spec(8), block_spec(9)],
        pl.BlockSpec((tokens, SET), lambda j: (0, j)),
        shaped((tokens, D), HIGH),
        (o, text, packed, packed),
        LARGE,
    )


def merge_back_kernel(grad_ref, w_self_ref, w_cross_ref, o_ref, text_ref):
    made = low(dot_right_t(grad_ref[...], joined(w_self_ref)))
    for m in range(o_ref.shape[0]):
        o_ref[m] = part_of(made, m)
    text_ref[...] = low(dot_right_t(grad_ref[...], joined(w_cross_ref)))


def merge_back(grad, packed):
    tokens = grad.shape[0]
    height = 2 * PAIR
    parts = height // ROWS_OF_PART
    return call(
        merge_back_kernel,
        (D // height,),
        [
            rows_spec((tokens, D)),
            pl.BlockSpec((parts, ROWS_OF_PART, D), lambda j: (j, 8, 0)),
            pl.BlockSpec((parts, ROWS_OF_PART, D), lambda j: (j, 9, 0)),
        ],
        [pl.BlockSpec((2, tokens, PAIR), lambda j: (j, 0, 0)), pl.BlockSpec((tokens, height), lambda j: (0, j))],
        [shaped((MEMBERS, tokens, PAIR)), shaped((tokens, D))],
        (grad, packed, packed),
        LARGE,
    )


def slices(count):
    width = STRIP // count
    return [slice(i * width, (i + 1) * width) for i in range(count)]


def feed_kernel(s_ref, up_ref, down_ref, upper_ref, active_ref, feed_ref):
    up, down = joined(up_ref), joined(down_ref)
    uppers = [dot(s_ref[...], up[:, at]) for at in slices(4)]
    actives = [low(jax.nn.gelu(x)) for x in uppers]
    for at, upper, active in zip(slices(4), uppers, actives):
        upper_ref[:, at] = low(upper)
        active_ref[:, at] = active
    add_over_steps(feed_ref, slice(None), sum(dot(x, down[at]) for at, x in zip(slices(4), actives)), 0)


def feed_specs(tokens):
    strip = pl.BlockSpec((tokens, STRIP), lambda j: (0, j))
    down = pl.BlockSpec((STRIP // (FF // PARTS), FF // PARTS, D), lambda j: (j, 0, 0))
    return rows_spec((tokens, D)), strip, wide_spec(4), down


def feed_call(second, packed):
    tokens = second.shape[0]
    full, strip, up, down = feed_specs(tokens)
    return call(
        feed_kernel,
        (FF // STRIP,),
        [full, up, down],
        [strip, strip, full],
        [shaped((tokens, FF)), shaped((tokens, FF)), shaped((tokens, D), HIGH)],
        (second, packed, packed),
        LARGE,
    )


def feed_back_kernel(f_ref, upper_ref, up_ref, down_ref, upper_grad_ref, second_grad_ref):
    up, down = joined(up_ref), joined(down_ref)
    grads = [dot_right_t(f_ref[...], down[at]) for at in slices(4)]
    grads = [low(jax.vjp(jax.nn.gelu, high(upper_ref[:, at]))[1](x)[0]) for at, x in zip(slices(4), grads)]
    for at, x in zip(slices(4), grads):
        upper_grad_ref[:, at] = x
    add_over_steps(second_grad_ref, slice(None), sum(dot_right_t(x, up[:, at]) for at, x in zip(slices(4), grads)), 0)


def feed_back_call(feed_grad, upper, packed):
    tokens = feed_grad.shape[0]
    full, strip, up, down = feed_specs(tokens)
    return call(
        feed_back_kernel,
        (FF // STRIP,),
        [full, strip, up, down],
        [strip, full],
        [shaped((tokens, FF)), shaped((tokens, D), HIGH)],
        (feed_grad, upper, packed, packed),
        LARGE,
    )


def pack_columns(x):
    rows = x.shape[0]
    return jnp.swapaxes(x.reshape(rows, -1, D), 0, 1).reshape(-1, D)


def unpack_columns(x, blocks):
    return jnp.swapaxes(x.reshape(blocks, -1, D), 0, 1).reshape(-1, blocks * D)


SPANS = ((FRAMES, FRAMES - 1), (2 * BH, 2 * FRAMES - 1 + 2 * BH - 1), (4 * BW, 2 * FRAMES - 1 + 4 * BH - 1 + 4 * BW - 1))
SPAN = sum(size for size, _ in SPANS)


def table_picks():
    picks = np.zeros((SPAN, SPAN, REL), np.float32)
    start = 0
    for size, middle in SPANS:
        for i in range(size):
            for j in range(size):
                picks[start + i, start + j, middle + i - j] = 1
        start += size
    return picks


def place_hot(frame, row, column):
    marks = []
    for (size, _), place in zip(SPANS, (frame, row, column)):
        marks.append(place[:, None] == jnp.arange(size)[None, :])
    return jnp.concatenate(marks, 1).astype(HIGH)


def places_of(member, within):
    cell = within & (CELLS - 1)
    return (
        within // CELLS + 0 * member,
        (member >> 2) * BH + cell // BW,
        (member & 3) * BW + (cell & (BW - 1)),
    )


def bias_of(table, hot_q, hot_k):
    exact = lax.Precision.HIGHEST
    blocks = jnp.einsum("hn,abn->hab", table, table_picks(), precision=exact)
    left = jnp.einsum("ia,hab->hib", hot_q, blocks, precision=exact)
    return jnp.einsum("hib,jb->hij", left, hot_k, precision=exact)


def bias_grad(grad, hot_q, hot_k):
    exact = lax.Precision.HIGHEST
    right = jnp.einsum("hij,jb->hib", grad, hot_k, precision=exact)
    blocks = jnp.einsum("ia,hib->hab", hot_q, right, precision=exact)
    return jnp.einsum("hab,abn->hn", blocks, table_picks(), precision=exact)


RING = [0, 2, 4, 6, 7, 5, 3, 1]
WAYS = (1, -1)


def together(*values):
    return lax.optimization_barrier(values)


def device_ring():
    device = lax.axis_index("dp")
    chip = device >> 1
    half = len(RING) // 2
    place = jnp.where((chip & 1) == 1, 2 * half - 1 - (chip >> 1), chip >> 1)
    spots = (place + jnp.arange(2 * half)) & (2 * half - 1)
    return jnp.where(spots < half, 2 * spots, 4 * half - 1 - 2 * spots), device & 1


def hop(x, way):
    count = lax.axis_size("dp")
    chips = len(RING)
    route = []
    for s in range(2):
        for i in range(chips):
            for c in range(2):
                source = s * count + RING[i] * 2 + c
                route.append((source, s * count + RING[(i + way) % chips] * 2 + c))
    return lax.ppermute(x, ("section", "dp"), route)


def ring_gather(own, early):
    chips = len(RING)
    half = own.shape[0] // 2
    chunks = [own[:half], own[half:]]
    held = []
    side = ()
    for step in range(chips):
        last = step + 1 == chips
        if not last:
            following = [hop(chunk, way) for chunk, way in zip(chunks, WAYS)]
        held.append([list(chunks), [swap(chunk, 1) for chunk in chunks]])
        if not last:
            side = yield side
            before = [x for pair in held[:-1] for x in pair[1]]
            tied = together(*following, *before, *side)
            chunks = list(tied[:2])
            for i, pair in enumerate(held[:-1]):
                pair[1] = list(tied[2 + 2 * i : 4 + 2 * i])
            side = tied[2 + len(before) :]
        if step == early:
            made = assembled(held, 0, early, None)
        if step == early + 1:
            made, *chunks = together(made, *chunks)
    return assembled(held, early, chips, made), side


def assembled(held, start, end, made):
    chips = len(RING)
    held = held[start:end]
    spots, core = device_ring()
    order = jnp.concatenate([spots, jnp.broadcast_to(core, (1,))]).astype(jnp.int32)
    flat = [x for own, other in held for x in own + other]
    half = flat[0].shape[0]
    shape = (chips, 2, 2 * half, D)

    def kernel(order_ref, *refs):
        sources, (sink, scratch, arrive, leave) = refs[: len(flat)], refs[-4:]
        arriving, leaving = [], []
        for i, ref in enumerate(sources):
            step, which, way = start + i // 4, i // 2 % 2, i % 2
            spot = order_ref[-WAYS[way] * step % chips]
            place = order_ref[chips] if which == 0 else 1 - order_ref[chips]
            where = (spot, place, pl.ds(way * half, half))
            arriving.append(pltpu.make_async_copy(ref, scratch.at[i], arrive.at[i]))
            leaving.append(pltpu.make_async_copy(scratch.at[i], sink.at[where], leave.at[i]))
        for copy in arriving:
            copy.start()
        for copy, onward in zip(arriving, leaving):
            copy.wait()
            onward.start()
        for copy in leaving:
            copy.wait()

    operands = flat if made is None else flat + [made]
    anywhere = pl.BlockSpec(memory_space=pl.ANY)
    made = pl.pallas_call(
        kernel,
        grid_spec=pltpu.PrefetchScalarGridSpec(
            num_scalar_prefetch=1,
            grid=(),
            in_specs=[anywhere] * len(operands),
            out_specs=anywhere,
            scratch_shapes=[pltpu.VMEM((len(flat),) + flat[0].shape, LOW)]
            + [pltpu.SemaphoreType.DMA((len(flat),))] * 2,
        ),
        out_shape=shaped(shape),
        input_output_aliases={} if made is None else {1 + len(flat): 0},
        cost_estimate=SHORT,
        compiler_params=pltpu.CompilerParams(vmem_limit_bytes=58 * MIB),
    )(order, *operands)
    return made if start == 0 else made.reshape(PARTS, 2 * half, D)


def ring_sums(right, left):
    def term(step):
        return [jnp.concatenate([high(x[step]) for x in arrays], 0) for arrays in (right, left)]

    totals = term(0)
    side = ()
    for step in range(1, len(RING)):
        arrived = [hop(low(total), way) for total, way in zip(totals, WAYS)]
        side = yield side
        tied = together(*arrived, *side)
        side = tied[2:]
        totals = [high(x) + y for x, y in zip(tied, term(step))]
    return totals, side


def no_ring(result):
    side = ()
    for _ in RING[1:]:
        side = yield side
    return result, side


class Stages:
    def __init__(self, generator):
        self.generator = generator
        self.result = None
        next(generator)

    def step(self, *side):
        try:
            return self.generator.send(side)
        except StopIteration as stop:
            self.result, side = stop.value
            return side


def ring_order():
    spots, core = device_ring()
    back = jnp.concatenate([spots[:0:-1], spots[:1]])
    ahead = jnp.concatenate([spots[1:], spots[:1]])
    return jnp.stack([back, ahead, jnp.broadcast_to(core, spots.shape)]).astype(jnp.int32)


def call_ordered(kernel, steps, in_specs, out_specs, out_shape, scratch, order, operands):
    return pl.pallas_call(
        kernel,
        grid_spec=pltpu.PrefetchScalarGridSpec(
            num_scalar_prefetch=1, grid=(steps,), in_specs=in_specs, out_specs=out_specs, scratch_shapes=scratch
        ),
        out_shape=out_shape,
        cost_estimate=SHORT,
        compiler_params=pltpu.CompilerParams(vmem_limit_bytes=24 * MIB),
    )(order, *operands)


def grad_spec(block):
    return pl.BlockSpec((len(RING), HEAD, SET), lambda j, order: (0, block(j) >> 1, block(j) & 1))


def packed_grad_kernel(order_ref, h_ref, o_ref, t_ref, w_ref, j_ref, j2_ref, a_ref, a2_ref, b_ref, b2_ref, k_ref, k2_ref, v_ref, v2_ref, right_ref, left_ref, rows_ref, grad_ref):
    step = pl.program_id(0)
    chips = len(RING)
    tokens, words = a_ref.shape[0], k_ref.shape[0]

    def pick(source_ref, way):
        width = source_ref.shape[1]
        for j in range(chips):
            start = pl.multiple_of((2 * order_ref[way, j] + order_ref[2, 0]) * HEAD, HEAD)
            rows_ref[j * HEAD : (j + 1) * HEAD, :width] = source_ref[pl.ds(start, HEAD)]

    pl.when(step == 0)(lambda: pick(h_ref, 0))
    pl.when(step == MEMBERS)(lambda: pick(o_ref, 1))
    pl.when(step == MEMBERS + 2)(lambda: pick(t_ref, 1))
    pl.when(step == MEMBERS + 4)(lambda: pick(w_ref, 1))

    @pl.when(step < MEMBERS)
    def _():
        for i, (joint, asked) in enumerate(((j_ref, a_ref), (j2_ref, a2_ref))):
            grad_ref[i * tokens : (i + 1) * tokens, : 3 * PAIR] = joint[0]
            grad_ref[i * tokens : (i + 1) * tokens, 3 * PAIR :] = asked[...]
        right_ref[...] = low(dot(rows_ref[...], grad_ref[...])).reshape(chips, HEAD, SET)

    @pl.when((step >= MEMBERS) & (step < MEMBERS + 4))
    def _():
        grad_ref[:tokens] = b_ref[...]
        grad_ref[tokens:] = b2_ref[...]
        left_ref[...] = low(dot(rows_ref[...], grad_ref[...])).reshape(chips, HEAD, SET)

    def memory(first, second):
        grad_ref[:words] = first[...]
        grad_ref[words : 2 * words] = second[...]
        made = dot(rows_ref[:, : 2 * words], grad_ref[: 2 * words])
        left_ref[...] = low(made).reshape(chips, HEAD, SET)

    pl.when((step >= MEMBERS + 4) & (step < MEMBERS + 6))(lambda: memory(k_ref, k2_ref))
    pl.when(step >= MEMBERS + 6)(lambda: memory(v_ref, v2_ref))


def packed_grads(order, hidden, o, text, words, joint_grad, asked_grad, branch_grad, keys_grad, values_grad):
    tokens = asked_grad[0].shape[0]
    chips = len(RING)

    def full(x):
        return pl.BlockSpec(x.shape, lambda j, order: (0, 0))

    def strips(x, first, last):
        return pl.BlockSpec((x.shape[0], SET), lambda j, order: (0, jnp.clip(j - first, 0, last)))

    joint = pl.BlockSpec((1, tokens, 3 * PAIR), lambda j, order: (jnp.minimum(j, MEMBERS - 1), 0, 0))
    asked = pl.BlockSpec((tokens, PAIR), lambda j, order: (0, jnp.minimum(j, MEMBERS - 1)))
    branch = pl.BlockSpec((tokens, SET), lambda j, order: (0, jnp.maximum(j - MEMBERS, 0) & 1))
    keys = strips(keys_grad[0], MEMBERS + 4, 1)
    values = strips(values_grad[0], MEMBERS + 6, 1)
    return call_ordered(
        packed_grad_kernel,
        2 * MEMBERS,
        [full(hidden), full(o), full(text), full(words), joint, joint, asked, asked, branch, branch]
        + [keys, keys, values, values],
        [
            grad_spec(lambda j: jnp.minimum(j, MEMBERS - 1)),
            grad_spec(lambda j: jnp.maximum(j - MEMBERS, 0)),
        ],
        [shaped((chips, 4 * HEAD, D))] * 2,
        [pltpu.VMEM((chips * HEAD, 2 * tokens), LOW), pltpu.VMEM((2 * tokens, SET), LOW)],
        order,
        (hidden, o, text, words) + joint_grad + asked_grad + branch_grad + keys_grad + values_grad,
    )


def turn_kernel(*refs):
    count = len(refs) // 3
    unit = (
        lax.broadcasted_iota(jnp.int32, (PAIR, PAIR), 0) == lax.broadcasted_iota(jnp.int32, (PAIR, PAIR), 1)
    ).astype(LOW)
    for i in range(count):
        own, other, out = refs[2 * i], refs[2 * i + 1], refs[2 * count + i]
        rows = own.shape[-2]
        for j, ref in enumerate((own, other)):
            out[:, j * rows : (j + 1) * rows] = low(dot_right_t(unit, ref[...].reshape(rows, PAIR)))


def turned(*pairs):
    def spec(x):
        if x.ndim == 3:
            return pl.BlockSpec((1, x.shape[1], PAIR), lambda j: (j, 0, 0))
        return pl.BlockSpec((x.shape[0], PAIR), lambda j: (0, j))

    rows = [pair[0].shape[-2] for pair in pairs]
    return call(
        turn_kernel,
        (D // PAIR,),
        [spec(x) for pair in pairs for x in pair],
        [pl.BlockSpec((PAIR, 2 * n), lambda j: (j, 0)) for n in rows],
        [shaped((D, 2 * n)) for n in rows],
        tuple(x for pair in pairs for x in pair),
    )


def feed_grad_kernel(order_ref, s_ref, u_ref, u2_ref, a_ref, a2_ref, f_ref, f2_ref, right_ref, left_ref, rows_ref):
    chips = len(RING)

    @pl.when(pl.program_id(0) == 0)
    def _():
        for j in range(chips):
            start = pl.multiple_of((2 * order_ref[0, j] + order_ref[2, 0]) * HEAD, HEAD)
            rows_ref[j * HEAD : (j + 1) * HEAD] = s_ref[pl.ds(start, HEAD)]

    grad = jnp.concatenate([u_ref[...], u2_ref[...]], 0)
    right_ref[...] = low(dot(rows_ref[...], grad)).reshape(chips, HEAD, SET)
    left_ref[0] = low(dot_left_t(a_ref[...], f_ref[...]) + dot_left_t(a2_ref[...], f2_ref[...]))


def feed_grads(order, second, upper_grad, active, feed_grad):
    tokens = upper_grad[0].shape[0]
    chips = len(RING)
    rows = FF // (2 * chips)
    strip = pl.BlockSpec((tokens, SET), lambda j, order: (0, j))
    hidden = pl.BlockSpec((tokens, rows), lambda j, order: (0, 2 * order[1, j] + order[2, 0]))
    full = pl.BlockSpec((tokens, D), lambda j, order: (0, 0))
    return call_ordered(
        feed_grad_kernel,
        chips,
        [pl.BlockSpec((D, 2 * tokens), lambda j, order: (0, 0)), strip, strip, hidden, hidden, full, full],
        [grad_spec(lambda j: j), pl.BlockSpec((1, rows, D), lambda j, order: (j, 0, 0))],
        [shaped((chips, 4 * HEAD, D)), shaped((chips, rows, D))],
        [pltpu.VMEM((chips * HEAD, 2 * tokens), LOW)],
        order,
        (second,) + upper_grad + active + feed_grad,
    )


def per_device(
    block_input,
    conditioning,
    text_embed,
    text_keep,
    cotangent,
    self_input,
    self_output,
    cross_query,
    cross_memory,
    cross_output,
    up_weight,
    down_weight,
    modulation,
    modulation_bias,
    position_bias,
):
    section = lax.axis_index("section")
    device = lax.axis_index("dp")
    count = lax.axis_size("dp")
    member = device & (MEMBERS - 1)
    clip = device >> 3
    clips = count // MEMBERS
    micro = block_input.shape[0]
    tokens = micro * ROWS
    shard = D // count
    words = MEMBERS * text_embed.shape[1]
    members = [list(range(c * MEMBERS, (c + 1) * MEMBERS)) for c in range(clips)]

    def chosen(first, second):
        return jnp.where(section == 1, second, first)

    def slice_at(x, start, size, axis):
        starts = [0] * x.ndim
        starts[axis] = start
        sizes = list(x.shape)
        sizes[axis] = size
        return lax.dynamic_slice(x, starts, sizes, allow_negative_indices=False)

    def trade(x):
        return lax.all_to_all(x, "dp", 0, 0, tiled=True, axis_index_groups=members)

    def collect(x):
        return trade(jnp.broadcast_to(x, (MEMBERS,) + x.shape))

    ringed = count == 2 * len(RING)

    def parts_of(x):
        x = x.reshape(-1, min(shard, ROWS_OF_PART), x.shape[1] // D, D)
        return jnp.swapaxes(x, 1, 2).reshape(-1, D)

    def gathered(pieces):
        full = [lax.all_gather(x, "dp", axis=0, tiled=True) for x in pieces]
        full = [jnp.swapaxes(x.reshape(PARTS, -1, x.shape[1] // D, D), 1, 2) for x in full]
        return jnp.concatenate([x.reshape(PARTS, -1, D) for x in full], 1)

    grouped = [x[0].reshape(shard, -1, MEMBERS, PAIR) for x in (self_input, cross_query)]
    grouped = jnp.swapaxes(low(jnp.concatenate(grouped, 1)), 1, 2).reshape(shard, 4 * D)
    pieces = [grouped, low(cross_memory[0])]
    if ringed:
        ring = Stages(ring_gather(jnp.concatenate([parts_of(x) for x in pieces], 0), 4))
    else:
        ring = Stages(no_ring(gathered(pieces)))

    cond_low = low(jax.nn.silu(high(conditioning)))
    cond_rows = slice_at(cond_low, device * shard, shard, 2)
    sums = jnp.einsum("bck,kn->cbn", cond_rows, low(modulation[0]), preferred_element_type=HIGH)
    keep = slice_at(text_keep, clip, 1, 1).astype(LOW)
    text = text_embed * keep[:, :, None]
    sums, text = ring.step(sums, text)

    bit = clips // 2
    while bit:
        upper = (clip & bit) > 0
        halves = (sums[:bit], sums[bit:])
        sums = jnp.where(upper, halves[1], halves[0]) + swap(
            jnp.where(upper, halves[0], halves[1]), bit * MEMBERS
        )
        bit //= 2
    sums = sums[0]
    (sums,) = ring.step(sums)

    sums = sums + swap(sums, 1)
    (sums,) = ring.step(sums)

    sums = sums + swap(sums, 2)
    (sums,) = ring.step(sums)

    sums = sums + swap(sums, 4)
    (sums,) = ring.step(sums)

    mods = (sums + modulation_bias[0]).reshape(micro, 6, 1, D)
    shift1, scale1, gate1, shift2, scale2, gate2 = [mods[:, i] for i in range(6)]
    hidden = low(layer_mod(high(block_input), shift1, scale1)).reshape(tokens, D)
    mods, hidden = ring.step(mods, hidden)
    shift1, scale1, gate1, shift2, scale2, gate2 = [mods[:, i] for i in range(6)]

    spread = jnp.arange(MEMBERS * CELLS)
    hot0 = place_hot(*places_of(spread // CELLS, spread % CELLS))
    own_table = slice_at(position_bias[0], 2 * member, 2, 0)
    bias0 = bias_of(own_table, hot0, hot0)
    pieces = [low(x[0]) for x in (down_weight, up_weight, self_output, cross_output)]
    hidden, bias0, *pieces = ring.step(hidden, bias0, *pieces)
    packed = ring.result

    def of_frames(x):
        return x.reshape(MEMBERS, -1, CELLS, x.shape[-1])

    def of_tokens(x):
        return x.reshape(MEMBERS, -1, x.shape[-1])

    def branch_and_norm(inputs, mixture, mixture_text):
        branch = merge(mixture, mixture_text, outer).reshape(micro, ROWS, D)
        middle = inputs + gate1 * branch
        second = low(layer_mod(middle, shift2, scale2)).reshape(tokens, D)
        return branch, middle, second

    def feed_forward(kept):
        upper, active, feed = feed_call(kept["second"], outer)
        feed = feed.reshape(micro, ROWS, D)
        kept.update(upper=upper, active=active, feed=feed)
        return low(kept["middle"] + gate2 * feed)

    if ringed:
        ring = Stages(ring_gather(jnp.concatenate([parts_of(x) for x in pieces], 0), 5))
    else:
        ring = Stages(no_ring(gathered(pieces)))
    joint, asked = project(hidden, packed)
    joint, asked = ring.step(joint, asked)
    joint = [joint[:, i * ROWS : (i + 1) * ROWS] for i in range(micro)]
    joint[0], *joint[1:] = ring.step(trade(joint[0]), *joint[1:])
    mixture, norm = [None] * micro, [None] * micro
    for i in range(micro):
        joint[i] = of_frames(joint[i])
        mixture[i], norm[i] = attend_frames(joint[i], bias0)
        mixture[i] = trade(of_tokens(mixture[i]))
        if i + 1 < micro:
            joint[i + 1], norm[i] = ring.step(trade(joint[i + 1]), norm[i])
    norm[-1], *mixture = ring.step(norm[-1], *mixture)
    mixture = jnp.concatenate(mixture, 1)
    within = jnp.arange(ROWS)
    mine, partner = places_of(member, within), places_of(member ^ 1, within)
    hot_q1 = place_hot(*mine)
    hot_k1 = jnp.concatenate([hot_q1, place_hot(*partner)])
    bias1 = bias_of(position_bias[0], hot_q1, hot_k1)
    text_all = collect(text)
    bias1, mixture, text_all = ring.step(bias1, mixture, text_all)
    text_all = jnp.swapaxes(text_all, 0, 1).reshape(micro * words, D)
    memory = text_project(text_all, packed).reshape(micro, words, 2 * D)
    mixture_text, text_norm = attend_text(asked, memory)
    text_all, memory, mixture_text, text_norm = ring.step(text_all, memory, mixture_text, text_norm)
    for _ in range(3 - micro):
        ring.step()
    outer = ring.result
    branch, middle, second = branch_and_norm(high(block_input), mixture, mixture_text)
    first = dict(
        x=high(block_input),
        hidden=hidden,
        joint=joint,
        asked=asked,
        norm=norm,
        mixture=mixture,
        mixture_text=mixture_text,
        text_norm=text_norm,
        branch=branch,
        middle=middle,
        second=second,
    )
    first_result = feed_forward(first)

    def back_feed(kept, grad_result):
        gate2_grad = jnp.sum(grad_result * kept["feed"], 1)
        feed_grad = low(gate2 * grad_result).reshape(tokens, D)
        upper_grad, second_grad = feed_back_call(feed_grad, kept["upper"], outer)
        kept.update(feed_grad=feed_grad, upper_grad=upper_grad, second_grad=second_grad, gate2_grad=gate2_grad)

    def back_norm2(kept, grad_result):
        second_grad = kept["second_grad"].reshape(micro, ROWS, D)
        middle_norm, shift2_grad, scale2_grad = jax.vjp(layer_mod, kept["middle"], shift2, scale2)[1](second_grad)
        middle_grad = grad_result + middle_norm
        gate1_grad = jnp.sum(middle_grad * kept["branch"], 1)
        branch_grad = low(gate1 * middle_grad).reshape(tokens, D)
        kept.update(
            middle_grad=middle_grad,
            branch_grad=branch_grad,
            late=[gate1_grad, shift2_grad[:, 0], scale2_grad[:, 0], kept["gate2_grad"]],
        )
        return merge_back(branch_grad, outer)

    def back_norm1(kept):
        hidden_grad = project_back(kept["joint_grad"], kept["asked_grad"], packed)
        inputs_norm, shift1_grad, scale1_grad = jax.vjp(layer_mod, kept["x"], shift1, scale1)[1](
            hidden_grad.reshape(micro, ROWS, D)
        )
        kept["mods"] = jnp.concatenate([shift1_grad[:, 0], scale1_grad[:, 0]] + kept["late"], 1)
        return low(kept["middle_grad"] + inputs_norm)

    received = lax.ppermute(first_result, "section", [(0, 1)])
    first["joint"], first["norm"] = jnp.concatenate(first["joint"], 1), jnp.concatenate(first["norm"], 0)
    received, bias1, first["joint"], first["norm"] = together(received, bias1, first["joint"], first["norm"])
    inputs = high(received)
    hidden = low(layer_mod(inputs, shift1, scale1)).reshape(tokens, D)
    joint, asked = project(hidden, packed)
    other = swap(joint, 1, (1,))
    mixture_text, text_norm = attend_text(asked, memory)
    mixture, norm = attend_window(joint, other, bias1)
    branch, middle, second = branch_and_norm(inputs, mixture, mixture_text)
    latter = dict(
        x=inputs, hidden=hidden, mixture=mixture, mixture_text=mixture_text, branch=branch, middle=middle, second=second
    )
    second_result = feed_forward(latter)
    grad_result = high(cotangent)
    back_feed(latter, grad_result)
    mixture_grad, text_grad = back_norm2(latter, grad_result)
    own, sent, dbias1 = attend_window_back(joint, other, bias1, norm, mixture_grad)
    arrived = swap(sent, 1, (1,))
    latter["asked_grad"], dkt1, dvt1 = attend_text_back(asked, memory, text_norm, text_grad)
    keys = low(high(own[:, :, PAIR:]) + high(arrived))
    latter["joint_grad"] = jnp.concatenate([own[:, :, :PAIR], keys], 2)
    second_grad = back_norm1(latter)
    returned = lax.ppermute(second_grad, "section", [(1, 0)])
    names = ("second", "active", "hidden", "mixture", "mixture_text")
    second_grad, dkt1, dvt1, *kept = together(second_grad, dkt1, dvt1, *[latter[name] for name in names])
    latter.update(zip(names, kept))

    def both(name):
        return chosen(first[name], latter[name])

    ready = [both(name) for name in names]
    apart = count != 2 * len(RING)
    order = None if apart else ring_order()

    def paired(x):
        return (x, x if apart else swap(x, 1))

    def summed(x):
        return high(lax.psum_scatter(x, "dp", scatter_dimension=0, tiled=True))

    second_all, active_all, hidden_all, mixture_all, text_all2 = ready
    columns = [paired(x) for x in (hidden_all, mixture_all, text_all2)] + [(text_all, text_all), paired(second_all)]
    columns = turned(*columns)
    returned, *flat = together(returned, *columns, *paired(active_all))
    columns, active2 = flat[:5], tuple(flat[5:])

    grad_result = high(returned)
    back_feed(first, grad_result)
    upper2, feed2 = paired(both("upper_grad")), paired(both("feed_grad"))
    mixture_grad, text_grad = back_norm2(first, grad_result)
    mixture_grad = of_frames(trade(mixture_grad))
    first["asked_grad"], dkt, dvt = attend_text_back(first["asked"], memory, first["text_norm"], text_grad)
    mixture_grad, dkt, dvt, *flat = together(mixture_grad, dkt, dvt, *upper2, *feed2)
    upper2, feed2 = tuple(flat[:2]), tuple(flat[2:])

    joint_grad, dbias0 = attend_frames_back(
        first["joint"], bias0, first["norm"], mixture_grad
    )
    feeds = () if apart else feed_grads(order, columns[4], upper2, active2, feed2)
    first["joint_grad"], *feeds = together(trade(of_tokens(joint_grad)), *feeds)
    ring = Stages(no_ring(None) if apart else ring_sums(feeds[:1], feeds[1:]))
    items = [paired(both(x)) for x in ("asked_grad", "branch_grad", "joint_grad")]
    items += [paired(chosen(x, y).reshape(micro * words, D)) for x, y in ((dkt, dkt1), (dvt, dvt1))]
    flat = ring.step(*[x for pair in items for x in pair])
    asked2, branch2, joint2, keys2, values2 = [tuple(flat[2 * i : 2 * i + 2]) for i in range(5)]
    if apart:
        joint_all = [jnp.swapaxes(joint2[0], 0, 1), asked2[0].reshape(tokens, MEMBERS, PAIR)]
        joint_all = jnp.concatenate(joint_all, 2).reshape(tokens, 4 * D)
        rights = (joint_all, branch2[0], branch2[0], keys2[0], values2[0], upper2[0], feed2[0])
        lefts = [x[:, :tokens] for x in columns[:3]] + [text_all.T] * 2 + [columns[4][:, :tokens], active2[0].T]
        grads = [summed(low(dot(x, y))) for x, y in zip(lefts, rights)]
    else:
        grads = packed_grads(order, *columns[:4], joint2, asked2, branch2, keys2, values2)
    first["joint_grad"], dbias0, dbias1, *grads = ring.step(first["joint_grad"], dbias0, dbias1, *grads)
    for _ in range(5):
        ring.step()
    feed_part = ring.result
    ring = Stages(no_ring(grads) if apart else ring_sums(grads[:1], grads[1:]))
    first_grad = back_norm1(first)
    (first_grad,) = ring.step(first_grad)

    table0 = lax.dynamic_update_slice(
        jnp.zeros((HEADS, REL), HIGH), bias_grad(dbias0, hot0, hot0), (2 * member, 0), allow_negative_indices=False
    )
    table = chosen(table0, bias_grad(dbias1, hot_q1, hot_k1))
    small = jnp.concatenate([both("mods").reshape(micro * 6 * D), table.reshape(HEADS * REL)])
    small = jnp.pad(small, (0, -small.shape[0] % 1024)).reshape(1, -1, 128)
    (small,) = ring.step(small)
    small = small + swap(small, 1)
    (small,) = ring.step(small)
    small = small + swap(small, 2)
    (small,) = ring.step(small)
    small = small + swap(small, 4)
    (small,) = ring.step(small)
    bit = 1
    while bit < clips:
        far = swap(small, bit * MEMBERS)
        upper = (clip & bit) > 0
        small = jnp.concatenate([jnp.where(upper, far, small), jnp.where(upper, small, far)])
        bit *= 2
    (small,) = ring.step(small)
    small = small.reshape(clips, -1)
    mods_all = small[:, : micro * 6 * D].reshape(clips, micro, 6 * D)
    table_sum = jnp.sum(small[:, micro * 6 * D : micro * 6 * D + HEADS * REL], 0).reshape(HEADS, REL)
    modul_shard = jnp.einsum("bck,cbn->kn", high(cond_rows), mods_all, precision=lax.Precision.HIGHEST)
    bias_sum = jnp.sum(mods_all, (0, 1))
    if apart:
        up_shard = down_shard = bias_sum
    else:
        up_shard, down_shard = feed_part
        up_shard = jnp.swapaxes(up_shard.reshape(4, shard, D), 0, 1).reshape(shard, 4 * D)
    modul_shard, bias_sum, table_sum, up_shard, down_shard = ring.step(
        modul_shard, bias_sum, table_sum, up_shard, down_shard
    )

    if apart:
        grouped, out_shard, cross_shard, keys, values, up_shard, down_shard = ring.result
        memory_shard = jnp.concatenate([keys, values], 1)
    else:
        grouped, outputs = ring.result
        grouped = jnp.swapaxes(grouped.reshape(4, shard, D), 0, 1).reshape(shard, 4 * D)
        out_shard, cross_shard = outputs[:shard], outputs[shard : 2 * shard]
        memory_shard = jnp.concatenate([outputs[2 * shard : 3 * shard], outputs[3 * shard :]], 1)
    grouped = jnp.swapaxes(grouped.reshape(shard, MEMBERS, 4, PAIR), 1, 2).reshape(shard, 4 * D)
    in_shard, query_shard = grouped[:, : 3 * D], grouped[:, 3 * D :]
    outputs = chosen(first_result, second_result)
    input_grads = chosen(first_grad, second_grad)
    return tuple(
        x[None]
        for x in (
            outputs,
            input_grads,
            in_shard,
            out_shard,
            query_shard,
            memory_shard,
            cross_shard,
            up_shard,
            down_shard,
            modul_shard,
            bias_sum,
            table_sum,
        )
    )


def solution(mesh):
    weights = P("section", "dp", None)
    return jax.shard_map(
        per_device,
        mesh=mesh,
        in_specs=(
            P(None, "dp", None),
            P(),
            P(None, "dp", None),
            P(),
            P(None, "dp", None),
        )
        + (weights,) * 8
        + (P("section", None), P("section", None, None)),
        out_specs=(P("section", None, "dp", None),) * 2
        + (weights,) * 8
        + (P("section", None), P("section", None, None)),
        check_vma=False,
    )
```
